32 devices in a mesh: expert: 8 (over z, y), batch: 4 (over x, core).
Axes of the slice: x: 2, y: 2, z: 4, core: 2. Of those that a mesh axis runs over, the one named last changes fastest.
Arguments:
- tokens: bfloat16 [8, 256, 7168], P('expert', 'batch'), may hold values from -6 to 6
- route_prob: float32 [8, 256], P('expert', 'batch'), may hold values from 0.2 to 1
- counts: int32 [8, 4], replicated, may hold values from 1 to 32, as said below
- w_gate: bfloat16 [8, 7168, 2048], P('expert', None, 'batch'), may hold values from -0.0625 to 0.0625
- w_up: bfloat16 [8, 7168, 2048], P('expert', None, 'batch'), may hold values from -0.0625 to 0.0625
- w_down: bfloat16 [8, 2048, 7168], P('expert', 'batch'), may hold values from -0.125 to 0.125
Outputs:
- returned: bfloat16 [8, 256, 7168], P('expert', 'batch')
The draws below stay inside these ranges and needn't reach their ends.
Inputs may be any that keep to these rules, and one draw needn't show every extreme that they name: Live slot counts of the blocks, at most 32; some block has exactly 32 in every draw, and experts differ in load.
All inputs are finite; a program needn't handle non-finite values.
Results may differ from the reference program's by a relative error of at most 0.014.
Values may be sent and summed in bfloat16 or wider, within the bound.
No kernel may reach another device: no remote copies, remote signals or barrier semaphores. Data moves between devices by JAX's collectives and lax.ppermute only.
A program may use at most 128 MiB of HBM per device.

```python
import jax
import jax.numpy as jnp
from jax import lax

D = 7168
FF = 2048
CAP = 64
LIVE = 32
E = 8
BTOK = 256
SLOT = 8
N_BATCH = 4


def draw_counts(key, part):
    keys = jax.random.split(key, 4)
    heat = jax.random.randint(keys[0], (E, 1), 1, 5)
    base = jax.random.randint(keys[1], (E, N_BATCH), max(CAP // 16, 1), CAP // 8 + 1)
    loads = jnp.clip(base * heat, 1, LIVE)
    first = jax.random.randint(keys[2], (), 0, E)
    second = jax.random.randint(keys[3], (), 0, N_BATCH)
    loads = loads.at[first, second].set(LIVE)
    return loads.astype(jnp.int32)


def block_scale(own_key, extent, shards, low, top_value):
    level = 1.0
    for position, blocks in shards:
        steps = jax.random.uniform(jax.random.fold_in(jax.random.fold_in(own_key, 6), position), (blocks,), jnp.float32, low / len(shards), top_value / len(shards))
        level = level * jnp.repeat(jnp.exp(steps), extent[position] // blocks).reshape((-1,) + (1,) * (len(extent) - 1 - position))
    return level


def noise(stream_key, extent, spread, limit, shards=(), kind=jnp.bfloat16):
    gain = block_scale(stream_key, extent, shards, -0.22, 0.18) if shards else 1.0
    result = jax.random.normal(stream_key, extent, jnp.float32) * spread * gain
    return jnp.minimum(jnp.maximum(result, -limit), limit).astype(kind)


def setup_inputs(seed: int = 0) -> dict:
    key_of = jax.random.split(jax.random.key(seed), 7)
    tokens = noise(key_of[0], (E, BTOK, D), 1.0, 6.0, ((0, 8), (1, 4)))
    route_prob = jnp.clip(0.2 + 0.8 * jax.random.uniform(key_of[1], (E, BTOK), jnp.float32) ** block_scale(key_of[1], (E, BTOK), ((0, 8), (1, 4)), -0.2, 0.2), 0.2, 1.0)
    counts = draw_counts(jax.random.fold_in(key_of[6], 71), 0)
    w_gate = noise(key_of[3], (E, D, FF), D ** -0.5, 0.0625, ((0, 8), (2, 4)))
    w_up = noise(key_of[4], (E, D, FF), D ** -0.5, 0.0625, ((0, 8), (2, 4)))
    w_down = noise(key_of[5], (E, FF, D), FF ** -0.5, 0.125, ((0, 8), (1, 4)))
    return {"tokens": tokens, "route_prob": route_prob, "counts": counts, "w_gate": w_gate, "w_up": w_up, "w_down": w_down}


def one_expert(operands):
    inputs, weights_prob, live_counts, gate_w, up_w, down_w = operands
    gate = jnp.dot(inputs, gate_w, preferred_element_type=jnp.float32)
    upper = jnp.dot(inputs, up_w, preferred_element_type=jnp.float32)
    hidden = (jax.nn.silu(gate) * upper).astype(jnp.bfloat16)
    group = FF // N_BATCH
    hidden_parts = hidden.reshape(BTOK, N_BATCH, group).transpose(1, 0, 2)
    down_parts = down_w.reshape(N_BATCH, group, D)

    def add_part(total, pair):
        hidden_piece, down_piece = pair
        partial_value = jnp.dot(hidden_piece, down_piece, preferred_element_type=jnp.float32).astype(jnp.bfloat16)
        partial_value = lax.optimization_barrier(partial_value)
        return total + partial_value.astype(jnp.float32), None

    summed, _ = lax.scan(add_part, jnp.zeros((BTOK, D), jnp.float32), (hidden_parts, down_parts))
    slots = jnp.arange(CAP, dtype=jnp.int32)
    live = (slots[None, :] < live_counts[:, None]).reshape(BTOK)
    scaled = weights_prob[:, None] * summed
    return jnp.where(live[:, None], scaled, 0.0).astype(jnp.bfloat16)


def reference(tokens, route_prob, counts, w_gate, w_up, w_down):
    expert_out = lax.map(one_expert, (tokens, route_prob, counts, w_gate, w_up, w_down))
    blocks = expert_out.reshape(E, N_BATCH, E, SLOT, D)
    return blocks.transpose(2, 1, 0, 3, 4).reshape(E, BTOK, D)
```

```python
import jax
import jax.numpy as jnp
from jax import lax
from jax.experimental import pallas as pl
from jax.experimental.pallas import tpu as pltpu
from jax.sharding import PartitionSpec as P

LIVE = 32
PROB_COLUMNS = 128
PARTS = 2
VMEM_LIMIT = 16 * 2**20
VMEM = pl.BlockSpec(memory_space=pltpu.VMEM)
HBM = pl.BlockSpec(memory_space=pltpu.HBM)
SMEM = pl.BlockSpec(memory_space=pltpu.SMEM)


def xor_pairs(size, offset):
    return [(i, i ^ offset) for i in range(size)]


def hidden_kernel(pieces, *refs):
    token_refs = refs[:pieces]
    gate_ref, up_ref, out_ref, gate_acc, up_acc = refs[pieces:]
    live = token_refs[0].shape[0]
    width = gate_ref.shape[0]
    step = width // 4

    def add(start, first):
        span = pl.ds(start, step)
        rows = jnp.concatenate([ref[:, span] for ref in token_refs], axis=0)
        gate = jnp.dot(rows, gate_ref[span, :], preferred_element_type=jnp.float32)
        upper = jnp.dot(rows, up_ref[span, :], preferred_element_type=jnp.float32)
        if first:
            gate_acc[...] = gate
            up_acc[...] = upper
        else:
            gate_acc[...] += gate
            up_acc[...] += upper

    add(0, True)

    @pl.loop(1, width // step)
    def _(i):
        add(pl.multiple_of(i * step, step), False)

    gate = gate_acc[...]
    out_ref[...] = (gate / (1.0 + jnp.exp(-gate)) * up_acc[...]).astype(out_ref.dtype)


def hidden_units(pieces, gate_w, up_w):
    live, width = pieces[0].shape
    units = gate_w.shape[1]
    rows = live * len(pieces)
    return pl.pallas_call(
        lambda *refs: hidden_kernel(len(pieces), *refs),
        out_shape=jax.ShapeDtypeStruct((rows, units), jnp.bfloat16),
        in_specs=[VMEM] * (len(pieces) + 2),
        out_specs=VMEM,
        scratch_shapes=[pltpu.VMEM((rows, units), jnp.float32)] * 2,
        compiler_params=pltpu.CompilerParams(vmem_limit_bytes=VMEM_LIMIT),
        cost_estimate=pl.CostEstimate(
            flops=4 * rows * width * units, bytes_accessed=4 * width * units, transcendentals=rows * units
        ),
        name="hidden_units",
    )(*pieces, gate_w, up_w)


def down_kernel(start, hidden_ref, down_ref, keep_ref, send_ref):
    width = keep_ref.shape[1]
    half = keep_ref.shape[0]
    step = width // 2

    @pl.loop(0, width // step)
    def _(i):
        span = pl.ds(pl.multiple_of(i * step, step), step)
        source = pl.ds(pl.multiple_of(start + i * step, step), step)
        terms = jnp.dot(hidden_ref[...], down_ref[:, source], preferred_element_type=jnp.float32).astype(
            keep_ref.dtype
        )
        keep_ref[:, span] = terms[:half]
        send_ref[:, span] = terms[half:]


def down_part(hidden, down_w, start, width):
    rows, units = hidden.shape
    shape = jax.ShapeDtypeStruct((rows // 2, width), jnp.bfloat16)
    return pl.pallas_call(
        lambda *refs: down_kernel(start, *refs),
        out_shape=[shape, shape],
        in_specs=[VMEM] * 2,
        out_specs=[VMEM] * 2,
        compiler_params=pltpu.CompilerParams(vmem_limit_bytes=VMEM_LIMIT),
        cost_estimate=pl.CostEstimate(
            flops=2 * rows * width * units, bytes_accessed=2 * width * units, transcendentals=0
        ),
        name="down_part",
    )(hidden, down_w)


def general_body(tokens, route_prob, counts, w_gate, w_up, w_down):
    cap, width = tokens.shape[1:]
    n_batch = lax.axis_size("batch")
    n_experts = lax.axis_size("expert")
    expert_id = lax.axis_index("expert")
    batch_id = lax.axis_index("batch")
    slot = cap // n_experts
    live_slots = LIVE // slot
    part = width // PARTS

    own = tokens[0, :LIVE]
    even = [own] + [lax.ppermute(own, "batch", xor_pairs(n_batch, d)) for d in range(2, n_batch, 2)]
    odd = [lax.ppermute(piece, "batch", xor_pairs(n_batch, 1)) for piece in even]
    hidden = hidden_units(even + odd, w_gate[0], w_up[0])

    count = counts[expert_id, batch_id]
    live = jnp.arange(LIVE, dtype=jnp.int32) < count
    scale = jnp.where(live, route_prob[0, :LIVE], 0.0)[:, None]

    columns = []
    for start in range(0, width, part):
        keep, send = down_part(hidden, w_down[0], start, part)
        received = lax.ppermute(send, "batch", xor_pairs(n_batch, 1))
        both = keep.astype(jnp.float32) + received.astype(jnp.float32)
        total = both[:LIVE]
        for i, d in enumerate(range(2, n_batch, 2), 1):
            term = both[i * LIVE : (i + 1) * LIVE].astype(jnp.bfloat16)
            total += lax.ppermute(term, "batch", xor_pairs(n_batch, d)).astype(jnp.float32)
        expert_out = jnp.where(live[:, None], scale * total, 0.0).astype(jnp.bfloat16)
        grouped = expert_out.reshape(live_slots, slot, part)

        picks = {}
        for d in sorted(range(1, n_experts), key=lambda d: (-(d // live_slots), d)):
            pairs = [(e, e ^ d) for e in range(n_experts) if e ^ d < live_slots]
            target = jnp.minimum(expert_id ^ d, live_slots - 1)
            payload = lax.dynamic_index_in_dim(grouped, target, 0, keepdims=False)
            picks[d] = lax.ppermute(payload, "expert", pairs)
        mine = lax.dynamic_index_in_dim(grouped, jnp.minimum(expert_id, live_slots - 1), 0, keepdims=False)
        picks[0] = jnp.where(expert_id < live_slots, mine, jnp.zeros_like(mine))
        stacked = jnp.stack([picks[d] for d in range(n_experts)])
        columns.append(jnp.take(stacked, jnp.arange(n_experts, dtype=jnp.int32) ^ expert_id, axis=0))
    returned = jnp.concatenate(columns, axis=-1)
    return returned.reshape(1, cap, width)


def call(kernel, outs, args, specs=None, scratch=(), out_specs=None, name=None):
    return pl.pallas_call(
        kernel,
        out_shape=outs,
        in_specs=specs or [VMEM] * len(args),
        out_specs=out_specs or jax.tree.map(lambda _: VMEM, outs),
        scratch_shapes=list(scratch),
        compiler_params=pltpu.CompilerParams(vmem_limit_bytes=VMEM_LIMIT),
        cost_estimate=pl.CostEstimate(flops=0, bytes_accessed=0, transcendentals=0),
        name=name,
    )(*args)


def live_rows_kernel(tokens_ref, prob_ref, out_ref, sem):
    rows = out_ref.shape[0]
    width = tokens_ref.shape[2]
    copy = pltpu.make_async_copy(tokens_ref.at[0, pl.ds(0, rows)], out_ref.at[:, pl.ds(0, width)], sem)
    copy.start()
    slots = prob_ref.shape[1]
    row = lax.broadcasted_iota(jnp.int32, (rows, slots), 0)
    lane = lax.broadcasted_iota(jnp.int32, (rows, slots), 1)
    prob = jnp.sum(jnp.where(row == lane, prob_ref[...], 0.0), axis=1, keepdims=True)
    column = lax.broadcasted_iota(jnp.int32, (rows, PROB_COLUMNS), 1)
    terms = jnp.zeros((rows, PROB_COLUMNS), jnp.float32)
    for i in range(3):
        term = prob.astype(jnp.bfloat16).astype(jnp.float32)
        prob = prob - term
        terms = jnp.where(column == i, term, terms)
    out_ref[:, width:] = terms.astype(out_ref.dtype)
    copy.wait()


def resident_kernel(*refs):
    count = len(refs) // 2
    sems = refs[-1]
    copies = [pltpu.make_async_copy(refs[i], refs[count + i], sems.at[i]) for i in range(count)]
    for copy in copies:
        copy.start()
    for copy in copies:
        copy.wait()


def resident(*arrays):
    return call(
        resident_kernel,
        [pltpu.VMEM(a.shape, a.dtype) for a in arrays],
        [pltpu.with_memory_space_constraint(a, pltpu.HBM) for a in arrays],
        [HBM] * len(arrays),
        [pltpu.SemaphoreType.DMA((len(arrays),))],
        name="resident",
    )


def after(value, *others):
    return lax.optimization_barrier((value, *others))[0]


def coordinates():
    e = lax.axis_index("expert")
    b = lax.axis_index("batch")
    return e // 2, e % 2, b // 2, b % 2


def swap(flag, first, second):
    return jnp.where(flag, second, first), jnp.where(flag, first, second)


def all_hidden_kernel(counts_ref, own_ref, near_ref, across_ref, diagonal_ref, gate_ref, up_ref, *refs):
    z, y, x, c = coordinates()
    outs, (gate_acc, up_acc) = refs[:-2], refs[-2:]
    width, units = gate_ref.shape
    steps = 4
    step = width // steps
    tokens = (own_ref, near_ref, across_ref, diagonal_ref)
    live = own_ref.shape[0]
    rows = live * len(tokens)

    def add(start, first):
        span = pl.ds(start, step)
        chunk = jnp.concatenate([ref[:, span] for ref in tokens], axis=0)
        gate = jnp.dot(chunk, gate_ref[span, :], preferred_element_type=jnp.float32)
        upper = jnp.dot(chunk, up_ref[span, :], preferred_element_type=jnp.float32)
        if first:
            gate_acc[...] = gate
            up_acc[...] = upper
        else:
            gate_acc[...] += gate
            up_acc[...] += upper

    add(0, True)

    @pl.loop(1, steps)
    def _(i):
        add(pl.multiple_of(i * step, step), False)

    gate = gate_acc[...]
    hidden = gate / (1.0 + jnp.exp(-gate)) * up_acc[...]
    row = lax.broadcasted_iota(jnp.int32, (live, 1), 0)
    scaled = []
    for i, ref in enumerate(tokens):
        prob = jnp.sum(ref[:, width:].astype(jnp.float32), axis=1, keepdims=True)
        count = counts_ref[(x * 2 + c) ^ i, z * 2 + y]
        scaled.append(jnp.where(row < count, hidden[i * live : (i + 1) * live] * prob, 0.0))
    hidden = jnp.concatenate(scaled, axis=0)
    grid = hidden.reshape(2, 2, len(outs), 2, rows // (8 * len(outs)), units)
    for part, out_ref in enumerate(outs):
        pieces = [[], []]
        for dx in range(2):
            for block in swap(c == 1, grid[dx, 0, part], grid[dx, 1, part]):
                kept, sent = swap((y ^ c) == 1, block[0], block[1])
                pieces[0].append(kept)
                pieces[1].append(sent)
        out_ref[...] = jnp.concatenate(pieces[0] + pieces[1], axis=0).astype(out_ref.dtype)


def part_down_kernel(hidden_ref, down_ref, keep_ref, send_ref):
    half, width = keep_ref.shape
    step = width // 4

    @pl.loop(0, width // step)
    def _(i):
        span = pl.ds(pl.multiple_of(i * step, step), step)
        terms = jnp.dot(hidden_ref[...], down_ref[:, span], preferred_element_type=jnp.float32).astype(
            keep_ref.dtype
        )
        keep_ref[:, span] = terms[:half]
        send_ref[:, span] = terms[half:]


def half_sums_kernel(keep_ref, received_ref, mine_ref, theirs_ref):
    half = mine_ref.shape[0]
    for ref, rows in ((theirs_ref, pl.ds(half, half)), (mine_ref, pl.ds(0, half))):
        total = keep_ref[rows, :].astype(jnp.float32) + received_ref[rows, :].astype(jnp.float32)
        ref[...] = total.astype(ref.dtype)


def finish_kernel(mine, along, crossed, out_ref):
    z, y, x, c = coordinates()
    first = jnp.where(c == 1, along[...], mine[...]).astype(jnp.float32)
    out_ref[...] = (first + crossed[...].astype(jnp.float32)).astype(out_ref.dtype)


def return_kernel(*refs):
    z, y, x, c = coordinates()
    held, out_ref = refs[:-1], refs[-1]
    count = len(held) // 2
    for part in range(2):

        @pl.when(z == part)
        def _():
            for i in range(count):
                out_ref[i] = held[part * count + i][1 - c]


def place_kernel(*refs):
    z, y, x, c = coordinates()
    *held, received, out_ref, zeros, sems = refs
    count = len(held) // 2

    def run(copies):
        for copy in copies:
            copy.start()
        for copy in copies:
            copy.wait()

    for part in range(2):

        @pl.when(z == part)
        def _():
            copies = []
            for i in range(count):
                source = (part, 1 - part, 2, 3)[i]
                mine, other = source * 2 + (y ^ c), source * 2 + (y ^ c ^ 1)
                copies.append(
                    pltpu.make_async_copy(held[part * count + i].at[c], out_ref.at[mine], sems.at[2 * i])
                )
                copies.append(pltpu.make_async_copy(received.at[i], out_ref.at[other], sems.at[2 * i + 1]))
            run(copies)

    @pl.when(z >= 2)
    def _():
        zeros[...] = jnp.zeros_like(zeros)
        run([pltpu.make_async_copy(zeros, out_ref.at[i], sems.at[i]) for i in range(2 * count)])


def ports_body(tokens, route_prob, counts, w_gate, w_up, w_down):
    cap, width = tokens.shape[1:]
    units = w_gate.shape[2]
    experts = lax.axis_size("expert")
    slot = cap // experts
    half = LIVE // 2
    both_axes = ("expert", "batch")

    def device(z, y, x, c):
        return (z * 2 + y) * 4 + x * 2 + c

    places = [(z, y, x, c) for z in range(4) for y in range(2) for x in range(2) for c in range(2)]

    def other_core(value):
        return lax.ppermute(value, "batch", xor_pairs(4, 1))

    def along_z(value, source, target):
        pairs = [(device(source, *p[1:]), device(target, *p[1:])) for p in places if p[0] == 0]
        return lax.ppermute(value, both_axes, pairs)

    def rows_of(*shape):
        return jax.ShapeDtypeStruct((*shape, width), jnp.bfloat16)

    own = call(
        live_rows_kernel,
        pltpu.VMEM((LIVE, width + PROB_COLUMNS), tokens.dtype),
        [pltpu.with_memory_space_constraint(tokens, pltpu.HBM), route_prob],
        [HBM, VMEM],
        [pltpu.SemaphoreType.DMA],
        name="live_rows",
    )
    across = lax.ppermute(own, "batch", xor_pairs(4, 2))
    near = other_core(own)
    gate_w, up_w = resident(after(w_gate[0], own), w_up[0])
    down_w, = resident(after(w_down[0], gate_w))
    across = after(across, down_w)
    hidden = call(
        all_hidden_kernel,
        [jax.ShapeDtypeStruct((4 * half, units), jnp.bfloat16)] * 2,
        [counts.T, own, near, across, other_core(across), gate_w, up_w],
        [SMEM] + [VMEM] * 6,
        scratch=[pltpu.VMEM((8 * half, units), jnp.float32)] * 2,
        name="all_hidden",
    )

    def half_sums(hidden):
        keep, send = call(part_down_kernel, [rows_of(2 * half)] * 2, [hidden, down_w], name="part_down")
        return call(half_sums_kernel, [rows_of(half)] * 2, [keep, other_core(send)], name="half_sums")

    def over_x_and_y(mine, theirs):
        along = lax.ppermute(
            mine, both_axes, [(device(*q), device(q[0], q[1] ^ 1, q[2], q[3])) for q in places if q[3] == 1]
        )
        crossed = lax.ppermute(
            theirs, both_axes, [(device(*q), device(q[0], q[1] ^ q[3], q[2] ^ 1, q[3])) for q in places]
        )
        return call(finish_kernel, rows_of(half), [mine, along, crossed], name="finish")

    first_sums = half_sums(hidden[0])
    second_sums = half_sums(hidden[1])
    first = over_x_and_y(*first_sums)
    second = over_x_and_y(*second_sums)
    held = [
        first,
        along_z(after(first, second), 1, 0),
        along_z(first, 2, 0),
        along_z(first, 3, 0),
        second,
        along_z(second, 0, 1),
        along_z(second, 2, 1),
        along_z(second, 3, 1),
    ]
    held = [rows.reshape(2, slot, width) for rows in held]
    received = other_core(call(return_kernel, rows_of(4, slot), held, name="return_rows"))
    returned = call(
        place_kernel,
        rows_of(experts, slot),
        [*held, received],
        scratch=[pltpu.VMEM((slot, width), jnp.bfloat16), pltpu.SemaphoreType.DMA((experts,))],
        out_specs=HBM,
        name="place_rows",
    )
    return returned.reshape(1, cap, width)


def solution(mesh):
    in_specs = (
        P("expert", "batch", None),
        P("expert", "batch"),
        P(),
        P("expert", None, "batch"),
        P("expert", None, "batch"),
        P("expert", "batch", None),
    )
    out_specs = P("expert", "batch", None)
    fits = dict(mesh.shape) == {"expert": 8, "batch": 4}
    body = ports_body if fits else general_body
    return jax.shard_map(body, mesh=mesh, in_specs=in_specs, out_specs=out_specs, check_vma=False)
```

```python
import jax
import jax.numpy as jnp
from jax import lax
from jax.experimental import pallas as pl
from jax.experimental.pallas import tpu as pltpu
from jax.sharding import PartitionSpec as P

LIVE = 32
PROB_COLUMNS = 256
PARTS = 2
VMEM_LIMIT = 16 * 2**20
VMEM = pl.BlockSpec(memory_space=pltpu.VMEM)
HBM = pl.BlockSpec(memory_space=pltpu.HBM)
ANY = pl.BlockSpec(memory_space=pl.ANY)
SMEM = pl.BlockSpec(memory_space=pltpu.SMEM)


def xor_pairs(size, offset):
    return [(i, i ^ offset) for i in range(size)]


def hidden_kernel(pieces, *refs):
    token_refs = refs[:pieces]
    gate_ref, up_ref, out_ref, gate_acc, up_acc = refs[pieces:]
    live = token_refs[0].shape[0]
    width = gate_ref.shape[0]
    step = width // 4

    def add(start, first):
        span = pl.ds(start, step)
        rows = jnp.concatenate([ref[:, span] for ref in token_refs], axis=0)
        gate = jnp.dot(rows, gate_ref[span, :], preferred_element_type=jnp.float32)
        upper = jnp.dot(rows, up_ref[span, :], preferred_element_type=jnp.float32)
        if first:
            gate_acc[...] = gate
            up_acc[...] = upper
        else:
            gate_acc[...] += gate
            up_acc[...] += upper

    add(0, True)

    @pl.loop(1, width // step)
    def _(i):
        add(pl.multiple_of(i * step, step), False)

    gate = gate_acc[...]
    out_ref[...] = (gate / (1.0 + jnp.exp(-gate)) * up_acc[...]).astype(out_ref.dtype)


def hidden_units(pieces, gate_w, up_w):
    live, width = pieces[0].shape
    units = gate_w.shape[1]
    rows = live * len(pieces)
    return pl.pallas_call(
        lambda *refs: hidden_kernel(len(pieces), *refs),
        out_shape=jax.ShapeDtypeStruct((rows, units), jnp.bfloat16),
        in_specs=[VMEM] * (len(pieces) + 2),
        out_specs=VMEM,
        scratch_shapes=[pltpu.VMEM((rows, units), jnp.float32)] * 2,
        compiler_params=pltpu.CompilerParams(vmem_limit_bytes=VMEM_LIMIT),
        cost_estimate=pl.CostEstimate(
            flops=4 * rows * width * units, bytes_accessed=4 * width * units, transcendentals=rows * units
        ),
        name="hidden_units",
    )(*pieces, gate_w, up_w)


def down_kernel(start, hidden_ref, down_ref, keep_ref, send_ref):
    width = keep_ref.shape[1]
    half = keep_ref.shape[0]
    step = width // 2

    @pl.loop(0, width // step)
    def _(i):
        span = pl.ds(pl.multiple_of(i * step, step), step)
        source = pl.ds(pl.multiple_of(start + i * step, step), step)
        terms = jnp.dot(hidden_ref[...], down_ref[:, source], preferred_element_type=jnp.float32).astype(
            keep_ref.dtype
        )
        keep_ref[:, span] = terms[:half]
        send_ref[:, span] = terms[half:]


def down_part(hidden, down_w, start, width):
    rows, units = hidden.shape
    shape = jax.ShapeDtypeStruct((rows // 2, width), jnp.bfloat16)
    return pl.pallas_call(
        lambda *refs: down_kernel(start, *refs),
        out_shape=[shape, shape],
        in_specs=[VMEM] * 2,
        out_specs=[VMEM] * 2,
        compiler_params=pltpu.CompilerParams(vmem_limit_bytes=VMEM_LIMIT),
        cost_estimate=pl.CostEstimate(
            flops=2 * rows * width * units, bytes_accessed=2 * width * units, transcendentals=0
        ),
        name="down_part",
    )(hidden, down_w)


def general_body(tokens, route_prob, counts, w_gate, w_up, w_down):
    cap, width = tokens.shape[1:]
    n_batch = lax.axis_size("batch")
    n_experts = lax.axis_size("expert")
    expert_id = lax.axis_index("expert")
    batch_id = lax.axis_index("batch")
    slot = cap // n_experts
    live_slots = LIVE // slot
    part = width // PARTS

    own = tokens[0, :LIVE]
    even = [own] + [lax.ppermute(own, "batch", xor_pairs(n_batch, d)) for d in range(2, n_batch, 2)]
    odd = [lax.ppermute(piece, "batch", xor_pairs(n_batch, 1)) for piece in even]
    hidden = hidden_units(even + odd, w_gate[0], w_up[0])

    count = counts[expert_id, batch_id]
    live = jnp.arange(LIVE, dtype=jnp.int32) < count
    scale = jnp.where(live, route_prob[0, :LIVE], 0.0)[:, None]

    columns = []
    for start in range(0, width, part):
        keep, send = down_part(hidden, w_down[0], start, part)
        received = lax.ppermute(send, "batch", xor_pairs(n_batch, 1))
        both = keep.astype(jnp.float32) + received.astype(jnp.float32)
        total = both[:LIVE]
        for i, d in enumerate(range(2, n_batch, 2), 1):
            term = both[i * LIVE : (i + 1) * LIVE].astype(jnp.bfloat16)
            total += lax.ppermute(term, "batch", xor_pairs(n_batch, d)).astype(jnp.float32)
        expert_out = jnp.where(live[:, None], scale * total, 0.0).astype(jnp.bfloat16)
        grouped = expert_out.reshape(live_slots, slot, part)

        picks = {}
        for d in sorted(range(1, n_experts), key=lambda d: (-(d // live_slots), d)):
            pairs = [(e, e ^ d) for e in range(n_experts) if e ^ d < live_slots]
            target = jnp.minimum(expert_id ^ d, live_slots - 1)
            payload = lax.dynamic_index_in_dim(grouped, target, 0, keepdims=False)
            picks[d] = lax.ppermute(payload, "expert", pairs)
        mine = lax.dynamic_index_in_dim(grouped, jnp.minimum(expert_id, live_slots - 1), 0, keepdims=False)
        picks[0] = jnp.where(expert_id < live_slots, mine, jnp.zeros_like(mine))
        stacked = jnp.stack([picks[d] for d in range(n_experts)])
        columns.append(jnp.take(stacked, jnp.arange(n_experts, dtype=jnp.int32) ^ expert_id, axis=0))
    returned = jnp.concatenate(columns, axis=-1)
    return returned.reshape(1, cap, width)


def call(kernel, outs, args, specs=None, scratch=(), out_specs=None, cost=0, aliases=None, name=None):
    return pl.pallas_call(
        kernel,
        out_shape=outs,
        in_specs=specs or [VMEM] * len(args),
        out_specs=out_specs or jax.tree.map(lambda _: VMEM, outs),
        scratch_shapes=list(scratch),
        input_output_aliases=aliases or {},
        compiler_params=pltpu.CompilerParams(vmem_limit_bytes=VMEM_LIMIT),
        cost_estimate=pl.CostEstimate(flops=0, bytes_accessed=cost, transcendentals=0),
        name=name,
    )(*args)


def live_rows_kernel(tokens_ref, prob_ref, *refs):
    *outs, prob_copy, sems = refs
    rows = outs[0].shape[0]
    copies = [pltpu.make_async_copy(prob_ref, prob_copy, sems.at[len(outs)])]
    start = 0
    for i, out in enumerate(outs):
        size = out.shape[1] - (PROB_COLUMNS if i == len(outs) - 1 else 0)
        source = tokens_ref.at[0, pl.ds(0, rows), pl.ds(start, size)]
        copies.append(pltpu.make_async_copy(source, out.at[:, pl.ds(0, size)], sems.at[i]))
        start += size
    for copy in copies:
        copy.start()
    copies[0].wait()
    slots = prob_copy.shape[1]
    row = lax.broadcasted_iota(jnp.int32, (rows, slots), 0)
    lane = lax.broadcasted_iota(jnp.int32, (rows, slots), 1)
    prob = jnp.sum(jnp.where(row == lane, prob_copy[...], 0.0), axis=1, keepdims=True)
    column = lax.broadcasted_iota(jnp.int32, (rows, PROB_COLUMNS), 1)
    terms = jnp.zeros((rows, PROB_COLUMNS), jnp.float32)
    for i in range(3):
        term = prob.astype(jnp.bfloat16).astype(jnp.float32)
        prob = prob - term
        terms = jnp.where(column == i, term, terms)
    outs[-1][:, size:] = terms.astype(outs[-1].dtype)
    for copy in copies[1:]:
        copy.wait()


def resident_kernel(*refs):
    count = len(refs) // 2
    sems = refs[-1]
    copies = [pltpu.make_async_copy(refs[i], refs[count + i], sems.at[i]) for i in range(count)]
    for copy in copies:
        copy.start()
    for copy in copies:
        copy.wait()


def resident(*arrays):
    return call(
        resident_kernel,
        [pltpu.VMEM(a.shape, a.dtype) for a in arrays],
        [pltpu.with_memory_space_constraint(a, pltpu.HBM) for a in arrays],
        [HBM] * len(arrays),
        [pltpu.SemaphoreType.DMA((len(arrays),))],
        name="resident",
    )


def after(value, *others):
    return lax.optimization_barrier((value, *others))[0]


def coordinates():
    e = lax.axis_index("expert")
    b = lax.axis_index("batch")
    return e // 2, e % 2, b // 2, b % 2


def swap(flag, first, second):
    return jnp.where(flag, second, first), jnp.where(flag, first, second)


def add_product(start, size, tokens, gate_ref, up_ref, gate_acc, up_acc, fresh):
    step = size // 256 * 128
    for i in range(2):
        span = pl.ds(i * step, size - step if i else step)
        source = pl.ds(start + i * step, span.size)
        chunk = jnp.concatenate([ref[:, span] for ref in tokens], axis=0)
        for weight, acc in ((gate_ref, gate_acc), (up_ref, up_acc)):
            product = jnp.dot(chunk, weight[source, :], preferred_element_type=jnp.float32)
            if fresh and i == 0:
                acc[...] = product
            else:
                acc[...] += product


def first_product_kernel(size, *refs):
    *tokens, gate_ref, up_ref, gate_acc, up_acc = refs
    add_product(0, size, tokens, gate_ref, up_ref, gate_acc, up_acc, True)


def hidden_kernel_of_rest(start, size, counts_ref, *refs):
    *tokens, gate_ref, up_ref, gate_in, up_in, out_ref, gate_acc, up_acc = refs
    z, y, x, c = coordinates()
    live = tokens[0].shape[0]
    gate_acc[...] = gate_in[...]
    up_acc[...] = up_in[...]
    add_product(start, size, tokens, gate_ref, up_ref, gate_acc, up_acc, False)
    row = lax.broadcasted_iota(jnp.int32, (live, 1), 0)
    kept, sent = [], []
    for i, ref in enumerate(tokens):
        span = pl.ds(i * live, live)
        gate = gate_acc[span, :]
        hidden = gate / (1.0 + jnp.exp(-gate)) * up_acc[span, :]
        prob = jnp.sum(ref[:, size : size + 128].astype(jnp.float32), axis=1, keepdims=True)
        count = counts_ref[(x * 2 + c) ^ i, z * 2 + y]
        hidden = jnp.where(row < count, hidden * prob, 0.0)
        slots = hidden.reshape(2, 2, live // 4, -1)
        same, other = swap(y == 1, slots[:, 0], slots[:, 1])
        block = jnp.concatenate([same, other]).reshape(live, -1)
        (sent if i % 2 else kept).append(block)
    out_ref[...] = jnp.concatenate(kept + sent, axis=0).astype(out_ref.dtype)


def ordered_down_kernel(hidden_ref, down_ref, *outs):
    keep_first, send_first, keep_rest, send_rest = outs
    width = down_ref.shape[1]
    rows = keep_first.shape[0]
    half = hidden_ref.shape[0] // 2
    steps = 4
    for i in range(steps):
        span = pl.ds(i * (width // steps), width // steps)
        terms = jnp.dot(hidden_ref[...], down_ref[:, span], preferred_element_type=jnp.float32).astype(
            keep_first.dtype
        )
        for base, first, rest in ((0, keep_first, keep_rest), (half, send_first, send_rest)):
            first[:, span] = terms[base + 2 * rows : base + 3 * rows]
            rest[: 2 * rows, span] = terms[base : base + 2 * rows]
            rest[2 * rows :, span] = terms[base + 3 * rows : base + 4 * rows]


def put(out, rows):
    width = rows.shape[1]
    out[:, :width] = rows
    if out.shape[1] > width:
        out[:, width:] = jnp.zeros((rows.shape[0], out.shape[1] - width), out.dtype)


def core_sums_kernel(keep_ref, received_ref, *outs):
    rows = outs[0].shape[0]
    for i, out in enumerate(outs):
        span = pl.ds(i * rows, rows)
        total = keep_ref[span, :].astype(jnp.float32) + received_ref[span, :].astype(jnp.float32)
        put(out, total.astype(out.dtype))


def finish_kernel(first, second, near_ref, *fars):
    z, y, x, c = coordinates()
    slot, width = first.shape[0] // 2, first.shape[1]
    total = first[...].astype(jnp.float32) + second[:, :width].astype(jnp.float32)
    near, far = swap(z % 2 == 1, total[:slot], total[slot:])
    put(near_ref, near.astype(near_ref.dtype))
    for far_ref in fars:
        put(far_ref, far.astype(far_ref.dtype))


def run_copies(pairs, sems):
    copies = [pltpu.make_async_copy(source, target, sems.at[i]) for i, (source, target) in enumerate(pairs)]
    for copy in copies:
        copy.start()
    for copy in copies:
        copy.wait()


def place_kernel(layout, *refs):
    z, y, x, c = coordinates()
    pieces, (out_ref, zeros, sems) = refs[: len(layout)], refs[len(layout) :]
    width = out_ref.shape[2]
    for mine in range(2):

        @pl.when(z == mine)
        def _():
            pairs = []
            for (index, other), piece in zip(layout, pieces):
                source = (mine, 1 - mine, 2 + mine, 3 - mine)[index]
                pairs.append((piece.at[:, pl.ds(0, width)], out_ref.at[source * 2 + (y ^ other)]))
            run_copies(pairs, sems)

    @pl.when(z >= 2)
    def _():
        zeros[...] = jnp.zeros_like(zeros)
        run_copies([(zeros, out_ref.at[i]) for i in range(out_ref.shape[0])], sems)


def ports_body(tokens, route_prob, counts, w_gate, w_up, w_down):
    cap, width = tokens.shape[1:]
    units = w_gate.shape[2]
    rows = LIVE // 2
    both_axes = ("expert", "batch")

    def device(z, y, x, c):
        return (z * 2 + y) * 4 + x * 2 + c

    places = [(z, y, x, c) for z in range(4) for y in range(2) for x in range(2) for c in range(2)]

    def other_core(value):
        return lax.ppermute(value, "batch", xor_pairs(4, 1))

    def across_plane(value, dx, dy):
        return lax.ppermute(value, both_axes, [(device(*p), device(p[0], p[1] ^ dy, p[2] ^ dx, p[3])) for p in places])

    def along_z(value, *moves):
        pairs = [(device(s, *p[1:]), device(t, *p[1:])) for s, t in moves for p in places if p[0] == 0]
        return lax.ppermute(value, both_axes, pairs)

    def array(rows, columns, dtype=jnp.bfloat16):
        return jax.ShapeDtypeStruct((rows, columns), dtype)

    depth = (width + PROB_COLUMNS) // 2
    rest = width - depth
    own = call(
        live_rows_kernel,
        [pltpu.VMEM((LIVE, depth), tokens.dtype), pltpu.VMEM((LIVE, depth), tokens.dtype)],
        [pltpu.with_memory_space_constraint(a, pltpu.HBM) for a in (tokens, route_prob)],
        [HBM, HBM],
        [pltpu.VMEM(route_prob.shape, route_prob.dtype), pltpu.SemaphoreType.DMA((3,))],
        name="live_rows",
    )
    across = [lax.ppermute(piece, "batch", xor_pairs(4, 2)) for piece in own]
    near = [other_core(piece) for piece in own]
    gate_w, up_w = resident(after(w_gate[0], *own), w_up[0])
    down_w, = resident(after(w_down[0], gate_w))
    across = [after(piece, down_w) for piece in across]
    pieces = [[own[0], near[0], across[0], other_core(across[0])], None]
    gate, upper = call(
        lambda *refs: first_product_kernel(depth, *refs),
        [array(4 * LIVE, units, jnp.float32)] * 2,
        [*pieces[0], gate_w, up_w],
        name="first_product",
    )
    pieces[1] = [own[1], near[1], across[1], other_core(across[1])]
    hidden = call(
        lambda *refs: hidden_kernel_of_rest(depth, rest, *refs),
        array(4 * LIVE, units),
        [counts.T, *pieces[1], gate_w, up_w, gate, upper],
        [SMEM] + [VMEM] * 8,
        scratch=[pltpu.VMEM((4 * LIVE, units), jnp.float32)] * 2,
        name="hidden",
    )

    slot = rows // 2
    keep_first, send_first, keep_rest, send_rest = call(
        ordered_down_kernel,
        [array(rows, width), array(rows, width), array(3 * rows, width), array(3 * rows, width)],
        [hidden, down_w],
        name="down",
    )
    across_same, = call(core_sums_kernel, [array(rows, width)], [keep_first, other_core(send_first)], name="core_sums")
    from_x = across_plane(across_same, 1, 0)
    own_same, own_other, across_other = call(
        core_sums_kernel,
        [array(rows, width), array(rows, width + 128), array(rows, width)],
        [keep_rest, other_core(after(send_rest, across_same))],
        name="core_sums",
    )
    from_y = across_plane(own_other, 0, 1)
    diagonal = across_plane(across_other, 1, 1)
    near_1, far_1, next_1 = call(
        finish_kernel, [array(slot, width + n) for n in (256, 256, 384)], [own_same, from_x], name="finish"
    )
    near_2, far_2, next_2 = call(
        finish_kernel, [array(slot, width + n) for n in (128, 128, 0)], [diagonal, from_y], name="finish"
    )
    pieces = [near_1, near_2]
    pieces += [along_z(rows, (2, 0), (3, 1)) for rows in (near_1, near_2)]
    pieces += [along_z(rows, (2, 1), (3, 0)) for rows in (far_1, far_2)]
    pieces += [along_z(rows, (0, 1), (1, 0)) for rows in (next_1, next_2)]
    layout = [(index, other) for index in (0, 2, 3, 1) for other in (0, 1)]
    out = call(
        lambda *refs: place_kernel(layout, *refs),
        jax.ShapeDtypeStruct((cap // slot, slot, width), jnp.bfloat16),
        pieces,
        [ANY] * len(pieces),
        [pltpu.VMEM((slot, width), jnp.bfloat16), pltpu.SemaphoreType.DMA((len(pieces),))],
        out_specs=HBM,
        name="place",
    )
    return out.reshape(1, cap, width)


def solution(mesh):
    in_specs = (
        P("expert", "batch", None),
        P("expert", "batch"),
        P(),
        P("expert", None, "batch"),
        P("expert", None, "batch"),
        P("expert", "batch", None),
    )
    out_specs = P("expert", "batch", None)
    fits = dict(mesh.shape) == {"expert": 8, "batch": 4}
    body = ports_body if fits else general_body
    return jax.shard_map(body, mesh=mesh, in_specs=in_specs, out_specs=out_specs, check_vma=False)
```

```python
import jax
import jax.numpy as jnp
from jax import lax
from jax.experimental import pallas as pl
from jax.experimental.pallas import tpu as pltpu
from jax.sharding import PartitionSpec as P

LIVE = 32
PROB_COLUMNS = 256
PARTS = 2
VMEM_LIMIT = 16 * 2**20
VMEM = pl.BlockSpec(memory_space=pltpu.VMEM)
HBM = pl.BlockSpec(memory_space=pltpu.HBM)
ANY = pl.BlockSpec(memory_space=pl.ANY)
SMEM = pl.BlockSpec(memory_space=pltpu.SMEM)


def xor_pairs(size, offset):
    return [(i, i ^ offset) for i in range(size)]


def hidden_kernel(pieces, *refs):
    token_refs = refs[:pieces]
    gate_ref, up_ref, out_ref, gate_acc, up_acc = refs[pieces:]
    live = token_refs[0].shape[0]
    width = gate_ref.shape[0]
    step = width // 4

    def add(start, first):
        span = pl.ds(start, step)
        rows = jnp.concatenate([ref[:, span] for ref in token_refs], axis=0)
        gate = jnp.dot(rows, gate_ref[span, :], preferred_element_type=jnp.float32)
        upper = jnp.dot(rows, up_ref[span, :], preferred_element_type=jnp.float32)
        if first:
            gate_acc[...] = gate
            up_acc[...] = upper
        else:
            gate_acc[...] += gate
            up_acc[...] += upper

    add(0, True)

    @pl.loop(1, width // step)
    def _(i):
        add(pl.multiple_of(i * step, step), False)

    gate = gate_acc[...]
    out_ref[...] = (gate / (1.0 + jnp.exp(-gate)) * up_acc[...]).astype(out_ref.dtype)


def hidden_units(pieces, gate_w, up_w):
    live, width = pieces[0].shape
    units = gate_w.shape[1]
    rows = live * len(pieces)
    return pl.pallas_call(
        lambda *refs: hidden_kernel(len(pieces), *refs),
        out_shape=jax.ShapeDtypeStruct((rows, units), jnp.bfloat16),
        in_specs=[VMEM] * (len(pieces) + 2),
        out_specs=VMEM,
        scratch_shapes=[pltpu.VMEM((rows, units), jnp.float32)] * 2,
        compiler_params=pltpu.CompilerParams(vmem_limit_bytes=VMEM_LIMIT),
        cost_estimate=pl.CostEstimate(
            flops=4 * rows * width * units, bytes_accessed=4 * width * units, transcendentals=rows * units
        ),
        name="hidden_units",
    )(*pieces, gate_w, up_w)


def down_kernel(start, hidden_ref, down_ref, keep_ref, send_ref):
    width = keep_ref.shape[1]
    half = keep_ref.shape[0]
    step = width // 2

    @pl.loop(0, width // step)
    def _(i):
        span = pl.ds(pl.multiple_of(i * step, step), step)
        source = pl.ds(pl.multiple_of(start + i * step, step), step)
        terms = jnp.dot(hidden_ref[...], down_ref[:, source], preferred_element_type=jnp.float32).astype(
            keep_ref.dtype
        )
        keep_ref[:, span] = terms[:half]
        send_ref[:, span] = terms[half:]


def down_part(hidden, down_w, start, width):
    rows, units = hidden.shape
    shape = jax.ShapeDtypeStruct((rows // 2, width), jnp.bfloat16)
    return pl.pallas_call(
        lambda *refs: down_kernel(start, *refs),
        out_shape=[shape, shape],
        in_specs=[VMEM] * 2,
        out_specs=[VMEM] * 2,
        compiler_params=pltpu.CompilerParams(vmem_limit_bytes=VMEM_LIMIT),
        cost_estimate=pl.CostEstimate(
            flops=2 * rows * width * units, bytes_accessed=2 * width * units, transcendentals=0
        ),
        name="down_part",
    )(hidden, down_w)


def general_body(tokens, route_prob, counts, w_gate, w_up, w_down):
    cap, width = tokens.shape[1:]
    n_batch = lax.axis_size("batch")
    n_experts = lax.axis_size("expert")
    expert_id = lax.axis_index("expert")
    batch_id = lax.axis_index("batch")
    slot = cap // n_experts
    live_slots = LIVE // slot
    part = width // PARTS

    own = tokens[0, :LIVE]
    even = [own] + [lax.ppermute(own, "batch", xor_pairs(n_batch, d)) for d in range(2, n_batch, 2)]
    odd = [lax.ppermute(piece, "batch", xor_pairs(n_batch, 1)) for piece in even]
    hidden = hidden_units(even + odd, w_gate[0], w_up[0])

    count = counts[expert_id, batch_id]
    live = jnp.arange(LIVE, dtype=jnp.int32) < count
    scale = jnp.where(live, route_prob[0, :LIVE], 0.0)[:, None]

    columns = []
    for start in range(0, width, part):
        keep, send = down_part(hidden, w_down[0], start, part)
        received = lax.ppermute(send, "batch", xor_pairs(n_batch, 1))
        both = keep.astype(jnp.float32) + received.astype(jnp.float32)
        total = both[:LIVE]
        for i, d in enumerate(range(2, n_batch, 2), 1):
            term = both[i * LIVE : (i + 1) * LIVE].astype(jnp.bfloat16)
            total += lax.ppermute(term, "batch", xor_pairs(n_batch, d)).astype(jnp.float32)
        expert_out = jnp.where(live[:, None], scale * total, 0.0).astype(jnp.bfloat16)
        grouped = expert_out.reshape(live_slots, slot, part)

        picks = {}
        for d in sorted(range(1, n_experts), key=lambda d: (-(d // live_slots), d)):
            pairs = [(e, e ^ d) for e in range(n_experts) if e ^ d < live_slots]
            target = jnp.minimum(expert_id ^ d, live_slots - 1)
            payload = lax.dynamic_index_in_dim(grouped, target, 0, keepdims=False)
            picks[d] = lax.ppermute(payload, "expert", pairs)
        mine = lax.dynamic_index_in_dim(grouped, jnp.minimum(expert_id, live_slots - 1), 0, keepdims=False)
        picks[0] = jnp.where(expert_id < live_slots, mine, jnp.zeros_like(mine))
        stacked = jnp.stack([picks[d] for d in range(n_experts)])
        columns.append(jnp.take(stacked, jnp.arange(n_experts, dtype=jnp.int32) ^ expert_id, axis=0))
    returned = jnp.concatenate(columns, axis=-1)
    return returned.reshape(1, cap, width)


def call(kernel, outs, args, specs=None, scratch=(), out_specs=None, cost=0, aliases=None, name=None):
    return pl.pallas_call(
        kernel,
        out_shape=outs,
        in_specs=specs or [VMEM] * len(args),
        out_specs=out_specs or jax.tree.map(lambda _: VMEM, outs),
        scratch_shapes=list(scratch),
        input_output_aliases=aliases or {},
        compiler_params=pltpu.CompilerParams(vmem_limit_bytes=VMEM_LIMIT),
        cost_estimate=pl.CostEstimate(flops=0, bytes_accessed=cost, transcendentals=0),
        name=name,
    )(*args)


def live_rows_kernel(tokens_ref, prob_ref, *refs):
    *outs, prob_copy, sems = refs
    rows = outs[0].shape[0]
    copies = [pltpu.make_async_copy(prob_ref, prob_copy, sems.at[len(outs)])]
    start = 0
    for i, out in enumerate(outs):
        size = out.shape[1] - (PROB_COLUMNS if i == len(outs) - 1 else 0)
        source = tokens_ref.at[0, pl.ds(0, rows), pl.ds(start, size)]
        copies.append(pltpu.make_async_copy(source, out.at[:, pl.ds(0, size)], sems.at[i]))
        start += size
    for copy in copies:
        copy.start()
    copies[0].wait()
    slots = prob_copy.shape[1]
    row = lax.broadcasted_iota(jnp.int32, (rows, slots), 0)
    lane = lax.broadcasted_iota(jnp.int32, (rows, slots), 1)
    prob = jnp.sum(jnp.where(row == lane, prob_copy[...], 0.0), axis=1, keepdims=True)
    column = lax.broadcasted_iota(jnp.int32, (rows, PROB_COLUMNS), 1)
    terms = jnp.zeros((rows, PROB_COLUMNS), jnp.float32)
    for i in range(3):
        term = prob.astype(jnp.bfloat16).astype(jnp.float32)
        prob = prob - term
        terms = jnp.where(column == i, term, terms)
    outs[-1][:, size:] = terms.astype(outs[-1].dtype)
    for copy in copies[1:]:
        copy.wait()


def resident_kernel(*refs):
    count = len(refs) // 2
    sems = refs[-1]
    copies = [pltpu.make_async_copy(refs[i], refs[count + i], sems.at[i]) for i in range(count)]
    for copy in copies:
        copy.start()
    for copy in copies:
        copy.wait()


def resident(*arrays):
    return call(
        resident_kernel,
        [pltpu.VMEM(a.shape, a.dtype) for a in arrays],
        [pltpu.with_memory_space_constraint(a, pltpu.HBM) for a in arrays],
        [HBM] * len(arrays),
        [pltpu.SemaphoreType.DMA((len(arrays),))],
        name="resident",
    )


def after(value, *others):
    return lax.optimization_barrier((value, *others))[0]


def coordinates():
    e = lax.axis_index("expert")
    b = lax.axis_index("batch")
    return e // 2, e % 2, b // 2, b % 2


def swap(flag, first, second):
    return jnp.where(flag, second, first), jnp.where(flag, first, second)


def add_product(start, size, tokens, gate_ref, up_ref, gate_acc, up_acc, fresh):
    step = size // 256 * 128
    for i in range(2):
        span = pl.ds(i * step, size - step if i else step)
        source = pl.ds(start + i * step, span.size)
        chunk = jnp.concatenate([ref[:, span] for ref in tokens], axis=0)
        for weight, acc in ((gate_ref, gate_acc), (up_ref, up_acc)):
            product = jnp.dot(chunk, weight[source, :], preferred_element_type=jnp.float32)
            if fresh and i == 0:
                acc[...] = product
            else:
                acc[...] += product


def first_product_kernel(size, *refs):
    *tokens, gate_ref, up_ref, gate_acc, up_acc = refs
    add_product(0, size, tokens, gate_ref, up_ref, gate_acc, up_acc, True)


def hidden_kernel_of_rest(start, size, counts_ref, *refs):
    *tokens, gate_ref, up_ref, gate_in, up_in, out_ref, gate_acc, up_acc = refs
    z, y, x, c = coordinates()
    live = tokens[0].shape[0]
    gate_acc[...] = gate_in[...]
    up_acc[...] = up_in[...]
    add_product(start, size, tokens, gate_ref, up_ref, gate_acc, up_acc, False)
    row = lax.broadcasted_iota(jnp.int32, (live, 1), 0)
    kept, sent = [], []
    for i, ref in enumerate(tokens):
        span = pl.ds(i * live, live)
        gate = gate_acc[span, :]
        hidden = gate / (1.0 + jnp.exp(-gate)) * up_acc[span, :]
        prob = jnp.sum(ref[:, size : size + 128].astype(jnp.float32), axis=1, keepdims=True)
        count = counts_ref[(x * 2 + c) ^ i, z * 2 + y]
        hidden = jnp.where(row < count, hidden * prob, 0.0)
        slots = hidden.reshape(2, 2, live // 4, -1)
        same, other = swap(y == 1, slots[:, 0], slots[:, 1])
        block = jnp.concatenate([same, other]).reshape(live, -1)
        (sent if i % 2 else kept).append(block)
    out_ref[...] = jnp.concatenate(kept + sent, axis=0).astype(out_ref.dtype)


def ordered_down_kernel(hidden_ref, down_ref, *outs):
    keep_first, send_first, keep_rest, send_rest = outs
    width = down_ref.shape[1]
    rows = keep_first.shape[0]
    half = hidden_ref.shape[0] // 2
    steps = 4
    for i in range(steps):
        span = pl.ds(i * (width // steps), width // steps)
        terms = jnp.dot(hidden_ref[...], down_ref[:, span], preferred_element_type=jnp.float32).astype(
            keep_first.dtype
        )
        for base, first, rest in ((0, keep_first, keep_rest), (half, send_first, send_rest)):
            first[:, span] = terms[base + 2 * rows : base + 3 * rows]
            rest[: 2 * rows, span] = terms[base : base + 2 * rows]
            rest[2 * rows :, span] = terms[base + 3 * rows : base + 4 * rows]


def put(out, rows):
    width = min(rows.shape[1], out.shape[1])
    out[:, :width] = rows[:, :width]
    if out.shape[1] > width:
        out[:, width:] = jnp.zeros((rows.shape[0], out.shape[1] - width), out.dtype)


def core_sum(keep_ref, received_ref, start, rows):
    span = pl.ds(start, rows)
    return keep_ref[span, :].astype(jnp.float32) + received_ref[span, :].astype(jnp.float32)


def by_z(rows):
    z, y, x, c = coordinates()
    slot = rows.shape[0] // 2
    return swap(z % 2 == 1, rows[:slot], rows[slot:])


def first_sums_kernel(keep_ref, received_ref, near_ref, far_ref):
    near, far = by_z(core_sum(keep_ref, received_ref, 0, keep_ref.shape[0]))
    put(near_ref, near.astype(near_ref.dtype))
    put(far_ref, far.astype(far_ref.dtype))


def other_sums_kernel(keep_ref, received_ref, near_ref, far_ref, along_ref, diagonal_ref):
    rows = along_ref.shape[0]
    near, far = by_z(core_sum(keep_ref, received_ref, 0, rows))
    near_ref[...] = near.astype(near_ref.dtype)
    far_ref[...] = far.astype(far_ref.dtype)
    put(along_ref, core_sum(keep_ref, received_ref, rows, rows).astype(along_ref.dtype))
    put(diagonal_ref, core_sum(keep_ref, received_ref, 2 * rows, rows).astype(diagonal_ref.dtype))


def add_kernel(first, second, *outs):
    width = first.shape[1]
    total = first[...].astype(jnp.float32) + second[:, :width].astype(jnp.float32)
    for out in outs:
        put(out, total.astype(out.dtype))


def add_by_z_kernel(first, second, *outs):
    width = first.shape[1]
    near, far = by_z(first[...].astype(jnp.float32) + second[:, :width].astype(jnp.float32))
    put(outs[0], near.astype(outs[0].dtype))
    for out in outs[1:]:
        put(out, far.astype(out.dtype))


def run_copies(pairs, sems):
    copies = [pltpu.make_async_copy(source, target, sems.at[i]) for i, (source, target) in enumerate(pairs)]
    for copy in copies:
        copy.start()
    for copy in copies:
        copy.wait()


def place_kernel(layout, *refs):
    z, y, x, c = coordinates()
    pieces, (_, out_ref, zeros, sems) = refs[: len(layout)], refs[len(layout) :]
    width = out_ref.shape[2]
    for mine in range(2):

        @pl.when(z == mine)
        def _():
            pairs = []
            for (index, other), piece in zip(layout, pieces):
                source = (mine, 1 - mine, 2 + mine, 3 - mine)[index]
                pairs.append((piece.at[:, pl.ds(0, width)], out_ref.at[source * 2 + (y ^ other)]))
            run_copies(pairs, sems)

    @pl.when(z >= 2)
    def _():
        zeros[...] = jnp.zeros_like(zeros)
        run_copies([(zeros, out_ref.at[i]) for i in range(out_ref.shape[0])], sems)


def ports_body(tokens, route_prob, counts, w_gate, w_up, w_down):
    cap, width = tokens.shape[1:]
    units = w_gate.shape[2]
    rows = LIVE // 2
    both_axes = ("expert", "batch")

    def device(z, y, x, c):
        return (z * 2 + y) * 4 + x * 2 + c

    places = [(z, y, x, c) for z in range(4) for y in range(2) for x in range(2) for c in range(2)]

    def other_core(value):
        return lax.ppermute(value, "batch", xor_pairs(4, 1))

    def across_plane(value, dx, dy):
        return lax.ppermute(value, both_axes, [(device(*p), device(p[0], p[1] ^ dy, p[2] ^ dx, p[3])) for p in places])

    def along_z(value, *moves):
        pairs = [(device(s, *p[1:]), device(t, *p[1:])) for s, t in moves for p in places if p[0] == 0]
        return lax.ppermute(value, both_axes, pairs)

    def array(rows, columns, dtype=jnp.bfloat16):
        return jax.ShapeDtypeStruct((rows, columns), dtype)

    depth = (width + PROB_COLUMNS) // 2
    rest = width - depth
    own = call(
        live_rows_kernel,
        [pltpu.VMEM((LIVE, depth), tokens.dtype), pltpu.VMEM((LIVE, depth), tokens.dtype)],
        [pltpu.with_memory_space_constraint(a, pltpu.HBM) for a in (tokens, route_prob)],
        [HBM, HBM],
        [pltpu.VMEM(route_prob.shape, route_prob.dtype), pltpu.SemaphoreType.DMA((3,))],
        name="live_rows",
    )
    across = [lax.ppermute(piece, "batch", xor_pairs(4, 2)) for piece in own]
    near = [other_core(piece) for piece in own]
    gate_w, up_w = resident(after(w_gate[0], *own), w_up[0])
    down_w, = resident(after(w_down[0], gate_w))
    across = [after(piece, down_w) for piece in across]
    pieces = [[own[0], near[0], across[0], other_core(across[0])], None]
    gate, upper = call(
        lambda *refs: first_product_kernel(depth, *refs),
        [array(4 * LIVE, units, jnp.float32)] * 2,
        [*pieces[0], gate_w, up_w],
        name="first_product",
    )
    pieces[1] = [own[1], near[1], across[1], other_core(across[1])]
    hidden = call(
        lambda *refs: hidden_kernel_of_rest(depth, rest, *refs),
        array(4 * LIVE, units),
        [counts.T, *pieces[1], gate_w, up_w, gate, upper],
        [SMEM] + [VMEM] * 8,
        scratch=[pltpu.VMEM((4 * LIVE, units), jnp.float32)] * 2,
        name="hidden",
    )

    slot = rows // 2
    keep_first, send_first, keep_rest, send_rest = call(
        ordered_down_kernel,
        [array(rows, width), array(rows, width), array(3 * rows, width), array(3 * rows, width)],
        [hidden, down_w],
        name="down",
    )
    near_x, far_x = call(
        first_sums_kernel,
        [array(slot, width + n) for n in (384, 384)],
        [keep_first, other_core(send_first)],
        name="first_sums",
    )
    own_near, own_far, own_other, across_other = call(
        other_sums_kernel,
        [array(slot, width), array(slot, width), array(rows, width + 128), array(rows, width)],
        [keep_rest, other_core(after(send_rest, near_x))],
        name="other_sums",
    )
    near_1, = call(
        add_kernel, [array(slot, width + 384)], [own_near, across_plane(near_x, 1, 0)], name="near_rows"
    )
    far_1, next_1 = call(
        add_kernel, [array(slot, width + n) for n in (128, 0)], [own_far, across_plane(far_x, 1, 0)], name="far_rows"
    )
    from_2 = [along_z(near_1, (2, 0), (3, 1))]
    from_3 = [along_z(far_1, (2, 1), (3, 0))]
    next_z = [along_z(next_1, (0, 1), (1, 0))]
    from_y = across_plane(own_other, 0, 1)
    diagonal = across_plane(across_other, 1, 1)
    diagonal, next_z[0] = lax.optimization_barrier((diagonal, next_z[0]))
    near_2, far_2, next_2, mark = call(
        add_by_z_kernel, [array(slot, width + n) for n in (128, 128, 0, -128)], [diagonal, from_y], name="other_rows"
    )
    from_2.append(along_z(near_2, (2, 0), (3, 1)))
    from_3.append(along_z(far_2, (2, 1), (3, 0)))
    next_z.append(along_z(next_2, (0, 1), (1, 0)))
    mark = other_core(after(mark, from_2[0], from_3[0]))
    pieces = [near_1, near_2, *from_2, *from_3, *next_z]
    layout = [(index, other) for index in (0, 2, 3, 1) for other in (0, 1)]
    out = call(
        lambda *refs: place_kernel(layout, *refs),
        jax.ShapeDtypeStruct((cap // slot, slot, width), jnp.bfloat16),
        [*pieces, mark],
        [ANY] * (len(pieces) + 1),
        [pltpu.VMEM((slot, width), jnp.bfloat16), pltpu.SemaphoreType.DMA((len(pieces),))],
        out_specs=HBM,
        name="place",
    )
    return out.reshape(1, cap, width)


def solution(mesh):
    in_specs = (
        P("expert", "batch", None),
        P("expert", "batch"),
        P(),
        P("expert", None, "batch"),
        P("expert", None, "batch"),
        P("expert", "batch", None),
    )
    out_specs = P("expert", "batch", None)
    fits = dict(mesh.shape) == {"expert": 8, "batch": 4}
    body = ports_body if fits else general_body
    return jax.shard_map(body, mesh=mesh, in_specs=in_specs, out_specs=out_specs, check_vma=False)
```

```python
import jax
import jax.numpy as jnp
from jax import lax
from jax.experimental import pallas as pl
from jax.experimental.pallas import tpu as pltpu
from jax.sharding import PartitionSpec as P

LIVE = 32
PROB_COLUMNS = 256
PARTS = 2
VMEM_LIMIT = 16 * 2**20
VMEM = pl.BlockSpec(memory_space=pltpu.VMEM)
HBM = pl.BlockSpec(memory_space=pltpu.HBM)
ANY = pl.BlockSpec(memory_space=pl.ANY)
SMEM = pl.BlockSpec(memory_space=pltpu.SMEM)


def xor_pairs(size, offset):
    return [(i, i ^ offset) for i in range(size)]


def hidden_kernel(pieces, *refs):
    token_refs = refs[:pieces]
    gate_ref, up_ref, out_ref, gate_acc, up_acc = refs[pieces:]
    live = token_refs[0].shape[0]
    width = gate_ref.shape[0]
    step = width // 4

    def add(start, first):
        span = pl.ds(start, step)
        rows = jnp.concatenate([ref[:, span] for ref in token_refs], axis=0)
        gate = jnp.dot(rows, gate_ref[span, :], preferred_element_type=jnp.float32)
        upper = jnp.dot(rows, up_ref[span, :], preferred_element_type=jnp.float32)
        if first:
            gate_acc[...] = gate
            up_acc[...] = upper
        else:
            gate_acc[...] += gate
            up_acc[...] += upper

    add(0, True)

    @pl.loop(1, width // step)
    def _(i):
        add(pl.multiple_of(i * step, step), False)

    gate = gate_acc[...]
    out_ref[...] = (gate / (1.0 + jnp.exp(-gate)) * up_acc[...]).astype(out_ref.dtype)


def hidden_units(pieces, gate_w, up_w):
    live, width = pieces[0].shape
    units = gate_w.shape[1]
    rows = live * len(pieces)
    return pl.pallas_call(
        lambda *refs: hidden_kernel(len(pieces), *refs),
        out_shape=jax.ShapeDtypeStruct((rows, units), jnp.bfloat16),
        in_specs=[VMEM] * (len(pieces) + 2),
        out_specs=VMEM,
        scratch_shapes=[pltpu.VMEM((rows, units), jnp.float32)] * 2,
        compiler_params=pltpu.CompilerParams(vmem_limit_bytes=VMEM_LIMIT),
        cost_estimate=pl.CostEstimate(
            flops=4 * rows * width * units, bytes_accessed=4 * width * units, transcendentals=rows * units
        ),
        name="hidden_units",
    )(*pieces, gate_w, up_w)


def down_kernel(start, hidden_ref, down_ref, keep_ref, send_ref):
    width = keep_ref.shape[1]
    half = keep_ref.shape[0]
    step = width // 2

    @pl.loop(0, width // step)
    def _(i):
        span = pl.ds(pl.multiple_of(i * step, step), step)
        source = pl.ds(pl.multiple_of(start + i * step, step), step)
        terms = jnp.dot(hidden_ref[...], down_ref[:, source], preferred_element_type=jnp.float32).astype(
            keep_ref.dtype
        )
        keep_ref[:, span] = terms[:half]
        send_ref[:, span] = terms[half:]


def down_part(hidden, down_w, start, width):
    rows, units = hidden.shape
    shape = jax.ShapeDtypeStruct((rows // 2, width), jnp.bfloat16)
    return pl.pallas_call(
        lambda *refs: down_kernel(start, *refs),
        out_shape=[shape, shape],
        in_specs=[VMEM] * 2,
        out_specs=[VMEM] * 2,
        compiler_params=pltpu.CompilerParams(vmem_limit_bytes=VMEM_LIMIT),
        cost_estimate=pl.CostEstimate(
            flops=2 * rows * width * units, bytes_accessed=2 * width * units, transcendentals=0
        ),
        name="down_part",
    )(hidden, down_w)


def general_body(tokens, route_prob, counts, w_gate, w_up, w_down):
    cap, width = tokens.shape[1:]
    n_batch = lax.axis_size("batch")
    n_experts = lax.axis_size("expert")
    expert_id = lax.axis_index("expert")
    batch_id = lax.axis_index("batch")
    slot = cap // n_experts
    live_slots = LIVE // slot
    part = width // PARTS

    own = tokens[0, :LIVE]
    even = [own] + [lax.ppermute(own, "batch", xor_pairs(n_batch, d)) for d in range(2, n_batch, 2)]
    odd = [lax.ppermute(piece, "batch", xor_pairs(n_batch, 1)) for piece in even]
    hidden = hidden_units(even + odd, w_gate[0], w_up[0])

    count = counts[expert_id, batch_id]
    live = jnp.arange(LIVE, dtype=jnp.int32) < count
    scale = jnp.where(live, route_prob[0, :LIVE], 0.0)[:, None]

    columns = []
    for start in range(0, width, part):
        keep, send = down_part(hidden, w_down[0], start, part)
        received = lax.ppermute(send, "batch", xor_pairs(n_batch, 1))
        both = keep.astype(jnp.float32) + received.astype(jnp.float32)
        total = both[:LIVE]
        for i, d in enumerate(range(2, n_batch, 2), 1):
            term = both[i * LIVE : (i + 1) * LIVE].astype(jnp.bfloat16)
            total += lax.ppermute(term, "batch", xor_pairs(n_batch, d)).astype(jnp.float32)
        expert_out = jnp.where(live[:, None], scale * total, 0.0).astype(jnp.bfloat16)
        grouped = expert_out.reshape(live_slots, slot, part)

        picks = {}
        for d in sorted(range(1, n_experts), key=lambda d: (-(d // live_slots), d)):
            pairs = [(e, e ^ d) for e in range(n_experts) if e ^ d < live_slots]
            target = jnp.minimum(expert_id ^ d, live_slots - 1)
            payload = lax.dynamic_index_in_dim(grouped, target, 0, keepdims=False)
            picks[d] = lax.ppermute(payload, "expert", pairs)
        mine = lax.dynamic_index_in_dim(grouped, jnp.minimum(expert_id, live_slots - 1), 0, keepdims=False)
        picks[0] = jnp.where(expert_id < live_slots, mine, jnp.zeros_like(mine))
        stacked = jnp.stack([picks[d] for d in range(n_experts)])
        columns.append(jnp.take(stacked, jnp.arange(n_experts, dtype=jnp.int32) ^ expert_id, axis=0))
    returned = jnp.concatenate(columns, axis=-1)
    return returned.reshape(1, cap, width)


def call(kernel, outs, args, specs=None, scratch=(), out_specs=None, cost=0, aliases=None, name=None):
    return pl.pallas_call(
        kernel,
        out_shape=outs,
        in_specs=specs or [VMEM] * len(args),
        out_specs=out_specs or jax.tree.map(lambda _: VMEM, outs),
        scratch_shapes=list(scratch),
        input_output_aliases=aliases or {},
        compiler_params=pltpu.CompilerParams(vmem_limit_bytes=VMEM_LIMIT),
        cost_estimate=pl.CostEstimate(flops=0, bytes_accessed=cost, transcendentals=0),
        name=name,
    )(*args)


def live_rows_kernel(tokens_ref, prob_ref, *refs):
    *outs, prob_copy, sems = refs
    rows = outs[0].shape[0]
    copies = [pltpu.make_async_copy(prob_ref, prob_copy, sems.at[len(outs)])]
    start = 0
    for i, out in enumerate(outs):
        size = out.shape[1] - (PROB_COLUMNS if i == len(outs) - 1 else 0)
        source = tokens_ref.at[0, pl.ds(0, rows), pl.ds(start, size)]
        copies.append(pltpu.make_async_copy(source, out.at[:, pl.ds(0, size)], sems.at[i]))
        start += size
    for copy in copies:
        copy.start()
    copies[0].wait()
    slots = prob_copy.shape[1]
    row = lax.broadcasted_iota(jnp.int32, (rows, slots), 0)
    lane = lax.broadcasted_iota(jnp.int32, (rows, slots), 1)
    prob = jnp.sum(jnp.where(row == lane, prob_copy[...], 0.0), axis=1, keepdims=True)
    column = lax.broadcasted_iota(jnp.int32, (rows, PROB_COLUMNS), 1)
    terms = jnp.zeros((rows, PROB_COLUMNS), jnp.float32)
    for i in range(3):
        term = prob.astype(jnp.bfloat16).astype(jnp.float32)
        prob = prob - term
        terms = jnp.where(column == i, term, terms)
    outs[-1][:, size:] = terms.astype(outs[-1].dtype)
    for copy in copies[1:]:
        copy.wait()


def resident_kernel(*refs):
    count = len(refs) // 2
    sems = refs[-1]
    copies = [pltpu.make_async_copy(refs[i], refs[count + i], sems.at[i]) for i in range(count)]
    for copy in copies:
        copy.start()
    for copy in copies:
        copy.wait()


def resident(*arrays):
    return call(
        resident_kernel,
        [pltpu.VMEM(a.shape, a.dtype) for a in arrays],
        [pltpu.with_memory_space_constraint(a, pltpu.HBM) for a in arrays],
        [HBM] * len(arrays),
        [pltpu.SemaphoreType.DMA((len(arrays),))],
        name="resident",
    )


def after(value, *others):
    return lax.optimization_barrier((value, *others))[0]


def coordinates():
    e = lax.axis_index("expert")
    b = lax.axis_index("batch")
    return e // 2, e % 2, b // 2, b % 2


def swap(flag, first, second):
    return jnp.where(flag, second, first), jnp.where(flag, first, second)


def add_product(start, size, tokens, gate_ref, up_ref, gate_acc, up_acc, fresh):
    step = size // 256 * 128
    for i in range(2):
        span = pl.ds(i * step, size - step if i else step)
        source = pl.ds(start + i * step, span.size)
        chunk = jnp.concatenate([ref[:, span] for ref in tokens], axis=0)
        for weight, acc in ((gate_ref, gate_acc), (up_ref, up_acc)):
            product = jnp.dot(chunk, weight[source, :], preferred_element_type=jnp.float32)
            if fresh and i == 0:
                acc[...] = product
            else:
                acc[...] += product


def first_product_kernel(size, *refs):
    *tokens, gate_ref, up_ref, gate_acc, up_acc = refs
    add_product(0, size, tokens, gate_ref, up_ref, gate_acc, up_acc, True)


def hidden_kernel_of_rest(start, size, counts_ref, *refs):
    *tokens, gate_ref, up_ref, gate_in, up_in, out_ref, gate_acc, up_acc = refs
    z, y, x, c = coordinates()
    live = tokens[0].shape[0]
    gate_acc[...] = gate_in[...]
    up_acc[...] = up_in[...]
    add_product(start, size, tokens, gate_ref, up_ref, gate_acc, up_acc, False)
    row = lax.broadcasted_iota(jnp.int32, (live, 1), 0)
    kept, sent = [], []
    for i, ref in enumerate(tokens):
        span = pl.ds(i * live, live)
        gate = gate_acc[span, :]
        hidden = gate / (1.0 + jnp.exp(-gate)) * up_acc[span, :]
        prob = jnp.sum(ref[:, size : size + 128].astype(jnp.float32), axis=1, keepdims=True)
        count = counts_ref[(x * 2 + c) ^ i, z * 2 + y]
        hidden = jnp.where(row < count, hidden * prob, 0.0)
        slots = hidden.reshape(2, 2, live // 4, -1)
        same, other = swap(y == 1, slots[:, 0], slots[:, 1])
        block = jnp.concatenate([same, other]).reshape(live, -1)
        (sent if i % 2 else kept).append(block)
    out_ref[...] = jnp.concatenate(kept + sent, axis=0).astype(out_ref.dtype)


def ordered_down_kernel(hidden_ref, down_ref, *outs):
    keep_first, send_first, keep_rest, send_rest = outs
    width = down_ref.shape[1]
    rows = keep_first.shape[0]
    half = hidden_ref.shape[0] // 2
    steps = 4
    for i in range(steps):
        span = pl.ds(i * (width // steps), width // steps)
        terms = jnp.dot(hidden_ref[...], down_ref[:, span], preferred_element_type=jnp.float32).astype(
            keep_first.dtype
        )
        for base, first, rest in ((0, keep_first, keep_rest), (half, send_first, send_rest)):
            first[:, span] = terms[base + 2 * rows : base + 3 * rows]
            rest[: 2 * rows, span] = terms[base : base + 2 * rows]
            rest[2 * rows :, span] = terms[base + 3 * rows : base + 4 * rows]


def put(out, rows):
    width = min(rows.shape[1], out.shape[1])
    out[:, :width] = rows[:, :width]
    if out.shape[1] > width:
        out[:, width:] = jnp.zeros((rows.shape[0], out.shape[1] - width), out.dtype)


def core_sum(keep_ref, received_ref, start, rows):
    span = pl.ds(start, rows)
    return keep_ref[span, :].astype(jnp.float32) + received_ref[span, :].astype(jnp.float32)


def by_z(rows):
    z, y, x, c = coordinates()
    slot = rows.shape[0] // 2
    return swap((z == 0) | (z == 3), rows[:slot], rows[slot:])


def first_sums_kernel(keep_ref, received_ref, near_ref, far_ref):
    near, far = by_z(core_sum(keep_ref, received_ref, 0, keep_ref.shape[0]))
    put(near_ref, near.astype(near_ref.dtype))
    put(far_ref, far.astype(far_ref.dtype))


def other_sums_kernel(keep_ref, received_ref, near_ref, far_ref, along_ref, diagonal_ref):
    rows = along_ref.shape[0]
    near, far = by_z(core_sum(keep_ref, received_ref, 0, rows))
    near_ref[...] = near.astype(near_ref.dtype)
    far_ref[...] = far.astype(far_ref.dtype)
    put(along_ref, core_sum(keep_ref, received_ref, rows, rows).astype(along_ref.dtype))
    put(diagonal_ref, core_sum(keep_ref, received_ref, 2 * rows, rows).astype(diagonal_ref.dtype))


def add_kernel(first, second, *outs):
    width = first.shape[1]
    total = first[...].astype(jnp.float32) + second[:, :width].astype(jnp.float32)
    for out in outs:
        put(out, total.astype(out.dtype))


def add_by_z_kernel(first, second, *outs):
    width = first.shape[1]
    halves = by_z(first[...].astype(jnp.float32) + second[:, :width].astype(jnp.float32))
    for i, out in enumerate(outs):
        put(out, halves[i // 2].astype(out.dtype))


def run_copies(pairs, sems):
    copies = [pltpu.make_async_copy(source, target, sems.at[i]) for i, (source, target) in enumerate(pairs)]
    for copy in copies:
        copy.start()
    for copy in copies:
        copy.wait()


def place_kernel(layout, *refs):
    z, y, x, c = coordinates()
    pieces, (_, out_ref, zeros, sems) = refs[: len(layout)], refs[len(layout) :]
    width = out_ref.shape[2]
    for mine in range(2):

        @pl.when(z == mine)
        def _():
            pairs = []
            for (index, other), piece in zip(layout, pieces):
                source = (mine, 1 - mine, 2 + mine, 3 - mine)[index]
                pairs.append((piece.at[:, pl.ds(0, width)], out_ref.at[source * 2 + (y ^ other)]))
            run_copies(pairs, sems)

    @pl.when(z >= 2)
    def _():
        zeros[...] = jnp.zeros_like(zeros)
        run_copies([(zeros, out_ref.at[i]) for i in range(out_ref.shape[0])], sems)


def ports_body(tokens, route_prob, counts, w_gate, w_up, w_down):
    cap, width = tokens.shape[1:]
    units = w_gate.shape[2]
    rows = LIVE // 2
    both_axes = ("expert", "batch")

    def device(z, y, x, c):
        return (z * 2 + y) * 4 + x * 2 + c

    places = [(z, y, x, c) for z in range(4) for y in range(2) for x in range(2) for c in range(2)]

    def other_core(value):
        return lax.ppermute(value, "batch", xor_pairs(4, 1))

    def across_plane(value, dx, dy):
        return lax.ppermute(value, both_axes, [(device(*p), device(p[0], p[1] ^ dy, p[2] ^ dx, p[3])) for p in places])

    def along_z(value, *moves):
        pairs = [(device(s, *p[1:]), device(t, *p[1:])) for s, t in moves for p in places if p[0] == 0]
        return lax.ppermute(value, both_axes, pairs)

    def array(rows, columns, dtype=jnp.bfloat16):
        return jax.ShapeDtypeStruct((rows, columns), dtype)

    depth = (width + PROB_COLUMNS) // 2
    rest = width - depth
    own = call(
        live_rows_kernel,
        [pltpu.VMEM((LIVE, depth), tokens.dtype), pltpu.VMEM((LIVE, depth), tokens.dtype)],
        [pltpu.with_memory_space_constraint(a, pltpu.HBM) for a in (tokens, route_prob)],
        [HBM, HBM],
        [pltpu.VMEM(route_prob.shape, route_prob.dtype), pltpu.SemaphoreType.DMA((3,))],
        name="live_rows",
    )
    across = [lax.ppermute(piece, "batch", xor_pairs(4, 2)) for piece in own]
    near = [other_core(piece) for piece in own]
    gate_w, up_w = resident(after(w_gate[0], *own), w_up[0])
    down_w, = resident(after(w_down[0], gate_w))
    across = [after(piece, down_w) for piece in across]
    pieces = [[own[0], near[0], across[0], other_core(across[0])], None]
    gate, upper = call(
        lambda *refs: first_product_kernel(depth, *refs),
        [array(4 * LIVE, units, jnp.float32)] * 2,
        [*pieces[0], gate_w, up_w],
        name="first_product",
    )
    pieces[1] = [own[1], near[1], across[1], other_core(across[1])]
    hidden = call(
        lambda *refs: hidden_kernel_of_rest(depth, rest, *refs),
        array(4 * LIVE, units),
        [counts.T, *pieces[1], gate_w, up_w, gate, upper],
        [SMEM] + [VMEM] * 8,
        scratch=[pltpu.VMEM((4 * LIVE, units), jnp.float32)] * 2,
        name="hidden",
    )

    slot = rows // 2
    keep_first, send_first, keep_rest, send_rest = call(
        ordered_down_kernel,
        [array(rows, width), array(rows, width), array(3 * rows, width), array(3 * rows, width)],
        [hidden, down_w],
        name="down",
    )
    lead_x, rest_x = call(
        first_sums_kernel,
        [array(slot, width + n) for n in (96, 192)],
        [keep_first, other_core(send_first)],
        name="first_sums",
    )
    own_lead, own_rest, own_other, across_other = call(
        other_sums_kernel,
        [array(slot, width), array(slot, width), array(rows, width + 32), array(rows, width + 0)],
        [keep_rest, other_core(after(send_rest, lead_x))],
        name="other_sums",
    )
    lead_1, next_1 = call(
        add_kernel,
        [array(slot, width + n) for n in (128, 0)],
        [own_lead, across_plane(lead_x, 1, 0)],
        name="lead_rows",
    )
    rest_1, = call(add_kernel, [array(slot, width + 0)], [own_rest, across_plane(rest_x, 1, 0)], name="rest_rows")
    from_2 = [along_z(lead_1, (2, 0), (3, 1))]
    from_3 = [along_z(rest_1, (2, 1), (3, 0))]
    next_z = [along_z(next_1, (0, 1), (1, 0))]
    from_y = across_plane(own_other, 0, 1)
    diagonal = across_plane(across_other, 1, 1)
    lead_2, next_2, rest_2, mark = call(
        add_by_z_kernel,
        [array(slot, width + n) for n in (64, 32, 0, -32)],
        [diagonal, from_y],
        name="other_rows",
    )
    from_2.append(along_z(lead_2, (2, 0), (3, 1)))
    from_3.append(along_z(rest_2, (2, 1), (3, 0)))
    next_z.append(along_z(after(next_2, next_z[0]), (0, 1), (1, 0)))
    mark = other_core(after(mark, from_2[0], from_3[0]))
    pieces = [rest_1, rest_2, *from_2, *from_3, *next_z]
    layout = [(index, other) for index in (0, 2, 3, 1) for other in (0, 1)]
    out = call(
        lambda *refs: place_kernel(layout, *refs),
        jax.ShapeDtypeStruct((cap // slot, slot, width), jnp.bfloat16),
        [*pieces, mark],
        [ANY] * (len(pieces) + 1),
        [pltpu.VMEM((slot, width), jnp.bfloat16), pltpu.SemaphoreType.DMA((len(pieces),))],
        out_specs=HBM,
        name="place",
    )
    return out.reshape(1, cap, width)


def solution(mesh):
    in_specs = (
        P("expert", "batch", None),
        P("expert", "batch"),
        P(),
        P("expert", None, "batch"),
        P("expert", None, "batch"),
        P("expert", "batch", None),
    )
    out_specs = P("expert", "batch", None)
    fits = dict(mesh.shape) == {"expert": 8, "batch": 4}
    body = ports_body if fits else general_body
    return jax.shard_map(body, mesh=mesh, in_specs=in_specs, out_specs=out_specs, check_vma=False)
```

```python
import jax
import jax.numpy as jnp
from jax import lax
from jax.experimental import pallas as pl
from jax.experimental.pallas import tpu as pltpu
from jax.sharding import PartitionSpec as P

LIVE = 32
PROB_COLUMNS = 256
PARTS = 2
VMEM_LIMIT = 16 * 2**20
VMEM = pl.BlockSpec(memory_space=pltpu.VMEM)
HBM = pl.BlockSpec(memory_space=pltpu.HBM)
ANY = pl.BlockSpec(memory_space=pl.ANY)
SMEM = pl.BlockSpec(memory_space=pltpu.SMEM)


def xor_pairs(size, offset):
    return [(i, i ^ offset) for i in range(size)]


def hidden_kernel(pieces, *refs):
    token_refs = refs[:pieces]
    gate_ref, up_ref, out_ref, gate_acc, up_acc = refs[pieces:]
    live = token_refs[0].shape[0]
    width = gate_ref.shape[0]
    step = width // 4

    def add(start, first):
        span = pl.ds(start, step)
        rows = jnp.concatenate([ref[:, span] for ref in token_refs], axis=0)
        gate = jnp.dot(rows, gate_ref[span, :], preferred_element_type=jnp.float32)
        upper = jnp.dot(rows, up_ref[span, :], preferred_element_type=jnp.float32)
        if first:
            gate_acc[...] = gate
            up_acc[...] = upper
        else:
            gate_acc[...] += gate
            up_acc[...] += upper

    add(0, True)

    @pl.loop(1, width // step)
    def _(i):
        add(pl.multiple_of(i * step, step), False)

    gate = gate_acc[...]
    out_ref[...] = (gate / (1.0 + jnp.exp(-gate)) * up_acc[...]).astype(out_ref.dtype)


def hidden_units(pieces, gate_w, up_w):
    live, width = pieces[0].shape
    units = gate_w.shape[1]
    rows = live * len(pieces)
    return pl.pallas_call(
        lambda *refs: hidden_kernel(len(pieces), *refs),
        out_shape=jax.ShapeDtypeStruct((rows, units), jnp.bfloat16),
        in_specs=[VMEM] * (len(pieces) + 2),
        out_specs=VMEM,
        scratch_shapes=[pltpu.VMEM((rows, units), jnp.float32)] * 2,
        compiler_params=pltpu.CompilerParams(vmem_limit_bytes=VMEM_LIMIT),
        cost_estimate=pl.CostEstimate(
            flops=4 * rows * width * units, bytes_accessed=4 * width * units, transcendentals=rows * units
        ),
        name="hidden_units",
    )(*pieces, gate_w, up_w)


def down_kernel(start, hidden_ref, down_ref, keep_ref, send_ref):
    width = keep_ref.shape[1]
    half = keep_ref.shape[0]
    step = width // 2

    @pl.loop(0, width // step)
    def _(i):
        span = pl.ds(pl.multiple_of(i * step, step), step)
        source = pl.ds(pl.multiple_of(start + i * step, step), step)
        terms = jnp.dot(hidden_ref[...], down_ref[:, source], preferred_element_type=jnp.float32).astype(
            keep_ref.dtype
        )
        keep_ref[:, span] = terms[:half]
        send_ref[:, span] = terms[half:]


def down_part(hidden, down_w, start, width):
    rows, units = hidden.shape
    shape = jax.ShapeDtypeStruct((rows // 2, width), jnp.bfloat16)
    return pl.pallas_call(
        lambda *refs: down_kernel(start, *refs),
        out_shape=[shape, shape],
        in_specs=[VMEM] * 2,
        out_specs=[VMEM] * 2,
        compiler_params=pltpu.CompilerParams(vmem_limit_bytes=VMEM_LIMIT),
        cost_estimate=pl.CostEstimate(
            flops=2 * rows * width * units, bytes_accessed=2 * width * units, transcendentals=0
        ),
        name="down_part",
    )(hidden, down_w)


def general_body(tokens, route_prob, counts, w_gate, w_up, w_down):
    cap, width = tokens.shape[1:]
    n_batch = lax.axis_size("batch")
    n_experts = lax.axis_size("expert")
    expert_id = lax.axis_index("expert")
    batch_id = lax.axis_index("batch")
    slot = cap // n_experts
    live_slots = LIVE // slot
    part = width // PARTS

    own = tokens[0, :LIVE]
    even = [own] + [lax.ppermute(own, "batch", xor_pairs(n_batch, d)) for d in range(2, n_batch, 2)]
    odd = [lax.ppermute(piece, "batch", xor_pairs(n_batch, 1)) for piece in even]
    hidden = hidden_units(even + odd, w_gate[0], w_up[0])

    count = counts[expert_id, batch_id]
    live = jnp.arange(LIVE, dtype=jnp.int32) < count
    scale = jnp.where(live, route_prob[0, :LIVE], 0.0)[:, None]

    columns = []
    for start in range(0, width, part):
        keep, send = down_part(hidden, w_down[0], start, part)
        received = lax.ppermute(send, "batch", xor_pairs(n_batch, 1))
        both = keep.astype(jnp.float32) + received.astype(jnp.float32)
        total = both[:LIVE]
        for i, d in enumerate(range(2, n_batch, 2), 1):
            term = both[i * LIVE : (i + 1) * LIVE].astype(jnp.bfloat16)
            total += lax.ppermute(term, "batch", xor_pairs(n_batch, d)).astype(jnp.float32)
        expert_out = jnp.where(live[:, None], scale * total, 0.0).astype(jnp.bfloat16)
        grouped = expert_out.reshape(live_slots, slot, part)

        picks = {}
        for d in sorted(range(1, n_experts), key=lambda d: (-(d // live_slots), d)):
            pairs = [(e, e ^ d) for e in range(n_experts) if e ^ d < live_slots]
            target = jnp.minimum(expert_id ^ d, live_slots - 1)
            payload = lax.dynamic_index_in_dim(grouped, target, 0, keepdims=False)
            picks[d] = lax.ppermute(payload, "expert", pairs)
        mine = lax.dynamic_index_in_dim(grouped, jnp.minimum(expert_id, live_slots - 1), 0, keepdims=False)
        picks[0] = jnp.where(expert_id < live_slots, mine, jnp.zeros_like(mine))
        stacked = jnp.stack([picks[d] for d in range(n_experts)])
        columns.append(jnp.take(stacked, jnp.arange(n_experts, dtype=jnp.int32) ^ expert_id, axis=0))
    returned = jnp.concatenate(columns, axis=-1)
    return returned.reshape(1, cap, width)


def call(kernel, outs, args, specs=None, scratch=(), out_specs=None, cost=0, aliases=None, name=None):
    return pl.pallas_call(
        kernel,
        out_shape=outs,
        in_specs=specs or [VMEM] * len(args),
        out_specs=out_specs or jax.tree.map(lambda _: VMEM, outs),
        scratch_shapes=list(scratch),
        input_output_aliases=aliases or {},
        compiler_params=pltpu.CompilerParams(vmem_limit_bytes=VMEM_LIMIT),
        cost_estimate=pl.CostEstimate(flops=0, bytes_accessed=cost, transcendentals=0),
        name=name,
    )(*args)


def live_rows_kernel(tokens_ref, prob_ref, *refs):
    *outs, prob_copy, sems = refs
    rows = outs[0].shape[0]
    copies = [pltpu.make_async_copy(prob_ref, prob_copy, sems.at[len(outs)])]
    start = 0
    for i, out in enumerate(outs):
        size = out.shape[1] - (PROB_COLUMNS if i == len(outs) - 1 else 0)
        source = tokens_ref.at[0, pl.ds(0, rows), pl.ds(start, size)]
        copies.append(pltpu.make_async_copy(source, out.at[:, pl.ds(0, size)], sems.at[i]))
        start += size
    for copy in copies:
        copy.start()
    copies[0].wait()
    slots = prob_copy.shape[1]
    row = lax.broadcasted_iota(jnp.int32, (rows, slots), 0)
    lane = lax.broadcasted_iota(jnp.int32, (rows, slots), 1)
    prob = jnp.sum(jnp.where(row == lane, prob_copy[...], 0.0), axis=1, keepdims=True)
    column = lax.broadcasted_iota(jnp.int32, (rows, PROB_COLUMNS), 1)
    terms = jnp.zeros((rows, PROB_COLUMNS), jnp.float32)
    for i in range(3):
        term = prob.astype(jnp.bfloat16).astype(jnp.float32)
        prob = prob - term
        terms = jnp.where(column == i, term, terms)
    outs[-1][:, size:] = terms.astype(outs[-1].dtype)
    for copy in copies[1:]:
        copy.wait()


def resident_kernel(*refs):
    count = len(refs) // 2
    sems = refs[-1]
    copies = [pltpu.make_async_copy(refs[i], refs[count + i], sems.at[i]) for i in range(count)]
    for copy in copies:
        copy.start()
    for copy in copies:
        copy.wait()


def resident(*arrays):
    return call(
        resident_kernel,
        [pltpu.VMEM(a.shape, a.dtype) for a in arrays],
        [pltpu.with_memory_space_constraint(a, pltpu.HBM) for a in arrays],
        [HBM] * len(arrays),
        [pltpu.SemaphoreType.DMA((len(arrays),))],
        name="resident",
    )


def after(value, *others):
    return lax.optimization_barrier((value, *others))[0]


def coordinates():
    e = lax.axis_index("expert")
    b = lax.axis_index("batch")
    return e // 2, e % 2, b // 2, b % 2


def swap(flag, first, second):
    return jnp.where(flag, second, first), jnp.where(flag, first, second)


def add_product(start, size, tokens, gate_ref, up_ref, gate_acc, up_acc, fresh):
    step = size // 256 * 128
    for i in range(2):
        span = pl.ds(i * step, size - step if i else step)
        source = pl.ds(start + i * step, span.size)
        chunk = jnp.concatenate([ref[:, span] for ref in tokens], axis=0)
        for weight, acc in ((gate_ref, gate_acc), (up_ref, up_acc)):
            product = jnp.dot(chunk, weight[source, :], preferred_element_type=jnp.float32)
            if fresh and i == 0:
                acc[...] = product
            else:
                acc[...] += product


def first_product_kernel(size, *refs):
    *tokens, gate_ref, up_ref, gate_acc, up_acc = refs
    add_product(0, size, tokens, gate_ref, up_ref, gate_acc, up_acc, True)


def hidden_kernel_of_rest(start, size, counts_ref, *refs):
    *tokens, gate_ref, up_ref, gate_in, up_in, out_ref, gate_acc, up_acc = refs
    z, y, x, c = coordinates()
    live = tokens[0].shape[0]
    gate_acc[...] = gate_in[...]
    up_acc[...] = up_in[...]
    add_product(start, size, tokens, gate_ref, up_ref, gate_acc, up_acc, False)
    row = lax.broadcasted_iota(jnp.int32, (live, 1), 0)
    kept, sent = [], []
    for i, ref in enumerate(tokens):
        span = pl.ds(i * live, live)
        gate = gate_acc[span, :]
        hidden = gate / (1.0 + jnp.exp(-gate)) * up_acc[span, :]
        prob = jnp.sum(ref[:, size : size + 128].astype(jnp.float32), axis=1, keepdims=True)
        count = counts_ref[(x * 2 + c) ^ i, z * 2 + y]
        hidden = jnp.where(row < count, hidden * prob, 0.0)
        slots = hidden.reshape(2, 2, live // 4, -1)
        same, other = swap(y == 1, slots[:, 0], slots[:, 1])
        block = jnp.concatenate([same, other]).reshape(live, -1)
        (sent if i % 2 else kept).append(block)
    out_ref[...] = jnp.concatenate(kept + sent, axis=0).astype(out_ref.dtype)


def ordered_down_kernel(hidden_ref, down_ref, *outs):
    keep_first, send_first, keep_rest, send_rest = outs
    width = down_ref.shape[1]
    rows = keep_first.shape[0]
    half = hidden_ref.shape[0] // 2
    steps = 4
    for i in range(steps):
        span = pl.ds(i * (width // steps), width // steps)
        terms = jnp.dot(hidden_ref[...], down_ref[:, span], preferred_element_type=jnp.float32).astype(
            keep_first.dtype
        )
        for base, first, rest in ((0, keep_first, keep_rest), (half, send_first, send_rest)):
            first[:, span] = terms[base + 2 * rows : base + 3 * rows]
            rest[: 2 * rows, span] = terms[base : base + 2 * rows]
            rest[2 * rows :, span] = terms[base + 3 * rows : base + 4 * rows]


def put(out, rows):
    width = min(rows.shape[1], out.shape[1])
    out[:, :width] = rows[:, :width]
    if out.shape[1] > width:
        out[:, width:] = jnp.zeros((rows.shape[0], out.shape[1] - width), out.dtype)


def core_sum(keep_ref, received_ref, start, rows):
    span = pl.ds(start, rows)
    return keep_ref[span, :].astype(jnp.float32) + received_ref[span, :].astype(jnp.float32)


def by_z(rows):
    z, y, x, c = coordinates()
    slot = rows.shape[0] // 2
    return swap((z == 0) | (z == 3), rows[:slot], rows[slot:])


def first_sums_kernel(keep_ref, received_ref, near_ref, far_ref):
    near, far = by_z(core_sum(keep_ref, received_ref, 0, keep_ref.shape[0]))
    put(near_ref, near.astype(near_ref.dtype))
    put(far_ref, far.astype(far_ref.dtype))


def other_sums_kernel(keep_ref, received_ref, near_ref, far_ref, along_ref, diagonal_ref):
    rows = along_ref.shape[0]
    near, far = by_z(core_sum(keep_ref, received_ref, 0, rows))
    near_ref[...] = near.astype(near_ref.dtype)
    far_ref[...] = far.astype(far_ref.dtype)
    put(along_ref, core_sum(keep_ref, received_ref, rows, rows).astype(along_ref.dtype))
    put(diagonal_ref, core_sum(keep_ref, received_ref, 2 * rows, rows).astype(diagonal_ref.dtype))


def add_kernel(first, second, *outs):
    width = first.shape[1]
    total = first[...].astype(jnp.float32) + second[:, :width].astype(jnp.float32)
    for out in outs:
        put(out, total.astype(out.dtype))


def add_by_z_kernel(first, second, *outs):
    width = first.shape[1]
    halves = by_z(first[...].astype(jnp.float32) + second[:, :width].astype(jnp.float32))
    for i, out in enumerate(outs):
        put(out, halves[i // 2].astype(out.dtype))


def run_copies(pairs, sems):
    copies = [pltpu.make_async_copy(source, target, sems.at[i]) for i, (source, target) in enumerate(pairs)]
    for copy in copies:
        copy.start()
    for copy in copies:
        copy.wait()


def place_kernel(layout, zeros, pieces, out_ref, sems):
    z, y, x, c = coordinates()
    width = out_ref.shape[2]
    for mine in range(2):

        @pl.when(z == mine)
        def _():
            pairs = []
            for (index, other), piece in zip(layout, pieces):
                source = (mine, 1 - mine, 2 + mine, 3 - mine)[index]
                pairs.append((piece.at[:, pl.ds(0, width)], out_ref.at[source * 2 + (y ^ other)]))
            run_copies(pairs, sems)

    if zeros is not None:

        @pl.when(z >= 2)
        def _():
            zeros[...] = jnp.zeros_like(zeros)
            run_copies([(zeros, out_ref.at[i]) for i in range(out_ref.shape[0])], sems)


def place_first_kernel(layout, *refs):
    *pieces, out_ref, zeros, sems = refs
    place_kernel(layout, zeros, pieces, out_ref, sems)


def place_rest_kernel(layout, *refs):
    *pieces, _, out_ref, sems = refs
    place_kernel(layout, None, pieces, out_ref, sems)


def ports_body(tokens, route_prob, counts, w_gate, w_up, w_down):
    cap, width = tokens.shape[1:]
    units = w_gate.shape[2]
    rows = LIVE // 2
    both_axes = ("expert", "batch")

    def device(z, y, x, c):
        return (z * 2 + y) * 4 + x * 2 + c

    places = [(z, y, x, c) for z in range(4) for y in range(2) for x in range(2) for c in range(2)]

    def other_core(value):
        return lax.ppermute(value, "batch", xor_pairs(4, 1))

    def across_plane(value, dx, dy):
        return lax.ppermute(value, both_axes, [(device(*p), device(p[0], p[1] ^ dy, p[2] ^ dx, p[3])) for p in places])

    def along_z(value, *moves):
        pairs = [(device(s, *p[1:]), device(t, *p[1:])) for s, t in moves for p in places if p[0] == 0]
        return lax.ppermute(value, both_axes, pairs)

    def array(rows, columns, dtype=jnp.bfloat16):
        return jax.ShapeDtypeStruct((rows, columns), dtype)

    depth = (width + PROB_COLUMNS) // 2
    rest = width - depth
    own = call(
        live_rows_kernel,
        [pltpu.VMEM((LIVE, depth), tokens.dtype), pltpu.VMEM((LIVE, depth), tokens.dtype)],
        [pltpu.with_memory_space_constraint(a, pltpu.HBM) for a in (tokens, route_prob)],
        [HBM, HBM],
        [pltpu.VMEM(route_prob.shape, route_prob.dtype), pltpu.SemaphoreType.DMA((3,))],
        name="live_rows",
    )
    across = [lax.ppermute(piece, "batch", xor_pairs(4, 2)) for piece in own]
    near = [other_core(piece) for piece in own]
    gate_w, up_w = resident(after(w_gate[0], *own), w_up[0])
    down_w, = resident(after(w_down[0], gate_w))
    across = [after(piece, down_w) for piece in across]
    pieces = [[own[0], near[0], across[0], other_core(across[0])], None]
    gate, upper = call(
        lambda *refs: first_product_kernel(depth, *refs),
        [array(4 * LIVE, units, jnp.float32)] * 2,
        [*pieces[0], gate_w, up_w],
        name="first_product",
    )
    pieces[1] = [own[1], near[1], across[1], other_core(across[1])]
    hidden = call(
        lambda *refs: hidden_kernel_of_rest(depth, rest, *refs),
        array(4 * LIVE, units),
        [counts.T, *pieces[1], gate_w, up_w, gate, upper],
        [SMEM] + [VMEM] * 8,
        scratch=[pltpu.VMEM((4 * LIVE, units), jnp.float32)] * 2,
        name="hidden",
    )

    slot = rows // 2
    keep_first, send_first, keep_rest, send_rest = call(
        ordered_down_kernel,
        [array(rows, width), array(rows, width), array(3 * rows, width), array(3 * rows, width)],
        [hidden, down_w],
        name="down",
    )
    lead_x, rest_x = call(
        first_sums_kernel,
        [array(slot, width + n) for n in (96, 192)],
        [keep_first, other_core(send_first)],
        name="first_sums",
    )
    own_lead, own_rest, own_other, across_other = call(
        other_sums_kernel,
        [array(slot, width), array(slot, width), array(rows, width + 32), array(rows, width + 0)],
        [keep_rest, other_core(after(send_rest, lead_x))],
        name="other_sums",
    )
    lead_1, next_1 = call(
        add_kernel,
        [array(slot, width + n) for n in (128, 0)],
        [own_lead, across_plane(lead_x, 1, 0)],
        name="lead_rows",
    )
    rest_1, = call(add_kernel, [array(slot, width + 0)], [own_rest, across_plane(rest_x, 1, 0)], name="rest_rows")
    from_2 = [along_z(lead_1, (2, 0), (3, 1))]
    from_3 = [along_z(rest_1, (2, 1), (3, 0))]
    next_z = [along_z(next_1, (0, 1), (1, 0))]
    from_y = across_plane(own_other, 0, 1)
    diagonal = across_plane(across_other, 1, 1)
    lead_2, next_2, rest_2, mark = call(
        add_by_z_kernel,
        [array(slot, width + n) for n in (64, 32, 0, -32)],
        [diagonal, from_y],
        name="other_rows",
    )
    from_2.append(along_z(lead_2, (2, 0), (3, 1)))
    from_3.append(along_z(rest_2, (2, 1), (3, 0)))
    next_z.append(along_z(after(next_2, next_z[0]), (0, 1), (1, 0)))
    mark = other_core(after(mark, from_2[0], from_3[0]))
    out = jax.ShapeDtypeStruct((cap // slot, slot, width), jnp.bfloat16)
    pieces = [rest_1, rest_2, from_2[0], from_3[0], next_z[0]]
    out = call(
        lambda *refs: place_first_kernel([(0, 0), (0, 1), (2, 0), (3, 0), (1, 0)], *refs),
        out,
        pieces,
        [ANY] * len(pieces),
        [pltpu.VMEM((slot, width), jnp.bfloat16), pltpu.SemaphoreType.DMA((cap // slot,))],
        out_specs=HBM,
        name="place_first",
    )
    pieces = [from_2[1], from_3[1], next_z[1], mark]
    out = call(
        lambda *refs: place_rest_kernel([(2, 1), (3, 1), (1, 1)], *refs),
        jax.ShapeDtypeStruct(out.shape, out.dtype),
        [*pieces, out],
        [ANY] * len(pieces) + [HBM],
        [pltpu.SemaphoreType.DMA((3,))],
        out_specs=HBM,
        aliases={len(pieces): 0},
        name="place_rest",
    )
    return out.reshape(1, cap, width)


def solution(mesh):
    in_specs = (
        P("expert", "batch", None),
        P("expert", "batch"),
        P(),
        P("expert", None, "batch"),
        P("expert", None, "batch"),
        P("expert", "batch", None),
    )
    out_specs = P("expert", "batch", None)
    fits = dict(mesh.shape) == {"expert": 8, "batch": 4}
    body = ports_body if fits else general_body
    return jax.shard_map(body, mesh=mesh, in_specs=in_specs, out_specs=out_specs, check_vma=False)
```

```python
import jax
import jax.numpy as jnp
from jax import lax
from jax.experimental import pallas as pl
from jax.experimental.pallas import tpu as pltpu
from jax.sharding import PartitionSpec as P

LIVE = 32
PROB_COLUMNS = 256
PARTS = 2
VMEM_LIMIT = 16 * 2**20
VMEM = pl.BlockSpec(memory_space=pltpu.VMEM)
HBM = pl.BlockSpec(memory_space=pltpu.HBM)
ANY = pl.BlockSpec(memory_space=pl.ANY)
SMEM = pl.BlockSpec(memory_space=pltpu.SMEM)


def xor_pairs(size, offset):
    return [(i, i ^ offset) for i in range(size)]


def hidden_kernel(pieces, *refs):
    token_refs = refs[:pieces]
    gate_ref, up_ref, out_ref, gate_acc, up_acc = refs[pieces:]
    live = token_refs[0].shape[0]
    width = gate_ref.shape[0]
    step = width // 4

    def add(start, first):
        span = pl.ds(start, step)
        rows = jnp.concatenate([ref[:, span] for ref in token_refs], axis=0)
        gate = jnp.dot(rows, gate_ref[span, :], preferred_element_type=jnp.float32)
        upper = jnp.dot(rows, up_ref[span, :], preferred_element_type=jnp.float32)
        if first:
            gate_acc[...] = gate
            up_acc[...] = upper
        else:
            gate_acc[...] += gate
            up_acc[...] += upper

    add(0, True)

    @pl.loop(1, width // step)
    def _(i):
        add(pl.multiple_of(i * step, step), False)

    gate = gate_acc[...]
    out_ref[...] = (gate / (1.0 + jnp.exp(-gate)) * up_acc[...]).astype(out_ref.dtype)


def hidden_units(pieces, gate_w, up_w):
    live, width = pieces[0].shape
    units = gate_w.shape[1]
    rows = live * len(pieces)
    return pl.pallas_call(
        lambda *refs: hidden_kernel(len(pieces), *refs),
        out_shape=jax.ShapeDtypeStruct((rows, units), jnp.bfloat16),
        in_specs=[VMEM] * (len(pieces) + 2),
        out_specs=VMEM,
        scratch_shapes=[pltpu.VMEM((rows, units), jnp.float32)] * 2,
        compiler_params=pltpu.CompilerParams(vmem_limit_bytes=VMEM_LIMIT),
        cost_estimate=pl.CostEstimate(
            flops=4 * rows * width * units, bytes_accessed=4 * width * units, transcendentals=rows * units
        ),
        name="hidden_units",
    )(*pieces, gate_w, up_w)


def down_kernel(start, hidden_ref, down_ref, keep_ref, send_ref):
    width = keep_ref.shape[1]
    half = keep_ref.shape[0]
    step = width // 2

    @pl.loop(0, width // step)
    def _(i):
        span = pl.ds(pl.multiple_of(i * step, step), step)
        source = pl.ds(pl.multiple_of(start + i * step, step), step)
        terms = jnp.dot(hidden_ref[...], down_ref[:, source], preferred_element_type=jnp.float32).astype(
            keep_ref.dtype
        )
        keep_ref[:, span] = terms[:half]
        send_ref[:, span] = terms[half:]


def down_part(hidden, down_w, start, width):
    rows, units = hidden.shape
    shape = jax.ShapeDtypeStruct((rows // 2, width), jnp.bfloat16)
    return pl.pallas_call(
        lambda *refs: down_kernel(start, *refs),
        out_shape=[shape, shape],
        in_specs=[VMEM] * 2,
        out_specs=[VMEM] * 2,
        compiler_params=pltpu.CompilerParams(vmem_limit_bytes=VMEM_LIMIT),
        cost_estimate=pl.CostEstimate(
            flops=2 * rows * width * units, bytes_accessed=2 * width * units, transcendentals=0
        ),
        name="down_part",
    )(hidden, down_w)


def general_body(tokens, route_prob, counts, w_gate, w_up, w_down):
    cap, width = tokens.shape[1:]
    n_batch = lax.axis_size("batch")
    n_experts = lax.axis_size("expert")
    expert_id = lax.axis_index("expert")
    batch_id = lax.axis_index("batch")
    slot = cap // n_experts
    live_slots = LIVE // slot
    part = width // PARTS

    own = tokens[0, :LIVE]
    even = [own] + [lax.ppermute(own, "batch", xor_pairs(n_batch, d)) for d in range(2, n_batch, 2)]
    odd = [lax.ppermute(piece, "batch", xor_pairs(n_batch, 1)) for piece in even]
    hidden = hidden_units(even + odd, w_gate[0], w_up[0])

    count = counts[expert_id, batch_id]
    live = jnp.arange(LIVE, dtype=jnp.int32) < count
    scale = jnp.where(live, route_prob[0, :LIVE], 0.0)[:, None]

    columns = []
    for start in range(0, width, part):
        keep, send = down_part(hidden, w_down[0], start, part)
        received = lax.ppermute(send, "batch", xor_pairs(n_batch, 1))
        both = keep.astype(jnp.float32) + received.astype(jnp.float32)
        total = both[:LIVE]
        for i, d in enumerate(range(2, n_batch, 2), 1):
            term = both[i * LIVE : (i + 1) * LIVE].astype(jnp.bfloat16)
            total += lax.ppermute(term, "batch", xor_pairs(n_batch, d)).astype(jnp.float32)
        expert_out = jnp.where(live[:, None], scale * total, 0.0).astype(jnp.bfloat16)
        grouped = expert_out.reshape(live_slots, slot, part)

        picks = {}
        for d in sorted(range(1, n_experts), key=lambda d: (-(d // live_slots), d)):
            pairs = [(e, e ^ d) for e in range(n_experts) if e ^ d < live_slots]
            target = jnp.minimum(expert_id ^ d, live_slots - 1)
            payload = lax.dynamic_index_in_dim(grouped, target, 0, keepdims=False)
            picks[d] = lax.ppermute(payload, "expert", pairs)
        mine = lax.dynamic_index_in_dim(grouped, jnp.minimum(expert_id, live_slots - 1), 0, keepdims=False)
        picks[0] = jnp.where(expert_id < live_slots, mine, jnp.zeros_like(mine))
        stacked = jnp.stack([picks[d] for d in range(n_experts)])
        columns.append(jnp.take(stacked, jnp.arange(n_experts, dtype=jnp.int32) ^ expert_id, axis=0))
    returned = jnp.concatenate(columns, axis=-1)
    return returned.reshape(1, cap, width)


def call(kernel, outs, args, specs=None, scratch=(), out_specs=None, cost=0, aliases=None, name=None):
    return pl.pallas_call(
        kernel,
        out_shape=outs,
        in_specs=specs or [VMEM] * len(args),
        out_specs=out_specs or jax.tree.map(lambda _: VMEM, outs),
        scratch_shapes=list(scratch),
        input_output_aliases=aliases or {},
        compiler_params=pltpu.CompilerParams(vmem_limit_bytes=VMEM_LIMIT),
        cost_estimate=pl.CostEstimate(flops=0, bytes_accessed=cost, transcendentals=0),
        name=name,
    )(*args)


def live_rows_kernel(tokens_ref, out_ref, sem):
    rows, size = out_ref.shape
    copy = pltpu.make_async_copy(tokens_ref.at[0, pl.ds(0, rows), pl.ds(0, size)], out_ref, sem)
    copy.start()
    copy.wait()


def live_rows_and_prob_kernel(start, tokens_ref, prob_ref, counts_ref, *refs):
    *outs, prob_copy, counts_copy, sems = refs
    z, y, x, c = coordinates()
    rows = outs[0].shape[0]
    copies = [
        pltpu.make_async_copy(prob_ref, prob_copy, sems.at[len(outs)]),
        pltpu.make_async_copy(counts_ref, counts_copy, sems.at[len(outs) + 1]),
    ]
    for i, out in enumerate(outs):
        size = out.shape[1] - (PROB_COLUMNS if i == len(outs) - 1 else 0)
        source = tokens_ref.at[0, pl.ds(0, rows), pl.ds(start, size)]
        copies.append(pltpu.make_async_copy(source, out.at[:, pl.ds(0, size)], sems.at[i]))
        start += size
    for copy in copies:
        copy.start()
    for copy in copies[:2]:
        copy.wait()
    block = lax.broadcasted_iota(jnp.int32, counts_copy.shape, 0) == x * 2 + c
    expert = lax.broadcasted_iota(jnp.int32, counts_copy.shape, 1) == z * 2 + y
    count = jnp.sum(jnp.where(block & expert, counts_copy[...], 0), axis=1, keepdims=True)
    count = jnp.sum(count, axis=0, keepdims=True)
    slots = prob_copy.shape[1]
    row = lax.broadcasted_iota(jnp.int32, (rows, slots), 0)
    lane = lax.broadcasted_iota(jnp.int32, (rows, slots), 1)
    prob = jnp.sum(jnp.where((row == lane) & (row < count), prob_copy[...], 0.0), axis=1, keepdims=True)
    column = lax.broadcasted_iota(jnp.int32, (rows, PROB_COLUMNS), 1)
    terms = jnp.zeros((rows, PROB_COLUMNS), jnp.float32)
    for i in range(3):
        term = prob.astype(jnp.bfloat16).astype(jnp.float32)
        prob = prob - term
        terms = jnp.where(column == i, term, terms)
    outs[-1][:, size:] = terms.astype(outs[-1].dtype)
    for copy in copies[2:]:
        copy.wait()


def resident_kernel(*refs):
    count = len(refs) // 2
    sems = refs[-1]
    copies = [pltpu.make_async_copy(refs[i], refs[count + i], sems.at[i]) for i in range(count)]
    for copy in copies:
        copy.start()
    for copy in copies:
        copy.wait()


def resident(*arrays):
    return call(
        resident_kernel,
        [pltpu.VMEM(a.shape, a.dtype) for a in arrays],
        [pltpu.with_memory_space_constraint(a, pltpu.HBM) for a in arrays],
        [HBM] * len(arrays),
        [pltpu.SemaphoreType.DMA((len(arrays),))],
        name="resident",
    )


def after(value, *others):
    return lax.optimization_barrier((value, *others))[0]


def coordinates():
    e = lax.axis_index("expert")
    b = lax.axis_index("batch")
    return e // 2, e % 2, b // 2, b % 2


def swap(flag, first, second):
    return jnp.where(flag, second, first), jnp.where(flag, first, second)


def add_product(start, size, tokens, gate_ref, up_ref, gate_acc, up_acc, fresh):
    step = size // 256 * 128
    for i in range(2):
        span = pl.ds(i * step, size - step if i else step)
        source = pl.ds(start + i * step, span.size)
        chunk = jnp.concatenate([ref[:, span] for ref in tokens], axis=0)
        for weight, acc in ((gate_ref, gate_acc), (up_ref, up_acc)):
            product = jnp.dot(chunk, weight[source, :], preferred_element_type=jnp.float32)
            if fresh and i == 0:
                acc[...] = product
            else:
                acc[...] += product


def first_product_kernel(size, *refs):
    *tokens, gate_ref, up_ref, gate_acc, up_acc = refs
    add_product(0, size, tokens, gate_ref, up_ref, gate_acc, up_acc, True)


def hidden_kernel_of_rest(start, size, *refs):
    *tokens, gate_ref, up_ref, gate_in, up_in, out_ref, gate_acc, up_acc = refs
    z, y, x, c = coordinates()
    live = tokens[0].shape[0]
    gate_acc[...] = gate_in[...]
    up_acc[...] = up_in[...]
    add_product(start, size, tokens, gate_ref, up_ref, gate_acc, up_acc, False)
    kept, sent = [], []
    for i, ref in enumerate(tokens):
        span = pl.ds(i * live, live)
        gate = gate_acc[span, :]
        hidden = gate / (1.0 + jnp.exp(-gate)) * up_acc[span, :]
        prob = jnp.sum(ref[:, size : size + 128].astype(jnp.float32), axis=1, keepdims=True)
        hidden = hidden * prob
        slots = hidden.reshape(2, 2, live // 4, -1)
        same, other = swap(y == 1, slots[:, 0], slots[:, 1])
        block = jnp.concatenate([same, other]).reshape(live, -1)
        (sent if i % 2 else kept).append(block)
    out_ref[...] = jnp.concatenate(kept + sent, axis=0).astype(out_ref.dtype)


def ordered_down_kernel(hidden_ref, down_ref, *outs):
    keep_first, send_first, keep_rest, send_rest = outs
    width = down_ref.shape[1]
    rows = keep_first.shape[0]
    half = hidden_ref.shape[0] // 2
    steps = 4
    for i in range(steps):
        span = pl.ds(i * (width // steps), width // steps)
        terms = jnp.dot(hidden_ref[...], down_ref[:, span], preferred_element_type=jnp.float32).astype(
            keep_first.dtype
        )
        for base, first, rest in ((0, keep_first, keep_rest), (half, send_first, send_rest)):
            first[:, span] = terms[base + 2 * rows : base + 3 * rows]
            rest[: 2 * rows, span] = terms[base : base + 2 * rows]
            rest[2 * rows :, span] = terms[base + 3 * rows : base + 4 * rows]


def put(out, rows):
    width = min(rows.shape[1], out.shape[1])
    out[:, :width] = rows[:, :width]
    if out.shape[1] > width:
        out[:, width:] = jnp.zeros((rows.shape[0], out.shape[1] - width), out.dtype)


def core_sum(keep_ref, received_ref, start, rows):
    span = pl.ds(start, rows)
    return keep_ref[span, :].astype(jnp.float32) + received_ref[span, :].astype(jnp.float32)


def by_z(rows):
    z, y, x, c = coordinates()
    slot = rows.shape[0] // 2
    return swap((z == 0) | (z == 3), rows[:slot], rows[slot:])


def first_sums_kernel(keep_ref, received_ref, near_ref, far_ref):
    near, far = by_z(core_sum(keep_ref, received_ref, 0, keep_ref.shape[0]))
    put(near_ref, near.astype(near_ref.dtype))
    put(far_ref, far.astype(far_ref.dtype))


def other_sums_kernel(keep_ref, received_ref, near_ref, far_ref, along_ref, diagonal_ref):
    rows = along_ref.shape[0]
    near, far = by_z(core_sum(keep_ref, received_ref, 0, rows))
    near_ref[...] = near.astype(near_ref.dtype)
    far_ref[...] = far.astype(far_ref.dtype)
    put(along_ref, core_sum(keep_ref, received_ref, rows, rows).astype(along_ref.dtype))
    put(diagonal_ref, core_sum(keep_ref, received_ref, 2 * rows, rows).astype(diagonal_ref.dtype))


def add_kernel(first, second, *outs):
    width = first.shape[1]
    total = first[...].astype(jnp.float32) + second[:, :width].astype(jnp.float32)
    for out in outs:
        put(out, total.astype(out.dtype))


def add_by_z_kernel(first, second, *outs):
    width = first.shape[1]
    halves = by_z(first[...].astype(jnp.float32) + second[:, :width].astype(jnp.float32))
    for i, out in enumerate(outs):
        put(out, halves[i // 2].astype(out.dtype))


def run_copies(pairs, sems):
    copies = [pltpu.make_async_copy(source, target, sems.at[i]) for i, (source, target) in enumerate(pairs)]
    for copy in copies:
        copy.start()
    for copy in copies:
        copy.wait()


def place_kernel(layout, zeros, pieces, out_ref, sems):
    z, y, x, c = coordinates()
    width = out_ref.shape[2]
    for mine in range(2):

        @pl.when(z == mine)
        def _():
            pairs = []
            for (index, other), piece in zip(layout, pieces):
                source = (mine, 1 - mine, 2 + mine, 3 - mine)[index]
                pairs.append((piece.at[:, pl.ds(0, width)], out_ref.at[source * 2 + (y ^ other)]))
            run_copies(pairs, sems)

    if zeros is not None:

        @pl.when(z >= 2)
        def _():
            zeros[...] = jnp.zeros_like(zeros)
            run_copies([(zeros, out_ref.at[i]) for i in range(out_ref.shape[0])], sems)


def place_first_kernel(layout, *refs):
    *pieces, out_ref, zeros, sems = refs
    place_kernel(layout, zeros, pieces, out_ref, sems)


def place_rest_kernel(layout, *refs):
    *pieces, _, out_ref, sems = refs
    place_kernel(layout, None, pieces, out_ref, sems)


def ports_body(tokens, route_prob, counts, w_gate, w_up, w_down):
    cap, width = tokens.shape[1:]
    units = w_gate.shape[2]
    rows = LIVE // 2
    both_axes = ("expert", "batch")

    def device(z, y, x, c):
        return (z * 2 + y) * 4 + x * 2 + c

    places = [(z, y, x, c) for z in range(4) for y in range(2) for x in range(2) for c in range(2)]

    def other_core(value):
        return lax.ppermute(value, "batch", xor_pairs(4, 1))

    def across_plane(value, dx, dy):
        return lax.ppermute(value, both_axes, [(device(*p), device(p[0], p[1] ^ dy, p[2] ^ dx, p[3])) for p in places])

    def along_z(value, *moves):
        pairs = [(device(s, *p[1:]), device(t, *p[1:])) for s, t in moves for p in places if p[0] == 0]
        return lax.ppermute(value, both_axes, pairs)

    def array(rows, columns, dtype=jnp.bfloat16):
        return jax.ShapeDtypeStruct((rows, columns), dtype)

    depth = (width + PROB_COLUMNS) // 2
    rest = width - depth
    in_hbm = [pltpu.with_memory_space_constraint(a, pltpu.HBM) for a in (tokens, route_prob, counts.T)]
    piece = pltpu.VMEM((LIVE, depth), tokens.dtype)
    own = [
        call(live_rows_kernel, piece, in_hbm[:1], [HBM], [pltpu.SemaphoreType.DMA], name="live_rows"),
        call(
            lambda *refs: live_rows_and_prob_kernel(depth, *refs),
            [piece],
            in_hbm,
            [HBM, HBM, HBM],
            [
                pltpu.VMEM(route_prob.shape, route_prob.dtype),
                pltpu.VMEM(counts.T.shape, counts.dtype),
                pltpu.SemaphoreType.DMA((3,)),
            ],
            name="live_rows_and_prob",
        )[0],
    ]
    across = [lax.ppermute(piece, "batch", xor_pairs(4, 2)) for piece in own]
    near = [other_core(piece) for piece in own]
    gate_w, up_w, down_w = resident(after(w_gate[0], *own), w_up[0], w_down[0])
    across = [after(piece, down_w) for piece in across]
    pieces = [[own[0], near[0], across[0], other_core(across[0])], None]
    gate, upper = call(
        lambda *refs: first_product_kernel(depth, *refs),
        [array(4 * LIVE, units, jnp.float32)] * 2,
        [*pieces[0], gate_w, up_w],
        name="first_product",
    )
    pieces[1] = [own[1], near[1], across[1], other_core(across[1])]
    hidden = call(
        lambda *refs: hidden_kernel_of_rest(depth, rest, *refs),
        array(4 * LIVE, units),
        [*pieces[1], gate_w, up_w, gate, upper],
        scratch=[pltpu.VMEM((4 * LIVE, units), jnp.float32)] * 2,
        name="hidden",
    )

    slot = rows // 2
    keep_first, send_first, keep_rest, send_rest = call(
        ordered_down_kernel,
        [array(rows, width), array(rows, width), array(3 * rows, width), array(3 * rows, width)],
        [hidden, down_w],
        name="down",
    )
    lead_x, rest_x = call(
        first_sums_kernel,
        [array(slot, width + n) for n in (96, 192)],
        [keep_first, other_core(send_first)],
        name="first_sums",
    )
    own_lead, own_rest, own_other, across_other = call(
        other_sums_kernel,
        [array(slot, width), array(slot, width), array(rows, width + 32), array(rows, width + 0)],
        [keep_rest, other_core(after(send_rest, lead_x))],
        name="other_sums",
    )
    lead_1, next_1 = call(
        add_kernel,
        [array(slot, width + n) for n in (128, 0)],
        [own_lead, across_plane(lead_x, 1, 0)],
        name="lead_rows",
    )
    rest_1, = call(add_kernel, [array(slot, width + 0)], [own_rest, across_plane(rest_x, 1, 0)], name="rest_rows")
    from_2 = [along_z(lead_1, (2, 0), (3, 1))]
    from_3 = [along_z(rest_1, (2, 1), (3, 0))]
    next_z = [along_z(next_1, (0, 1), (1, 0))]
    from_y = across_plane(own_other, 0, 1)
    diagonal = across_plane(across_other, 1, 1)
    lead_2, next_2, rest_2, mark = call(
        add_by_z_kernel,
        [array(slot, width + n) for n in (64, 32, 0, -32)],
        [diagonal, from_y],
        name="other_rows",
    )
    from_2.append(along_z(lead_2, (2, 0), (3, 1)))
    from_3.append(along_z(rest_2, (2, 1), (3, 0)))
    next_z.append(along_z(after(next_2, next_z[0]), (0, 1), (1, 0)))
    mark = other_core(after(mark, from_2[0], from_3[0]))
    out = jax.ShapeDtypeStruct((cap // slot, slot, width), jnp.bfloat16)
    pieces = [rest_1, rest_2, from_2[0], from_3[0], next_z[0]]
    out = call(
        lambda *refs: place_first_kernel([(0, 0), (0, 1), (2, 0), (3, 0), (1, 0)], *refs),
        out,
        pieces,
        [ANY] * len(pieces),
        [pltpu.VMEM((slot, width), jnp.bfloat16), pltpu.SemaphoreType.DMA((cap // slot,))],
        out_specs=HBM,
        name="place_first",
    )
    pieces = [from_2[1], from_3[1], next_z[1], mark]
    out = call(
        lambda *refs: place_rest_kernel([(2, 1), (3, 1), (1, 1)], *refs),
        jax.ShapeDtypeStruct(out.shape, out.dtype),
        [*pieces, out],
        [ANY] * len(pieces) + [HBM],
        [pltpu.SemaphoreType.DMA((3,))],
        out_specs=HBM,
        aliases={len(pieces): 0},
        name="place_rest",
    )
    return out.reshape(1, cap, width)


def solution(mesh):
    in_specs = (
        P("expert", "batch", None),
        P("expert", "batch"),
        P(),
        P("expert", None, "batch"),
        P("expert", None, "batch"),
        P("expert", "batch", None),
    )
    out_specs = P("expert", "batch", None)
    fits = dict(mesh.shape) == {"expert": 8, "batch": 4}
    body = ports_body if fits else general_body
    return jax.shard_map(body, mesh=mesh, in_specs=in_specs, out_specs=out_specs, check_vma=False)
```

```python
import jax
import jax.numpy as jnp
from jax import lax
from jax.experimental import pallas as pl
from jax.experimental.pallas import tpu as pltpu
from jax.sharding import PartitionSpec as P

LIVE = 32
PROB_COLUMNS = 256
PARTS = 2
VMEM_LIMIT = 16 * 2**20
VMEM = pl.BlockSpec(memory_space=pltpu.VMEM)
HBM = pl.BlockSpec(memory_space=pltpu.HBM)
ANY = pl.BlockSpec(memory_space=pl.ANY)
SMEM = pl.BlockSpec(memory_space=pltpu.SMEM)


def xor_pairs(size, offset):
    return [(i, i ^ offset) for i in range(size)]


def hidden_kernel(pieces, *refs):
    token_refs = refs[:pieces]
    gate_ref, up_ref, out_ref, gate_acc, up_acc = refs[pieces:]
    live = token_refs[0].shape[0]
    width = gate_ref.shape[0]
    step = width // 4

    def add(start, first):
        span = pl.ds(start, step)
        rows = jnp.concatenate([ref[:, span] for ref in token_refs], axis=0)
        gate = jnp.dot(rows, gate_ref[span, :], preferred_element_type=jnp.float32)
        upper = jnp.dot(rows, up_ref[span, :], preferred_element_type=jnp.float32)
        if first:
            gate_acc[...] = gate
            up_acc[...] = upper
        else:
            gate_acc[...] += gate
            up_acc[...] += upper

    add(0, True)

    @pl.loop(1, width // step)
    def _(i):
        add(pl.multiple_of(i * step, step), False)

    gate = gate_acc[...]
    out_ref[...] = (gate / (1.0 + jnp.exp(-gate)) * up_acc[...]).astype(out_ref.dtype)


def hidden_units(pieces, gate_w, up_w):
    live, width = pieces[0].shape
    units = gate_w.shape[1]
    rows = live * len(pieces)
    return pl.pallas_call(
        lambda *refs: hidden_kernel(len(pieces), *refs),
        out_shape=jax.ShapeDtypeStruct((rows, units), jnp.bfloat16),
        in_specs=[VMEM] * (len(pieces) + 2),
        out_specs=VMEM,
        scratch_shapes=[pltpu.VMEM((rows, units), jnp.float32)] * 2,
        compiler_params=pltpu.CompilerParams(vmem_limit_bytes=VMEM_LIMIT),
        cost_estimate=pl.CostEstimate(
            flops=4 * rows * width * units, bytes_accessed=4 * width * units, transcendentals=rows * units
        ),
        name="hidden_units",
    )(*pieces, gate_w, up_w)


def down_kernel(start, hidden_ref, down_ref, keep_ref, send_ref):
    width = keep_ref.shape[1]
    half = keep_ref.shape[0]
    step = width // 2

    @pl.loop(0, width // step)
    def _(i):
        span = pl.ds(pl.multiple_of(i * step, step), step)
        source = pl.ds(pl.multiple_of(start + i * step, step), step)
        terms = jnp.dot(hidden_ref[...], down_ref[:, source], preferred_element_type=jnp.float32).astype(
            keep_ref.dtype
        )
        keep_ref[:, span] = terms[:half]
        send_ref[:, span] = terms[half:]


def down_part(hidden, down_w, start, width):
    rows, units = hidden.shape
    shape = jax.ShapeDtypeStruct((rows // 2, width), jnp.bfloat16)
    return pl.pallas_call(
        lambda *refs: down_kernel(start, *refs),
        out_shape=[shape, shape],
        in_specs=[VMEM] * 2,
        out_specs=[VMEM] * 2,
        compiler_params=pltpu.CompilerParams(vmem_limit_bytes=VMEM_LIMIT),
        cost_estimate=pl.CostEstimate(
            flops=2 * rows * width * units, bytes_accessed=2 * width * units, transcendentals=0
        ),
        name="down_part",
    )(hidden, down_w)


def general_body(tokens, route_prob, counts, w_gate, w_up, w_down):
    cap, width = tokens.shape[1:]
    n_batch = lax.axis_size("batch")
    n_experts = lax.axis_size("expert")
    expert_id = lax.axis_index("expert")
    batch_id = lax.axis_index("batch")
    slot = cap // n_experts
    live_slots = LIVE // slot
    part = width // PARTS

    own = tokens[0, :LIVE]
    even = [own] + [lax.ppermute(own, "batch", xor_pairs(n_batch, d)) for d in range(2, n_batch, 2)]
    odd = [lax.ppermute(piece, "batch", xor_pairs(n_batch, 1)) for piece in even]
    hidden = hidden_units(even + odd, w_gate[0], w_up[0])

    count = counts[expert_id, batch_id]
    live = jnp.arange(LIVE, dtype=jnp.int32) < count
    scale = jnp.where(live, route_prob[0, :LIVE], 0.0)[:, None]

    columns = []
    for start in range(0, width, part):
        keep, send = down_part(hidden, w_down[0], start, part)
        received = lax.ppermute(send, "batch", xor_pairs(n_batch, 1))
        both = keep.astype(jnp.float32) + received.astype(jnp.float32)
        total = both[:LIVE]
        for i, d in enumerate(range(2, n_batch, 2), 1):
            term = both[i * LIVE : (i + 1) * LIVE].astype(jnp.bfloat16)
            total += lax.ppermute(term, "batch", xor_pairs(n_batch, d)).astype(jnp.float32)
        expert_out = jnp.where(live[:, None], scale * total, 0.0).astype(jnp.bfloat16)
        grouped = expert_out.reshape(live_slots, slot, part)

        picks = {}
        for d in sorted(range(1, n_experts), key=lambda d: (-(d // live_slots), d)):
            pairs = [(e, e ^ d) for e in range(n_experts) if e ^ d < live_slots]
            target = jnp.minimum(expert_id ^ d, live_slots - 1)
            payload = lax.dynamic_index_in_dim(grouped, target, 0, keepdims=False)
            picks[d] = lax.ppermute(payload, "expert", pairs)
        mine = lax.dynamic_index_in_dim(grouped, jnp.minimum(expert_id, live_slots - 1), 0, keepdims=False)
        picks[0] = jnp.where(expert_id < live_slots, mine, jnp.zeros_like(mine))
        stacked = jnp.stack([picks[d] for d in range(n_experts)])
        columns.append(jnp.take(stacked, jnp.arange(n_experts, dtype=jnp.int32) ^ expert_id, axis=0))
    returned = jnp.concatenate(columns, axis=-1)
    return returned.reshape(1, cap, width)


def call(kernel, outs, args, specs=None, scratch=(), out_specs=None, aliases=None, name=None):
    return pl.pallas_call(
        kernel,
        out_shape=outs,
        in_specs=specs or [VMEM] * len(args),
        out_specs=out_specs or jax.tree.map(lambda _: VMEM, outs),
        scratch_shapes=list(scratch),
        input_output_aliases=aliases or {},
        compiler_params=pltpu.CompilerParams(vmem_limit_bytes=VMEM_LIMIT),
        cost_estimate=pl.CostEstimate(flops=0, bytes_accessed=0, transcendentals=0),
        name=name,
    )(*args)


def live_rows_kernel(tokens_ref, out_ref, sem):
    rows, size = out_ref.shape
    copy = pltpu.make_async_copy(tokens_ref.at[0, pl.ds(0, rows), pl.ds(0, size)], out_ref, sem)
    copy.start()
    copy.wait()


def live_rows_and_prob_kernel(start, tokens_ref, prob_ref, counts_ref, *refs):
    *outs, prob_copy, counts_copy, sems = refs
    z, y, x, c = coordinates()
    rows = outs[0].shape[0]
    copies = [
        pltpu.make_async_copy(prob_ref, prob_copy, sems.at[len(outs)]),
        pltpu.make_async_copy(counts_ref, counts_copy, sems.at[len(outs) + 1]),
    ]
    for i, out in enumerate(outs):
        size = out.shape[1] - (PROB_COLUMNS if i == len(outs) - 1 else 0)
        source = tokens_ref.at[0, pl.ds(0, rows), pl.ds(start, size)]
        copies.append(pltpu.make_async_copy(source, out.at[:, pl.ds(0, size)], sems.at[i]))
        start += size
    for copy in copies:
        copy.start()
    for copy in copies[:2]:
        copy.wait()
    block = lax.broadcasted_iota(jnp.int32, counts_copy.shape, 0) == x * 2 + c
    expert = lax.broadcasted_iota(jnp.int32, counts_copy.shape, 1) == z * 2 + y
    count = jnp.sum(jnp.where(block & expert, counts_copy[...], 0), axis=1, keepdims=True)
    count = jnp.sum(count, axis=0, keepdims=True)
    slots = prob_copy.shape[1]
    row = lax.broadcasted_iota(jnp.int32, (rows, slots), 0)
    lane = lax.broadcasted_iota(jnp.int32, (rows, slots), 1)
    prob = jnp.sum(jnp.where((row == lane) & (row < count), prob_copy[...], 0.0), axis=1, keepdims=True)
    column = lax.broadcasted_iota(jnp.int32, (rows, PROB_COLUMNS), 1)
    terms = jnp.zeros((rows, PROB_COLUMNS), jnp.float32)
    for i in range(3):
        term = prob.astype(jnp.bfloat16).astype(jnp.float32)
        prob = prob - term
        terms = jnp.where(column == i, term, terms)
    outs[-1][:, size:] = terms.astype(outs[-1].dtype)
    for copy in copies[2:]:
        copy.wait()


def resident_kernel(*refs):
    count = len(refs) // 2
    sems = refs[-1]
    copies = [pltpu.make_async_copy(refs[i], refs[count + i], sems.at[i]) for i in range(count)]
    for copy in copies:
        copy.start()
    for copy in copies:
        copy.wait()


def resident(*arrays):
    return call(
        resident_kernel,
        [pltpu.VMEM(a.shape, a.dtype) for a in arrays],
        [pltpu.with_memory_space_constraint(a, pltpu.HBM) for a in arrays],
        [HBM] * len(arrays),
        [pltpu.SemaphoreType.DMA((len(arrays),))],
        name="resident",
    )


def after(value, *others):
    return lax.optimization_barrier((value, *others))[0]


def coordinates():
    e = lax.axis_index("expert")
    b = lax.axis_index("batch")
    return e // 2, e % 2, b // 2, b % 2


def swap(flag, first, second):
    return jnp.where(flag, second, first), jnp.where(flag, first, second)


def add_product(start, size, tokens, gate_ref, up_ref, gate_acc, up_acc, fresh):
    step = size // 256 * 128
    for i in range(2):
        span = pl.ds(i * step, size - step if i else step)
        source = pl.ds(start + i * step, span.size)
        chunk = jnp.concatenate([ref[:, span] for ref in tokens], axis=0)
        for weight, acc in ((gate_ref, gate_acc), (up_ref, up_acc)):
            product = jnp.dot(chunk, weight[source, :], preferred_element_type=jnp.float32)
            if fresh and i == 0:
                acc[...] = product
            else:
                acc[...] += product


def first_product_kernel(size, *refs):
    *tokens, gate_ref, up_ref, gate_acc, up_acc = refs
    add_product(0, size, tokens, gate_ref, up_ref, gate_acc, up_acc, True)


def hidden_kernel_of_rest(start, size, *refs):
    *tokens, gate_ref, up_ref, gate_in, up_in, out_ref, gate_acc, up_acc = refs
    z, y, x, c = coordinates()
    live = tokens[0].shape[0]
    gate_acc[...] = gate_in[...]
    up_acc[...] = up_in[...]
    add_product(start, size, tokens, gate_ref, up_ref, gate_acc, up_acc, False)
    kept, sent = [], []
    for i, ref in enumerate(tokens):
        span = pl.ds(i * live, live)
        gate = gate_acc[span, :]
        hidden = gate / (1.0 + jnp.exp(-gate)) * up_acc[span, :]
        prob = jnp.sum(ref[:, size : size + 128].astype(jnp.float32), axis=1, keepdims=True)
        hidden = hidden * prob
        slots = hidden.reshape(2, 2, live // 4, -1)
        same, other = swap(y == 1, slots[:, 0], slots[:, 1])
        block = jnp.concatenate([same, other]).reshape(live, -1)
        (sent if i % 2 else kept).append(block)
    out_ref[...] = jnp.concatenate(kept + sent, axis=0).astype(out_ref.dtype)


def ordered_down_kernel(hidden_ref, down_ref, *outs):
    keep_first, send_first, keep_rest, send_rest = outs
    width = down_ref.shape[1]
    rows = keep_first.shape[0]
    half = hidden_ref.shape[0] // 2
    steps = 4
    for i in range(steps):
        span = pl.ds(i * (width // steps), width // steps)
        terms = jnp.dot(hidden_ref[...], down_ref[:, span], preferred_element_type=jnp.float32).astype(
            keep_first.dtype
        )
        for base, first, rest in ((0, keep_first, keep_rest), (half, send_first, send_rest)):
            first[:, span] = terms[base + 2 * rows : base + 3 * rows]
            rest[: 2 * rows, span] = terms[base : base + 2 * rows]
            rest[2 * rows :, span] = terms[base + 3 * rows : base + 4 * rows]


def put(out, rows):
    width = min(rows.shape[1], out.shape[1])
    out[:, :width] = rows[:, :width]
    if out.shape[1] > width:
        out[:, width:] = jnp.zeros((rows.shape[0], out.shape[1] - width), out.dtype)


def core_sum(keep_ref, received_ref, start, rows):
    span = pl.ds(start, rows)
    return keep_ref[span, :].astype(jnp.float32) + received_ref[span, :].astype(jnp.float32)


def by_z(rows):
    z, y, x, c = coordinates()
    slot = rows.shape[0] // 2
    return swap((z == 0) | (z == 3), rows[:slot], rows[slot:])


def first_sums_kernel(keep_ref, received_ref, near_ref, far_ref):
    near, far = by_z(core_sum(keep_ref, received_ref, 0, keep_ref.shape[0]))
    put(near_ref, near.astype(near_ref.dtype))
    put(far_ref, far.astype(far_ref.dtype))


def other_sums_kernel(keep_ref, received_ref, near_ref, far_ref, along_ref, diagonal_ref):
    rows = along_ref.shape[0]
    near, far = by_z(core_sum(keep_ref, received_ref, 0, rows))
    near_ref[...] = near.astype(near_ref.dtype)
    far_ref[...] = far.astype(far_ref.dtype)
    put(along_ref, core_sum(keep_ref, received_ref, rows, rows).astype(along_ref.dtype))
    put(diagonal_ref, core_sum(keep_ref, received_ref, 2 * rows, rows).astype(diagonal_ref.dtype))


def add_kernel(first, second, *outs):
    width = first.shape[1]
    total = first[...].astype(jnp.float32) + second[:, :width].astype(jnp.float32)
    for out in outs:
        put(out, total.astype(out.dtype))


def add_by_z_kernel(first, second, *outs):
    width = first.shape[1]
    halves = by_z(first[...].astype(jnp.float32) + second[:, :width].astype(jnp.float32))
    for i, out in enumerate(outs):
        put(out, halves[min(i // 2, 1)].astype(out.dtype))


def run_copies(pairs, sems):
    copies = [pltpu.make_async_copy(source, target, sems.at[i]) for i, (source, target) in enumerate(pairs)]
    for copy in copies:
        copy.start()
    for copy in copies:
        copy.wait()


def place_kernel(layout, zeros, pieces, out_ref, sems):
    z, y, x, c = coordinates()
    width = out_ref.shape[2]
    for mine in range(2):

        @pl.when(z == mine)
        def _():
            pairs = []
            for (index, other, *only), piece in zip(layout, pieces):
                if mine not in (only or (0, 1)):
                    continue
                source = (mine, 1 - mine, 2 + mine, 3 - mine)[index]
                pairs.append((piece.at[:, pl.ds(0, width)], out_ref.at[source * 2 + (y ^ other)]))
            run_copies(pairs, sems)

    if zeros is not None:

        @pl.when(z >= 2)
        def _():
            zeros[...] = jnp.zeros_like(zeros)
            run_copies([(zeros, out_ref.at[i]) for i in range(out_ref.shape[0])], sems)


def place_first_kernel(layout, *refs):
    *pieces, out_ref, zeros, sems = refs
    place_kernel(layout, zeros, pieces, out_ref, sems)


def place_rest_kernel(layout, *refs):
    out_ref, sems = refs[-2:]
    place_kernel(layout, None, refs[: len(layout)], out_ref, sems)


def ports_body(tokens, route_prob, counts, w_gate, w_up, w_down):
    cap, width = tokens.shape[1:]
    units = w_gate.shape[2]
    rows = LIVE // 2
    both_axes = ("expert", "batch")

    def device(z, y, x, c):
        return (z * 2 + y) * 4 + x * 2 + c

    places = [(z, y, x, c) for z in range(4) for y in range(2) for x in range(2) for c in range(2)]

    def other_core(value):
        return lax.ppermute(value, "batch", xor_pairs(4, 1))

    def across_plane(value, dx, dy):
        return lax.ppermute(value, both_axes, [(device(*p), device(p[0], p[1] ^ dy, p[2] ^ dx, p[3])) for p in places])

    def along_z(value, *moves):
        pairs = [(device(s, *p[1:]), device(t, *p[1:])) for s, t in moves for p in places if p[0] == 0]
        return lax.ppermute(value, both_axes, pairs)

    def array(rows, columns, dtype=jnp.bfloat16):
        return jax.ShapeDtypeStruct((rows, columns), dtype)

    depth = (width + PROB_COLUMNS) // 2
    rest = width - depth
    in_hbm = [pltpu.with_memory_space_constraint(a, pltpu.HBM) for a in (tokens, route_prob, counts.T)]
    piece = pltpu.VMEM((LIVE, depth), tokens.dtype)
    own = [
        call(live_rows_kernel, piece, in_hbm[:1], [HBM], [pltpu.SemaphoreType.DMA], name="live_rows"),
        call(
            lambda *refs: live_rows_and_prob_kernel(depth, *refs),
            [piece],
            in_hbm,
            [HBM, HBM, HBM],
            [
                pltpu.VMEM(route_prob.shape, route_prob.dtype),
                pltpu.VMEM(counts.T.shape, counts.dtype),
                pltpu.SemaphoreType.DMA((3,)),
            ],
            name="live_rows_and_prob",
        )[0],
    ]
    across = [lax.ppermute(piece, "batch", xor_pairs(4, 2)) for piece in own]
    near = [other_core(piece) for piece in own]
    gate_w, up_w, down_w = resident(after(w_gate[0], *own), w_up[0], w_down[0])
    across = [after(piece, down_w) for piece in across]
    pieces = [[own[0], near[0], across[0], other_core(across[0])], None]
    gate, upper = call(
        lambda *refs: first_product_kernel(depth, *refs),
        [array(4 * LIVE, units, jnp.float32)] * 2,
        [*pieces[0], gate_w, up_w],
        name="first_product",
    )
    pieces[1] = [own[1], near[1], across[1], other_core(across[1])]
    hidden = call(
        lambda *refs: hidden_kernel_of_rest(depth, rest, *refs),
        array(4 * LIVE, units),
        [*pieces[1], gate_w, up_w, gate, upper],
        scratch=[pltpu.VMEM((4 * LIVE, units), jnp.float32)] * 2,
        name="hidden",
    )

    slot = rows // 2
    keep_first, send_first, keep_rest, send_rest = call(
        ordered_down_kernel,
        [array(rows, width), array(rows, width), array(3 * rows, width), array(3 * rows, width)],
        [hidden, down_w],
        name="down",
    )
    lead_x, rest_x = call(
        first_sums_kernel,
        [array(slot, width + n) for n in (96, 192)],
        [keep_first, other_core(send_first)],
        name="first_sums",
    )
    own_lead, own_rest, own_other, across_other = call(
        other_sums_kernel,
        [array(slot, width), array(slot, width), array(rows, width + 32), array(rows, width + 0)],
        [keep_rest, other_core(after(send_rest, lead_x))],
        name="other_sums",
    )
    lead_1, next_1 = call(
        add_kernel,
        [array(slot, width + n) for n in (128, 0)],
        [own_lead, across_plane(lead_x, 1, 0)],
        name="lead_rows",
    )
    rest_1, = call(add_kernel, [array(slot, width + 0)], [own_rest, across_plane(rest_x, 1, 0)], name="rest_rows")
    from_2 = [along_z(lead_1, (2, 0), (3, 1))]
    from_3 = [along_z(rest_1, (2, 1), (3, 0))]
    next_z = [along_z(next_1, (0, 1), (1, 0))]
    from_y = across_plane(own_other, 0, 1)
    diagonal = across_plane(across_other, 1, 1)
    lead_2, next_2, rest_2, rest_2_to_0, mark = call(
        add_by_z_kernel,
        [array(slot, width + n) for n in (64, 32, 0, 48, -32)],
        [diagonal, from_y],
        name="other_rows",
    )
    from_2.append(along_z(lead_2, (2, 0), (3, 1)))
    to_0, to_1 = along_z(rest_2_to_0, (3, 0)), along_z(rest_2, (2, 1))
    next_z.append(along_z(after(next_2, next_z[0]), (0, 1), (1, 0)))
    mark = other_core(after(mark, from_2[0], from_3[0]))
    out = jax.ShapeDtypeStruct((cap // slot, slot, width), jnp.bfloat16)
    pieces = [rest_1, rest_2, from_2[0], from_3[0], next_z[0]]
    out = call(
        lambda *refs: place_first_kernel([(0, 0), (0, 1), (2, 0), (3, 0), (1, 0)], *refs),
        out,
        pieces,
        [ANY] * len(pieces),
        [pltpu.VMEM((slot, width), jnp.bfloat16), pltpu.SemaphoreType.DMA((cap // slot,))],
        out_specs=HBM,
        name="place_first",
    )
    pieces = [from_2[1], to_0, to_1, next_z[1], mark]
    out = call(
        lambda *refs: place_rest_kernel([(2, 1), (3, 1, 0), (3, 1, 1), (1, 1)], *refs),
        jax.ShapeDtypeStruct(out.shape, out.dtype),
        [*pieces, out],
        [ANY] * len(pieces) + [HBM],
        [pltpu.SemaphoreType.DMA((len(pieces),))],
        out_specs=HBM,
        aliases={len(pieces): 0},
        name="place_rest",
    )
    return out.reshape(1, cap, width)


def solution(mesh):
    in_specs = (
        P("expert", "batch", None),
        P("expert", "batch"),
        P(),
        P("expert", None, "batch"),
        P("expert", None, "batch"),
        P("expert", "batch", None),
    )
    out_specs = P("expert", "batch", None)
    fits = dict(mesh.shape) == {"expert": 8, "batch": 4}
    body = ports_body if fits else general_body
    return jax.shard_map(body, mesh=mesh, in_specs=in_specs, out_specs=out_specs, check_vma=False)
```

```python
import jax
import jax.numpy as jnp
from jax import lax
from jax.experimental import pallas as pl
from jax.experimental.pallas import tpu as pltpu
from jax.sharding import PartitionSpec as P

LIVE = 32
PROB_COLUMNS = 256
PARTS = 2
VMEM_LIMIT = 16 * 2**20
VMEM = pl.BlockSpec(memory_space=pltpu.VMEM)
HBM = pl.BlockSpec(memory_space=pltpu.HBM)
ANY = pl.BlockSpec(memory_space=pl.ANY)
SMEM = pl.BlockSpec(memory_space=pltpu.SMEM)


def xor_pairs(size, offset):
    return [(i, i ^ offset) for i in range(size)]


def hidden_kernel(pieces, *refs):
    token_refs = refs[:pieces]
    gate_ref, up_ref, out_ref, gate_acc, up_acc = refs[pieces:]
    live = token_refs[0].shape[0]
    width = gate_ref.shape[0]
    step = width // 4

    def add(start, first):
        span = pl.ds(start, step)
        rows = jnp.concatenate([ref[:, span] for ref in token_refs], axis=0)
        gate = jnp.dot(rows, gate_ref[span, :], preferred_element_type=jnp.float32)
        upper = jnp.dot(rows, up_ref[span, :], preferred_element_type=jnp.float32)
        if first:
            gate_acc[...] = gate
            up_acc[...] = upper
        else:
            gate_acc[...] += gate
            up_acc[...] += upper

    add(0, True)

    @pl.loop(1, width // step)
    def _(i):
        add(pl.multiple_of(i * step, step), False)

    gate = gate_acc[...]
    out_ref[...] = (gate / (1.0 + jnp.exp(-gate)) * up_acc[...]).astype(out_ref.dtype)


def hidden_units(pieces, gate_w, up_w):
    live, width = pieces[0].shape
    units = gate_w.shape[1]
    rows = live * len(pieces)
    return pl.pallas_call(
        lambda *refs: hidden_kernel(len(pieces), *refs),
        out_shape=jax.ShapeDtypeStruct((rows, units), jnp.bfloat16),
        in_specs=[VMEM] * (len(pieces) + 2),
        out_specs=VMEM,
        scratch_shapes=[pltpu.VMEM((rows, units), jnp.float32)] * 2,
        compiler_params=pltpu.CompilerParams(vmem_limit_bytes=VMEM_LIMIT),
        cost_estimate=pl.CostEstimate(
            flops=4 * rows * width * units, bytes_accessed=4 * width * units, transcendentals=rows * units
        ),
        name="hidden_units",
    )(*pieces, gate_w, up_w)


def down_kernel(start, hidden_ref, down_ref, keep_ref, send_ref):
    width = keep_ref.shape[1]
    half = keep_ref.shape[0]
    step = width // 2

    @pl.loop(0, width // step)
    def _(i):
        span = pl.ds(pl.multiple_of(i * step, step), step)
        source = pl.ds(pl.multiple_of(start + i * step, step), step)
        terms = jnp.dot(hidden_ref[...], down_ref[:, source], preferred_element_type=jnp.float32).astype(
            keep_ref.dtype
        )
        keep_ref[:, span] = terms[:half]
        send_ref[:, span] = terms[half:]


def down_part(hidden, down_w, start, width):
    rows, units = hidden.shape
    shape = jax.ShapeDtypeStruct((rows // 2, width), jnp.bfloat16)
    return pl.pallas_call(
        lambda *refs: down_kernel(start, *refs),
        out_shape=[shape, shape],
        in_specs=[VMEM] * 2,
        out_specs=[VMEM] * 2,
        compiler_params=pltpu.CompilerParams(vmem_limit_bytes=VMEM_LIMIT),
        cost_estimate=pl.CostEstimate(
            flops=2 * rows * width * units, bytes_accessed=2 * width * units, transcendentals=0
        ),
        name="down_part",
    )(hidden, down_w)


def general_body(tokens, route_prob, counts, w_gate, w_up, w_down):
    cap, width = tokens.shape[1:]
    n_batch = lax.axis_size("batch")
    n_experts = lax.axis_size("expert")
    expert_id = lax.axis_index("expert")
    batch_id = lax.axis_index("batch")
    slot = cap // n_experts
    live_slots = LIVE // slot
    part = width // PARTS

    own = tokens[0, :LIVE]
    even = [own] + [lax.ppermute(own, "batch", xor_pairs(n_batch, d)) for d in range(2, n_batch, 2)]
    odd = [lax.ppermute(piece, "batch", xor_pairs(n_batch, 1)) for piece in even]
    hidden = hidden_units(even + odd, w_gate[0], w_up[0])

    count = counts[expert_id, batch_id]
    live = jnp.arange(LIVE, dtype=jnp.int32) < count
    scale = jnp.where(live, route_prob[0, :LIVE], 0.0)[:, None]

    columns = []
    for start in range(0, width, part):
        keep, send = down_part(hidden, w_down[0], start, part)
        received = lax.ppermute(send, "batch", xor_pairs(n_batch, 1))
        both = keep.astype(jnp.float32) + received.astype(jnp.float32)
        total = both[:LIVE]
        for i, d in enumerate(range(2, n_batch, 2), 1):
            term = both[i * LIVE : (i + 1) * LIVE].astype(jnp.bfloat16)
            total += lax.ppermute(term, "batch", xor_pairs(n_batch, d)).astype(jnp.float32)
        expert_out = jnp.where(live[:, None], scale * total, 0.0).astype(jnp.bfloat16)
        grouped = expert_out.reshape(live_slots, slot, part)

        picks = {}
        for d in sorted(range(1, n_experts), key=lambda d: (-(d // live_slots), d)):
            pairs = [(e, e ^ d) for e in range(n_experts) if e ^ d < live_slots]
            target = jnp.minimum(expert_id ^ d, live_slots - 1)
            payload = lax.dynamic_index_in_dim(grouped, target, 0, keepdims=False)
            picks[d] = lax.ppermute(payload, "expert", pairs)
        mine = lax.dynamic_index_in_dim(grouped, jnp.minimum(expert_id, live_slots - 1), 0, keepdims=False)
        picks[0] = jnp.where(expert_id < live_slots, mine, jnp.zeros_like(mine))
        stacked = jnp.stack([picks[d] for d in range(n_experts)])
        columns.append(jnp.take(stacked, jnp.arange(n_experts, dtype=jnp.int32) ^ expert_id, axis=0))
    returned = jnp.concatenate(columns, axis=-1)
    return returned.reshape(1, cap, width)


def call(kernel, outs, args, specs=None, scratch=(), out_specs=None, aliases=None, name=None):
    return pl.pallas_call(
        kernel,
        out_shape=outs,
        in_specs=specs or [VMEM] * len(args),
        out_specs=out_specs or jax.tree.map(lambda _: VMEM, outs),
        scratch_shapes=list(scratch),
        input_output_aliases=aliases or {},
        compiler_params=pltpu.CompilerParams(vmem_limit_bytes=VMEM_LIMIT),
        cost_estimate=pl.CostEstimate(flops=0, bytes_accessed=0, transcendentals=0),
        name=name,
    )(*args)


def live_rows_kernel(tokens_ref, out_ref, sem):
    rows, size = out_ref.shape
    copy = pltpu.make_async_copy(tokens_ref.at[0, pl.ds(0, rows), pl.ds(0, size)], out_ref, sem)
    copy.start()
    copy.wait()


def live_rows_and_prob_kernel(start, tokens_ref, prob_ref, counts_ref, *refs):
    *outs, prob_copy, counts_copy, sems = refs
    z, y, x, c = coordinates()
    rows = outs[0].shape[0]
    copies = [
        pltpu.make_async_copy(prob_ref, prob_copy, sems.at[len(outs)]),
        pltpu.make_async_copy(counts_ref, counts_copy, sems.at[len(outs) + 1]),
    ]
    for i, out in enumerate(outs):
        size = out.shape[1] - (PROB_COLUMNS if i == len(outs) - 1 else 0)
        source = tokens_ref.at[0, pl.ds(0, rows), pl.ds(start, size)]
        copies.append(pltpu.make_async_copy(source, out.at[:, pl.ds(0, size)], sems.at[i]))
        start += size
    for copy in copies:
        copy.start()
    for copy in copies[:2]:
        copy.wait()
    block = lax.broadcasted_iota(jnp.int32, counts_copy.shape, 0) == x * 2 + c
    expert = lax.broadcasted_iota(jnp.int32, counts_copy.shape, 1) == z * 2 + y
    count = jnp.sum(jnp.where(block & expert, counts_copy[...], 0), axis=1, keepdims=True)
    count = jnp.sum(count, axis=0, keepdims=True)
    slots = prob_copy.shape[1]
    row = lax.broadcasted_iota(jnp.int32, (rows, slots), 0)
    lane = lax.broadcasted_iota(jnp.int32, (rows, slots), 1)
    prob = jnp.sum(jnp.where((row == lane) & (row < count), prob_copy[...], 0.0), axis=1, keepdims=True)
    column = lax.broadcasted_iota(jnp.int32, (rows, PROB_COLUMNS), 1)
    terms = jnp.zeros((rows, PROB_COLUMNS), jnp.float32)
    for i in range(3):
        term = prob.astype(jnp.bfloat16).astype(jnp.float32)
        prob = prob - term
        terms = jnp.where(column == i, term, terms)
    outs[-1][:, size:] = terms.astype(outs[-1].dtype)
    for copy in copies[2:]:
        copy.wait()


def resident_kernel(*refs):
    count = len(refs) // 2
    sems = refs[-1]
    copies = [pltpu.make_async_copy(refs[i], refs[count + i], sems.at[i]) for i in range(count)]
    for copy in copies:
        copy.start()
    for copy in copies:
        copy.wait()


def resident(*arrays):
    return call(
        resident_kernel,
        [pltpu.VMEM(a.shape, a.dtype) for a in arrays],
        [pltpu.with_memory_space_constraint(a, pltpu.HBM) for a in arrays],
        [HBM] * len(arrays),
        [pltpu.SemaphoreType.DMA((len(arrays),))],
        name="resident",
    )


def after(value, *others):
    return lax.optimization_barrier((value, *others))[0]


def coordinates():
    e = lax.axis_index("expert")
    b = lax.axis_index("batch")
    return e // 2, e % 2, b // 2, b % 2


def swap(flag, first, second):
    return jnp.where(flag, second, first), jnp.where(flag, first, second)


def add_product(start, size, tokens, gate_ref, up_ref, gate_acc, up_acc, fresh):
    step = size // 256 * 128
    for i in range(2):
        span = pl.ds(i * step, size - step if i else step)
        source = pl.ds(start + i * step, span.size)
        chunk = jnp.concatenate([ref[:, span] for ref in tokens], axis=0)
        for weight, acc in ((gate_ref, gate_acc), (up_ref, up_acc)):
            product = jnp.dot(chunk, weight[source, :], preferred_element_type=jnp.float32)
            if fresh and i == 0:
                acc[...] = product
            else:
                acc[...] += product


def first_product_kernel(size, *refs):
    *tokens, gate_ref, up_ref, gate_acc, up_acc = refs
    add_product(0, size, tokens, gate_ref, up_ref, gate_acc, up_acc, True)


def hidden_kernel_of_rest(start, size, *refs):
    *tokens, gate_ref, up_ref, gate_in, up_in, out_ref, gate_acc, up_acc = refs
    z, y, x, c = coordinates()
    live = tokens[0].shape[0]
    gate_acc[...] = gate_in[...]
    up_acc[...] = up_in[...]
    add_product(start, size, tokens, gate_ref, up_ref, gate_acc, up_acc, False)
    kept, sent = [], []
    for i, ref in enumerate(tokens):
        span = pl.ds(i * live, live)
        gate = gate_acc[span, :]
        hidden = gate / (1.0 + jnp.exp(-gate)) * up_acc[span, :]
        prob = jnp.sum(ref[:, size : size + 128].astype(jnp.float32), axis=1, keepdims=True)
        hidden = hidden * prob
        slots = hidden.reshape(2, 2, live // 4, -1)
        same, other = swap(y == 1, slots[:, 0], slots[:, 1])
        block = jnp.concatenate([same, other]).reshape(live, -1)
        (sent if i % 2 else kept).append(block)
    out_ref[...] = jnp.concatenate(kept + sent, axis=0).astype(out_ref.dtype)


def ordered_down_kernel(hidden_ref, down_ref, *outs):
    keep_first, send_first, keep_rest, send_rest = outs
    width = down_ref.shape[1]
    slot = keep_first.shape[0]
    half = hidden_ref.shape[0] // 2
    steps = 4
    for i in range(steps):
        span = pl.ds(i * (width // steps), width // steps)
        terms = jnp.dot(hidden_ref[...], down_ref[:, span], preferred_element_type=jnp.float32)
        for base, first, rest in ((0, keep_first, keep_rest), (half, send_first, send_rest)):
            lead, other = by_z(terms[base + 4 * slot : base + 6 * slot])
            first[:, span] = lead.astype(first.dtype)
            rest[: 4 * slot, span] = terms[base : base + 4 * slot].astype(first.dtype)
            rest[4 * slot : 6 * slot, span] = terms[base + 6 * slot : base + 8 * slot].astype(first.dtype)
            rest[6 * slot :, span] = other.astype(first.dtype)


def put(out, rows):
    width = min(rows.shape[1], out.shape[1])
    out[:, :width] = rows[:, :width]
    if out.shape[1] > width:
        out[:, width:] = jnp.zeros((rows.shape[0], out.shape[1] - width), out.dtype)


def core_sum(keep_ref, received_ref, start, rows):
    span = pl.ds(start, rows)
    return keep_ref[span, :].astype(jnp.float32) + received_ref[span, :].astype(jnp.float32)


def by_z(rows):
    z, y, x, c = coordinates()
    slot = rows.shape[0] // 2
    return swap((z == 0) | (z == 3), rows[:slot], rows[slot:])


def first_sums_kernel(keep_ref, received_ref, lead_ref):
    put(lead_ref, core_sum(keep_ref, received_ref, 0, keep_ref.shape[0]).astype(lead_ref.dtype))


def other_sums_kernel(keep_ref, received_ref, lead_ref, rest_ref, along_ref, diagonal_ref, across_ref):
    rows = along_ref.shape[0]
    put(across_ref, core_sum(keep_ref, received_ref, 3 * rows, rows // 2).astype(across_ref.dtype))
    put(along_ref, core_sum(keep_ref, received_ref, rows, rows).astype(along_ref.dtype))
    put(diagonal_ref, core_sum(keep_ref, received_ref, 2 * rows, rows).astype(diagonal_ref.dtype))
    lead, rest = by_z(core_sum(keep_ref, received_ref, 0, rows))
    lead_ref[...] = lead.astype(lead_ref.dtype)
    rest_ref[...] = rest.astype(rest_ref.dtype)


def add_kernel(first, second, *outs):
    width = first.shape[1]
    total = first[...].astype(jnp.float32) + second[:, :width].astype(jnp.float32)
    for out in outs:
        put(out, total.astype(out.dtype))


def add_by_z_kernel(first, second, *outs):
    width = first.shape[1]
    halves = by_z(first[...].astype(jnp.float32) + second[:, :width].astype(jnp.float32))
    for i, out in enumerate(outs):
        put(out, halves[min(i // 2, 1)].astype(out.dtype))


def run_copies(pairs, sems):
    copies = [pltpu.make_async_copy(source, target, sems.at[i]) for i, (source, target) in enumerate(pairs)]
    for copy in copies:
        copy.start()
    for copy in copies:
        copy.wait()


def place_kernel(layout, zeros, pieces, out_ref, sems):
    z, y, x, c = coordinates()
    width = out_ref.shape[2]
    for mine in range(2):

        @pl.when(z == mine)
        def _():
            pairs = []
            for (index, other, *only), piece in zip(layout, pieces):
                if mine not in (only or (0, 1)):
                    continue
                source = (mine, 1 - mine, 2 + mine, 3 - mine)[index]
                pairs.append((piece.at[:, pl.ds(0, width)], out_ref.at[source * 2 + (y ^ other)]))
            run_copies(pairs, sems)

    if zeros is not None:

        @pl.when(z >= 2)
        def _():
            zeros[...] = jnp.zeros_like(zeros)
            run_copies([(zeros, out_ref.at[i]) for i in range(out_ref.shape[0])], sems)


def place_first_kernel(layout, *refs):
    *pieces, out_ref, zeros, sems = refs
    place_kernel(layout, zeros, pieces, out_ref, sems)


def place_rest_kernel(layout, *refs):
    out_ref, sems = refs[-2:]
    place_kernel(layout, None, refs[: len(layout)], out_ref, sems)


def ports_body(tokens, route_prob, counts, w_gate, w_up, w_down):
    cap, width = tokens.shape[1:]
    units = w_gate.shape[2]
    rows = LIVE // 2
    both_axes = ("expert", "batch")

    def device(z, y, x, c):
        return (z * 2 + y) * 4 + x * 2 + c

    places = [(z, y, x, c) for z in range(4) for y in range(2) for x in range(2) for c in range(2)]

    def other_core(value):
        return lax.ppermute(value, "batch", xor_pairs(4, 1))

    def across_plane(value, dx, dy):
        return lax.ppermute(value, both_axes, [(device(*p), device(p[0], p[1] ^ dy, p[2] ^ dx, p[3])) for p in places])

    def along_z(value, *moves):
        pairs = [(device(s, *p[1:]), device(t, *p[1:])) for s, t in moves for p in places if p[0] == 0]
        return lax.ppermute(value, both_axes, pairs)

    def array(rows, columns, dtype=jnp.bfloat16):
        return jax.ShapeDtypeStruct((rows, columns), dtype)

    depth = (width + PROB_COLUMNS) // 2
    rest = width - depth
    in_hbm = [pltpu.with_memory_space_constraint(a, pltpu.HBM) for a in (tokens, route_prob, counts.T)]
    piece = pltpu.VMEM((LIVE, depth), tokens.dtype)
    own = [
        call(live_rows_kernel, piece, in_hbm[:1], [HBM], [pltpu.SemaphoreType.DMA], name="live_rows"),
        call(
            lambda *refs: live_rows_and_prob_kernel(depth, *refs),
            [piece],
            in_hbm,
            [HBM, HBM, HBM],
            [
                pltpu.VMEM(route_prob.shape, route_prob.dtype),
                pltpu.VMEM(counts.T.shape, counts.dtype),
                pltpu.SemaphoreType.DMA((3,)),
            ],
            name="live_rows_and_prob",
        )[0],
    ]
    across = [lax.ppermute(piece, "batch", xor_pairs(4, 2)) for piece in own]
    near = [other_core(piece) for piece in own]
    gate_w, up_w, down_w = resident(after(w_gate[0], *own), w_up[0], w_down[0])
    across = [after(piece, down_w) for piece in across]
    pieces = [[own[0], near[0], across[0], other_core(across[0])], None]
    gate, upper = call(
        lambda *refs: first_product_kernel(depth, *refs),
        [array(4 * LIVE, units, jnp.float32)] * 2,
        [*pieces[0], gate_w, up_w],
        name="first_product",
    )
    pieces[1] = [own[1], near[1], across[1], other_core(across[1])]
    hidden = call(
        lambda *refs: hidden_kernel_of_rest(depth, rest, *refs),
        array(4 * LIVE, units),
        [*pieces[1], gate_w, up_w, gate, upper],
        scratch=[pltpu.VMEM((4 * LIVE, units), jnp.float32)] * 2,
        name="hidden",
    )

    slot = rows // 2
    keep_first, send_first, keep_rest, send_rest = call(
        ordered_down_kernel,
        [array(slot, width), array(slot, width), array(7 * slot, width), array(7 * slot, width)],
        [hidden, down_w],
        name="down",
    )
    lead_x, = call(
        first_sums_kernel,
        [array(slot, width + 96)],
        [keep_first, other_core(send_first)],
        name="first_sums",
    )
    own_lead, own_rest, own_other, across_other, rest_x = call(
        other_sums_kernel,
        [array(slot, width), array(slot, width), array(rows, width + 32), array(rows, width), array(slot, width + 128)],
        [keep_rest, other_core(after(send_rest, lead_x))],
        name="other_sums",
    )
    lead_1, next_1 = call(
        add_kernel,
        [array(slot, width + n) for n in (128, 0)],
        [own_lead, across_plane(lead_x, 1, 0)],
        name="lead_rows",
    )
    rest_1, = call(add_kernel, [array(slot, width + 0)], [own_rest, across_plane(rest_x, 1, 0)], name="rest_rows")
    from_2 = [along_z(lead_1, (2, 0), (3, 1))]
    from_3 = [along_z(rest_1, (2, 1), (3, 0))]
    next_z = [along_z(next_1, (0, 1), (1, 0))]
    from_y = across_plane(own_other, 0, 1)
    diagonal = across_plane(across_other, 1, 1)
    lead_2, next_2, rest_2, rest_2_to_0, mark = call(
        add_by_z_kernel,
        [array(slot, width + n) for n in (64, 32, 0, 48, -32)],
        [diagonal, from_y],
        name="other_rows",
    )
    from_2.append(along_z(lead_2, (2, 0), (3, 1)))
    to_0, to_1 = along_z(rest_2_to_0, (3, 0)), along_z(rest_2, (2, 1))
    next_z.append(along_z(after(next_2, next_z[0]), (0, 1), (1, 0)))
    mark = other_core(after(mark, from_2[0], from_3[0]))
    out = jax.ShapeDtypeStruct((cap // slot, slot, width), jnp.bfloat16)
    pieces = [rest_1, rest_2, from_2[0], from_3[0], next_z[0]]
    out = call(
        lambda *refs: place_first_kernel([(0, 0), (0, 1), (2, 0), (3, 0), (1, 0)], *refs),
        out,
        pieces,
        [ANY] * len(pieces),
        [pltpu.VMEM((slot, width), jnp.bfloat16), pltpu.SemaphoreType.DMA((cap // slot,))],
        out_specs=HBM,
        name="place_first",
    )
    pieces = [from_2[1], to_0, to_1, next_z[1], mark]
    out = call(
        lambda *refs: place_rest_kernel([(2, 1), (3, 1, 0), (3, 1, 1), (1, 1)], *refs),
        jax.ShapeDtypeStruct(out.shape, out.dtype),
        [*pieces, out],
        [ANY] * len(pieces) + [HBM],
        [pltpu.SemaphoreType.DMA((len(pieces),))],
        out_specs=HBM,
        aliases={len(pieces): 0},
        name="place_rest",
    )
    return out.reshape(1, cap, width)


def solution(mesh):
    in_specs = (
        P("expert", "batch", None),
        P("expert", "batch"),
        P(),
        P("expert", None, "batch"),
        P("expert", None, "batch"),
        P("expert", "batch", None),
    )
    out_specs = P("expert", "batch", None)
    fits = dict(mesh.shape) == {"expert": 8, "batch": 4}
    body = ports_body if fits else general_body
    return jax.shard_map(body, mesh=mesh, in_specs=in_specs, out_specs=out_specs, check_vma=False)
```

```python
import jax
import jax.numpy as jnp
from jax import lax
from jax.experimental import pallas as pl
from jax.experimental.pallas import tpu as pltpu
from jax.sharding import PartitionSpec as P

LIVE = 32
PROB_COLUMNS = 256
PARTS = 2
VMEM_LIMIT = 16 * 2**20
VMEM = pl.BlockSpec(memory_space=pltpu.VMEM)
HBM = pl.BlockSpec(memory_space=pltpu.HBM)
ANY = pl.BlockSpec(memory_space=pl.ANY)
SMEM = pl.BlockSpec(memory_space=pltpu.SMEM)


def xor_pairs(size, offset):
    return [(i, i ^ offset) for i in range(size)]


def hidden_kernel(pieces, *refs):
    token_refs = refs[:pieces]
    gate_ref, up_ref, out_ref, gate_acc, up_acc = refs[pieces:]
    live = token_refs[0].shape[0]
    width = gate_ref.shape[0]
    step = width // 4

    def add(start, first):
        span = pl.ds(start, step)
        rows = jnp.concatenate([ref[:, span] for ref in token_refs], axis=0)
        gate = jnp.dot(rows, gate_ref[span, :], preferred_element_type=jnp.float32)
        upper = jnp.dot(rows, up_ref[span, :], preferred_element_type=jnp.float32)
        if first:
            gate_acc[...] = gate
            up_acc[...] = upper
        else:
            gate_acc[...] += gate
            up_acc[...] += upper

    add(0, True)

    @pl.loop(1, width // step)
    def _(i):
        add(pl.multiple_of(i * step, step), False)

    gate = gate_acc[...]
    out_ref[...] = (gate / (1.0 + jnp.exp(-gate)) * up_acc[...]).astype(out_ref.dtype)


def hidden_units(pieces, gate_w, up_w):
    live, width = pieces[0].shape
    units = gate_w.shape[1]
    rows = live * len(pieces)
    return pl.pallas_call(
        lambda *refs: hidden_kernel(len(pieces), *refs),
        out_shape=jax.ShapeDtypeStruct((rows, units), jnp.bfloat16),
        in_specs=[VMEM] * (len(pieces) + 2),
        out_specs=VMEM,
        scratch_shapes=[pltpu.VMEM((rows, units), jnp.float32)] * 2,
        compiler_params=pltpu.CompilerParams(vmem_limit_bytes=VMEM_LIMIT),
        cost_estimate=pl.CostEstimate(
            flops=4 * rows * width * units, bytes_accessed=4 * width * units, transcendentals=rows * units
        ),
        name="hidden_units",
    )(*pieces, gate_w, up_w)


def down_kernel(start, hidden_ref, down_ref, keep_ref, send_ref):
    width = keep_ref.shape[1]
    half = keep_ref.shape[0]
    step = width // 2

    @pl.loop(0, width // step)
    def _(i):
        span = pl.ds(pl.multiple_of(i * step, step), step)
        source = pl.ds(pl.multiple_of(start + i * step, step), step)
        terms = jnp.dot(hidden_ref[...], down_ref[:, source], preferred_element_type=jnp.float32).astype(
            keep_ref.dtype
        )
        keep_ref[:, span] = terms[:half]
        send_ref[:, span] = terms[half:]


def down_part(hidden, down_w, start, width):
    rows, units = hidden.shape
    shape = jax.ShapeDtypeStruct((rows // 2, width), jnp.bfloat16)
    return pl.pallas_call(
        lambda *refs: down_kernel(start, *refs),
        out_shape=[shape, shape],
        in_specs=[VMEM] * 2,
        out_specs=[VMEM] * 2,
        compiler_params=pltpu.CompilerParams(vmem_limit_bytes=VMEM_LIMIT),
        cost_estimate=pl.CostEstimate(
            flops=2 * rows * width * units, bytes_accessed=2 * width * units, transcendentals=0
        ),
        name="down_part",
    )(hidden, down_w)


def general_body(tokens, route_prob, counts, w_gate, w_up, w_down):
    cap, width = tokens.shape[1:]
    n_batch = lax.axis_size("batch")
    n_experts = lax.axis_size("expert")
    expert_id = lax.axis_index("expert")
    batch_id = lax.axis_index("batch")
    slot = cap // n_experts
    live_slots = LIVE // slot
    part = width // PARTS

    own = tokens[0, :LIVE]
    even = [own] + [lax.ppermute(own, "batch", xor_pairs(n_batch, d)) for d in range(2, n_batch, 2)]
    odd = [lax.ppermute(piece, "batch", xor_pairs(n_batch, 1)) for piece in even]
    hidden = hidden_units(even + odd, w_gate[0], w_up[0])

    count = counts[expert_id, batch_id]
    live = jnp.arange(LIVE, dtype=jnp.int32) < count
    scale = jnp.where(live, route_prob[0, :LIVE], 0.0)[:, None]

    columns = []
    for start in range(0, width, part):
        keep, send = down_part(hidden, w_down[0], start, part)
        received = lax.ppermute(send, "batch", xor_pairs(n_batch, 1))
        both = keep.astype(jnp.float32) + received.astype(jnp.float32)
        total = both[:LIVE]
        for i, d in enumerate(range(2, n_batch, 2), 1):
            term = both[i * LIVE : (i + 1) * LIVE].astype(jnp.bfloat16)
            total += lax.ppermute(term, "batch", xor_pairs(n_batch, d)).astype(jnp.float32)
        expert_out = jnp.where(live[:, None], scale * total, 0.0).astype(jnp.bfloat16)
        grouped = expert_out.reshape(live_slots, slot, part)

        picks = {}
        for d in sorted(range(1, n_experts), key=lambda d: (-(d // live_slots), d)):
            pairs = [(e, e ^ d) for e in range(n_experts) if e ^ d < live_slots]
            target = jnp.minimum(expert_id ^ d, live_slots - 1)
            payload = lax.dynamic_index_in_dim(grouped, target, 0, keepdims=False)
            picks[d] = lax.ppermute(payload, "expert", pairs)
        mine = lax.dynamic_index_in_dim(grouped, jnp.minimum(expert_id, live_slots - 1), 0, keepdims=False)
        picks[0] = jnp.where(expert_id < live_slots, mine, jnp.zeros_like(mine))
        stacked = jnp.stack([picks[d] for d in range(n_experts)])
        columns.append(jnp.take(stacked, jnp.arange(n_experts, dtype=jnp.int32) ^ expert_id, axis=0))
    returned = jnp.concatenate(columns, axis=-1)
    return returned.reshape(1, cap, width)


def call(kernel, outs, args, specs=None, scratch=(), out_specs=None, aliases=None, name=None):
    return pl.pallas_call(
        kernel,
        out_shape=outs,
        in_specs=specs or [VMEM] * len(args),
        out_specs=out_specs or jax.tree.map(lambda _: VMEM, outs),
        scratch_shapes=list(scratch),
        input_output_aliases=aliases or {},
        compiler_params=pltpu.CompilerParams(vmem_limit_bytes=VMEM_LIMIT),
        cost_estimate=pl.CostEstimate(flops=0, bytes_accessed=0, transcendentals=0),
        name=name,
    )(*args)


def live_rows_kernel(tokens_ref, out_ref, sem):
    rows, size = out_ref.shape
    copy = pltpu.make_async_copy(tokens_ref.at[0, pl.ds(0, rows), pl.ds(0, size)], out_ref, sem)
    copy.start()
    copy.wait()


def live_rows_and_prob_kernel(start, tokens_ref, prob_ref, counts_ref, *refs):
    *outs, prob_copy, counts_copy, sems = refs
    z, y, x, c = coordinates()
    rows = outs[0].shape[0]
    copies = [
        pltpu.make_async_copy(prob_ref, prob_copy, sems.at[len(outs)]),
        pltpu.make_async_copy(counts_ref, counts_copy, sems.at[len(outs) + 1]),
    ]
    for i, out in enumerate(outs):
        size = out.shape[1] - (PROB_COLUMNS if i == len(outs) - 1 else 0)
        source = tokens_ref.at[0, pl.ds(0, rows), pl.ds(start, size)]
        copies.append(pltpu.make_async_copy(source, out.at[:, pl.ds(0, size)], sems.at[i]))
        start += size
    for copy in copies:
        copy.start()
    for copy in copies[:2]:
        copy.wait()
    block = lax.broadcasted_iota(jnp.int32, counts_copy.shape, 0) == x * 2 + c
    expert = lax.broadcasted_iota(jnp.int32, counts_copy.shape, 1) == z * 2 + y
    count = jnp.sum(jnp.where(block & expert, counts_copy[...], 0), axis=1, keepdims=True)
    count = jnp.sum(count, axis=0, keepdims=True)
    slots = prob_copy.shape[1]
    row = lax.broadcasted_iota(jnp.int32, (rows, slots), 0)
    lane = lax.broadcasted_iota(jnp.int32, (rows, slots), 1)
    prob = jnp.sum(jnp.where((row == lane) & (row < count), prob_copy[...], 0.0), axis=1, keepdims=True)
    column = lax.broadcasted_iota(jnp.int32, (rows, PROB_COLUMNS), 1)
    terms = jnp.zeros((rows, PROB_COLUMNS), jnp.float32)
    for i in range(3):
        term = prob.astype(jnp.bfloat16).astype(jnp.float32)
        prob = prob - term
        terms = jnp.where(column == i, term, terms)
    outs[-1][:, size:] = terms.astype(outs[-1].dtype)
    for copy in copies[2:]:
        copy.wait()


def resident_kernel(*refs):
    count = len(refs) // 2
    sems = refs[-1]
    copies = [pltpu.make_async_copy(refs[i], refs[count + i], sems.at[i]) for i in range(count)]
    for copy in copies:
        copy.start()
    for copy in copies:
        copy.wait()


def resident(*arrays):
    return call(
        resident_kernel,
        [pltpu.VMEM(a.shape, a.dtype) for a in arrays],
        [pltpu.with_memory_space_constraint(a, pltpu.HBM) for a in arrays],
        [HBM] * len(arrays),
        [pltpu.SemaphoreType.DMA((len(arrays),))],
        name="resident",
    )


def after(value, *others):
    return lax.optimization_barrier((value, *others))[0]


def coordinates():
    e = lax.axis_index("expert")
    b = lax.axis_index("batch")
    return e // 2, e % 2, b // 2, b % 2


def swap(flag, first, second):
    return jnp.where(flag, second, first), jnp.where(flag, first, second)


def add_product(start, size, tokens, gate_ref, up_ref, gate_acc, up_acc, fresh):
    step = size // 256 * 128
    for i in range(2):
        span = pl.ds(i * step, size - step if i else step)
        source = pl.ds(start + i * step, span.size)
        chunk = jnp.concatenate([ref[:, span] for ref in tokens], axis=0)
        for weight, acc in ((gate_ref, gate_acc), (up_ref, up_acc)):
            product = jnp.dot(chunk, weight[source, :], preferred_element_type=jnp.float32)
            if fresh and i == 0:
                acc[...] = product
            else:
                acc[...] += product


def first_product_kernel(size, *refs):
    *tokens, gate_ref, up_ref, gate_acc, up_acc = refs
    add_product(0, size, tokens, gate_ref, up_ref, gate_acc, up_acc, True)


def hidden_kernel_of_rest(start, size, *refs):
    *tokens, gate_ref, up_ref, gate_in, up_in, out_ref, gate_acc, up_acc = refs
    z, y, x, c = coordinates()
    live = tokens[0].shape[0]
    gate_acc[...] = gate_in[...]
    up_acc[...] = up_in[...]
    add_product(start, size, tokens, gate_ref, up_ref, gate_acc, up_acc, False)
    kept, sent = [], []
    for i, ref in enumerate(tokens):
        span = pl.ds(i * live, live)
        gate = gate_acc[span, :]
        hidden = gate / (1.0 + jnp.exp(-gate)) * up_acc[span, :]
        prob = jnp.sum(ref[:, size : size + 128].astype(jnp.float32), axis=1, keepdims=True)
        hidden = hidden * prob
        slots = hidden.reshape(2, 2, live // 4, -1)
        same, other = swap(y == 1, slots[:, 0], slots[:, 1])
        block = jnp.concatenate([same, other]).reshape(live, -1)
        (sent if i % 2 else kept).append(block)
    out_ref[...] = jnp.concatenate(kept + sent, axis=0).astype(out_ref.dtype)


def ordered_down_kernel(hidden_ref, down_ref, *outs):
    keep_first, send_first, keep_rest, send_rest = outs
    width = down_ref.shape[1]
    rows = keep_first.shape[0]
    half = hidden_ref.shape[0] // 2
    steps = 4
    for i in range(steps):
        span = pl.ds(i * (width // steps), width // steps)
        terms = jnp.dot(hidden_ref[...], down_ref[:, span], preferred_element_type=jnp.float32).astype(
            keep_first.dtype
        )
        for base, first, rest in ((0, keep_first, keep_rest), (half, send_first, send_rest)):
            first[:, span] = terms[base + 2 * rows : base + 3 * rows]
            rest[: 2 * rows, span] = terms[base : base + 2 * rows]
            rest[2 * rows :, span] = terms[base + 3 * rows : base + 4 * rows]


def put(out, rows):
    width = min(rows.shape[1], out.shape[1])
    out[:, :width] = rows[:, :width]
    if out.shape[1] > width:
        out[:, width:] = jnp.zeros((rows.shape[0], out.shape[1] - width), out.dtype)


def core_sum(keep_ref, received_ref, start, rows):
    span = pl.ds(start, rows)
    return keep_ref[span, :].astype(jnp.float32) + received_ref[span, :].astype(jnp.float32)


def by_z(rows):
    z, y, x, c = coordinates()
    slot = rows.shape[0] // 2
    return swap((z == 0) | (z == 3), rows[:slot], rows[slot:])


def first_sums_kernel(keep_ref, received_ref, near_ref, far_ref):
    near, far = by_z(core_sum(keep_ref, received_ref, 0, keep_ref.shape[0]))
    put(near_ref, near.astype(near_ref.dtype))
    put(far_ref, far.astype(far_ref.dtype))


def other_sums_kernel(keep_ref, received_ref, near_ref, far_ref, along_ref, diagonal_ref):
    rows = along_ref.shape[0]
    near, far = by_z(core_sum(keep_ref, received_ref, 0, rows))
    near_ref[...] = near.astype(near_ref.dtype)
    far_ref[...] = far.astype(far_ref.dtype)
    put(along_ref, core_sum(keep_ref, received_ref, rows, rows).astype(along_ref.dtype))
    put(diagonal_ref, core_sum(keep_ref, received_ref, 2 * rows, rows).astype(diagonal_ref.dtype))


def add_kernel(first, second, *outs):
    width = first.shape[1]
    total = first[...].astype(jnp.float32) + second[:, :width].astype(jnp.float32)
    for out in outs:
        put(out, total.astype(out.dtype))


def add_by_z_kernel(first, second, *outs):
    width = first.shape[1]
    halves = by_z(first[...].astype(jnp.float32) + second[:, :width].astype(jnp.float32))
    for i, out in enumerate(outs):
        put(out, halves[min(i // 2, 1)].astype(out.dtype))


def run_copies(pairs, sems):
    copies = [pltpu.make_async_copy(source, target, sems.at[i]) for i, (source, target) in enumerate(pairs)]
    for copy in copies:
        copy.start()
    for copy in copies:
        copy.wait()


def place_kernel(layout, zeros, pieces, out_ref, sems):
    z, y, x, c = coordinates()
    width = out_ref.shape[2]
    for mine in range(2):

        @pl.when(z == mine)
        def _():
            pairs = []
            for (index, other, *only), piece in zip(layout, pieces):
                if mine not in (only or (0, 1)):
                    continue
                source = (mine, 1 - mine, 2 + mine, 3 - mine)[index]
                pairs.append((piece.at[:, pl.ds(0, width)], out_ref.at[source * 2 + (y ^ other)]))
            run_copies(pairs, sems)

    if zeros is not None:

        @pl.when(z >= 2)
        def _():
            zeros[...] = jnp.zeros_like(zeros)
            run_copies([(zeros, out_ref.at[i]) for i in range(out_ref.shape[0])], sems)


def place_first_kernel(layout, *refs):
    *pieces, out_ref, zeros, sems = refs
    place_kernel(layout, zeros, pieces, out_ref, sems)


def place_rest_kernel(layout, *refs):
    out_ref, sems = refs[-2:]
    place_kernel(layout, None, refs[: len(layout)], out_ref, sems)


def ports_body(tokens, route_prob, counts, w_gate, w_up, w_down):
    cap, width = tokens.shape[1:]
    units = w_gate.shape[2]
    rows = LIVE // 2
    both_axes = ("expert", "batch")

    def device(z, y, x, c):
        return (z * 2 + y) * 4 + x * 2 + c

    places = [(z, y, x, c) for z in range(4) for y in range(2) for x in range(2) for c in range(2)]

    def other_core(value):
        return lax.ppermute(value, "batch", xor_pairs(4, 1))

    def across_plane(value, dx, dy):
        return lax.ppermute(value, both_axes, [(device(*p), device(p[0], p[1] ^ dy, p[2] ^ dx, p[3])) for p in places])

    def along_z(value, *moves):
        pairs = [(device(s, *p[1:]), device(t, *p[1:])) for s, t in moves for p in places if p[0] == 0]
        return lax.ppermute(value, both_axes, pairs)

    def array(rows, columns, dtype=jnp.bfloat16):
        return jax.ShapeDtypeStruct((rows, columns), dtype)

    depth = (width + PROB_COLUMNS) // 2
    rest = width - depth
    in_hbm = [pltpu.with_memory_space_constraint(a, pltpu.HBM) for a in (tokens, route_prob, counts.T)]
    piece = pltpu.VMEM((LIVE, depth), tokens.dtype)
    own = [
        call(live_rows_kernel, piece, in_hbm[:1], [HBM], [pltpu.SemaphoreType.DMA], name="live_rows"),
        call(
            lambda *refs: live_rows_and_prob_kernel(depth, *refs),
            [piece],
            in_hbm,
            [HBM, HBM, HBM],
            [
                pltpu.VMEM(route_prob.shape, route_prob.dtype),
                pltpu.VMEM(counts.T.shape, counts.dtype),
                pltpu.SemaphoreType.DMA((3,)),
            ],
            name="live_rows_and_prob",
        )[0],
    ]
    across = [lax.ppermute(piece, "batch", xor_pairs(4, 2)) for piece in own]
    near = [other_core(piece) for piece in own]
    gate_w, up_w, down_w = resident(after(w_gate[0], *own), w_up[0], w_down[0])
    across = [after(piece, down_w) for piece in across]
    pieces = [[own[0], near[0], across[0], other_core(across[0])], None]
    gate, upper = call(
        lambda *refs: first_product_kernel(depth, *refs),
        [array(4 * LIVE, units, jnp.float32)] * 2,
        [*pieces[0], gate_w, up_w],
        name="first_product",
    )
    pieces[1] = [own[1], near[1], across[1], other_core(across[1])]
    hidden = call(
        lambda *refs: hidden_kernel_of_rest(depth, rest, *refs),
        array(4 * LIVE, units),
        [*pieces[1], gate_w, up_w, gate, upper],
        scratch=[pltpu.VMEM((4 * LIVE, units), jnp.float32)] * 2,
        name="hidden",
    )

    slot = rows // 2
    keep_first, send_first, keep_rest, send_rest = call(
        ordered_down_kernel,
        [array(rows, width), array(rows, width), array(3 * rows, width), array(3 * rows, width)],
        [hidden, down_w],
        name="down",
    )
    lead_x, rest_x = call(
        first_sums_kernel,
        [array(slot, width + n) for n in (96, 192)],
        [keep_first, other_core(send_first)],
        name="first_sums",
    )
    own_lead, own_rest, own_other, across_other = call(
        other_sums_kernel,
        [array(slot, width), array(slot, width), array(rows, width + 32), array(rows, width + 0)],
        [keep_rest, other_core(after(send_rest, lead_x))],
        name="other_sums",
    )
    lead_1, next_1 = call(
        add_kernel,
        [array(slot, width + n) for n in (128, 0)],
        [own_lead, across_plane(lead_x, 1, 0)],
        name="lead_rows",
    )
    rest_1, = call(add_kernel, [array(slot, width + 0)], [own_rest, across_plane(rest_x, 1, 0)], name="rest_rows")
    from_2 = [along_z(lead_1, (2, 0), (3, 1))]
    from_3 = [along_z(rest_1, (2, 1), (3, 0))]
    next_z = [along_z(next_1, (0, 1), (1, 0))]
    from_y = across_plane(own_other, 0, 1)
    diagonal = across_plane(across_other, 1, 1)
    lead_2, next_2, rest_2, rest_2_to_0, mark = call(
        add_by_z_kernel,
        [array(slot, width + n) for n in (64, 48, 0, 32, -32)],
        [diagonal, from_y],
        name="other_rows",
    )
    from_2.append(along_z(lead_2, (2, 0), (3, 1)))
    to_0, to_1 = along_z(rest_2_to_0, (3, 0)), along_z(rest_2, (2, 1))
    next_z.append(along_z(after(next_2, next_z[0]), (0, 1), (1, 0)))
    mark = other_core(after(mark, from_2[0], from_3[0]))
    out = jax.ShapeDtypeStruct((cap // slot, slot, width), jnp.bfloat16)
    pieces = [rest_1, rest_2, from_2[0], from_3[0], next_z[0]]
    out = call(
        lambda *refs: place_first_kernel([(0, 0), (0, 1), (2, 0), (3, 0), (1, 0)], *refs),
        out,
        pieces,
        [ANY] * len(pieces),
        [pltpu.VMEM((slot, width), jnp.bfloat16), pltpu.SemaphoreType.DMA((cap // slot,))],
        out_specs=HBM,
        name="place_first",
    )
    pieces = [from_2[1], to_0, to_1, next_z[1], mark]
    out = call(
        lambda *refs: place_rest_kernel([(2, 1), (3, 1, 0), (3, 1, 1), (1, 1)], *refs),
        jax.ShapeDtypeStruct(out.shape, out.dtype),
        [*pieces, out],
        [ANY] * len(pieces) + [HBM],
        [pltpu.SemaphoreType.DMA((len(pieces),))],
        out_specs=HBM,
        aliases={len(pieces): 0},
        name="place_rest",
    )
    return out.reshape(1, cap, width)


def solution(mesh):
    in_specs = (
        P("expert", "batch", None),
        P("expert", "batch"),
        P(),
        P("expert", None, "batch"),
        P("expert", None, "batch"),
        P("expert", "batch", None),
    )
    out_specs = P("expert", "batch", None)
    fits = dict(mesh.shape) == {"expert": 8, "batch": 4}
    body = ports_body if fits else general_body
    return jax.shard_map(body, mesh=mesh, in_specs=in_specs, out_specs=out_specs, check_vma=False)
```

```python
import jax
import jax.numpy as jnp
from jax import lax
from jax.experimental import pallas as pl
from jax.experimental.pallas import tpu as pltpu
from jax.sharding import PartitionSpec as P

LIVE = 32
PROB_COLUMNS = 256
PARTS = 2
VMEM_LIMIT = 16 * 2**20
VMEM = pl.BlockSpec(memory_space=pltpu.VMEM)
HBM = pl.BlockSpec(memory_space=pltpu.HBM)
ANY = pl.BlockSpec(memory_space=pl.ANY)
SMEM = pl.BlockSpec(memory_space=pltpu.SMEM)


def xor_pairs(size, offset):
    return [(i, i ^ offset) for i in range(size)]


def hidden_kernel(pieces, *refs):
    token_refs = refs[:pieces]
    gate_ref, up_ref, out_ref, gate_acc, up_acc = refs[pieces:]
    live = token_refs[0].shape[0]
    width = gate_ref.shape[0]
    step = width // 4

    def add(start, first):
        span = pl.ds(start, step)
        rows = jnp.concatenate([ref[:, span] for ref in token_refs], axis=0)
        gate = jnp.dot(rows, gate_ref[span, :], preferred_element_type=jnp.float32)
        upper = jnp.dot(rows, up_ref[span, :], preferred_element_type=jnp.float32)
        if first:
            gate_acc[...] = gate
            up_acc[...] = upper
        else:
            gate_acc[...] += gate
            up_acc[...] += upper

    add(0, True)

    @pl.loop(1, width // step)
    def _(i):
        add(pl.multiple_of(i * step, step), False)

    gate = gate_acc[...]
    out_ref[...] = (gate / (1.0 + jnp.exp(-gate)) * up_acc[...]).astype(out_ref.dtype)


def hidden_units(pieces, gate_w, up_w):
    live, width = pieces[0].shape
    units = gate_w.shape[1]
    rows = live * len(pieces)
    return pl.pallas_call(
        lambda *refs: hidden_kernel(len(pieces), *refs),
        out_shape=jax.ShapeDtypeStruct((rows, units), jnp.bfloat16),
        in_specs=[VMEM] * (len(pieces) + 2),
        out_specs=VMEM,
        scratch_shapes=[pltpu.VMEM((rows, units), jnp.float32)] * 2,
        compiler_params=pltpu.CompilerParams(vmem_limit_bytes=VMEM_LIMIT),
        cost_estimate=pl.CostEstimate(
            flops=4 * rows * width * units, bytes_accessed=4 * width * units, transcendentals=rows * units
        ),
        name="hidden_units",
    )(*pieces, gate_w, up_w)


def down_kernel(start, hidden_ref, down_ref, keep_ref, send_ref):
    width = keep_ref.shape[1]
    half = keep_ref.shape[0]
    step = width // 2

    @pl.loop(0, width // step)
    def _(i):
        span = pl.ds(pl.multiple_of(i * step, step), step)
        source = pl.ds(pl.multiple_of(start + i * step, step), step)
        terms = jnp.dot(hidden_ref[...], down_ref[:, source], preferred_element_type=jnp.float32).astype(
            keep_ref.dtype
        )
        keep_ref[:, span] = terms[:half]
        send_ref[:, span] = terms[half:]


def down_part(hidden, down_w, start, width):
    rows, units = hidden.shape
    shape = jax.ShapeDtypeStruct((rows // 2, width), jnp.bfloat16)
    return pl.pallas_call(
        lambda *refs: down_kernel(start, *refs),
        out_shape=[shape, shape],
        in_specs=[VMEM] * 2,
        out_specs=[VMEM] * 2,
        compiler_params=pltpu.CompilerParams(vmem_limit_bytes=VMEM_LIMIT),
        cost_estimate=pl.CostEstimate(
            flops=2 * rows * width * units, bytes_accessed=2 * width * units, transcendentals=0
        ),
        name="down_part",
    )(hidden, down_w)


def general_body(tokens, route_prob, counts, w_gate, w_up, w_down):
    cap, width = tokens.shape[1:]
    n_batch = lax.axis_size("batch")
    n_experts = lax.axis_size("expert")
    expert_id = lax.axis_index("expert")
    batch_id = lax.axis_index("batch")
    slot = cap // n_experts
    live_slots = LIVE // slot
    part = width // PARTS

    own = tokens[0, :LIVE]
    even = [own] + [lax.ppermute(own, "batch", xor_pairs(n_batch, d)) for d in range(2, n_batch, 2)]
    odd = [lax.ppermute(piece, "batch", xor_pairs(n_batch, 1)) for piece in even]
    hidden = hidden_units(even + odd, w_gate[0], w_up[0])

    count = counts[expert_id, batch_id]
    live = jnp.arange(LIVE, dtype=jnp.int32) < count
    scale = jnp.where(live, route_prob[0, :LIVE], 0.0)[:, None]

    columns = []
    for start in range(0, width, part):
        keep, send = down_part(hidden, w_down[0], start, part)
        received = lax.ppermute(send, "batch", xor_pairs(n_batch, 1))
        both = keep.astype(jnp.float32) + received.astype(jnp.float32)
        total = both[:LIVE]
        for i, d in enumerate(range(2, n_batch, 2), 1):
            term = both[i * LIVE : (i + 1) * LIVE].astype(jnp.bfloat16)
            total += lax.ppermute(term, "batch", xor_pairs(n_batch, d)).astype(jnp.float32)
        expert_out = jnp.where(live[:, None], scale * total, 0.0).astype(jnp.bfloat16)
        grouped = expert_out.reshape(live_slots, slot, part)

        picks = {}
        for d in sorted(range(1, n_experts), key=lambda d: (-(d // live_slots), d)):
            pairs = [(e, e ^ d) for e in range(n_experts) if e ^ d < live_slots]
            target = jnp.minimum(expert_id ^ d, live_slots - 1)
            payload = lax.dynamic_index_in_dim(grouped, target, 0, keepdims=False)
            picks[d] = lax.ppermute(payload, "expert", pairs)
        mine = lax.dynamic_index_in_dim(grouped, jnp.minimum(expert_id, live_slots - 1), 0, keepdims=False)
        picks[0] = jnp.where(expert_id < live_slots, mine, jnp.zeros_like(mine))
        stacked = jnp.stack([picks[d] for d in range(n_experts)])
        columns.append(jnp.take(stacked, jnp.arange(n_experts, dtype=jnp.int32) ^ expert_id, axis=0))
    returned = jnp.concatenate(columns, axis=-1)
    return returned.reshape(1, cap, width)


def call(kernel, outs, args, specs=None, scratch=(), out_specs=None, aliases=None, name=None):
    return pl.pallas_call(
        kernel,
        out_shape=outs,
        in_specs=specs or [VMEM] * len(args),
        out_specs=out_specs or jax.tree.map(lambda _: VMEM, outs),
        scratch_shapes=list(scratch),
        input_output_aliases=aliases or {},
        compiler_params=pltpu.CompilerParams(vmem_limit_bytes=VMEM_LIMIT),
        cost_estimate=pl.CostEstimate(flops=0, bytes_accessed=0, transcendentals=0),
        name=name,
    )(*args)


def live_rows_kernel(tokens_ref, out_ref, sem):
    rows, size = out_ref.shape
    copy = pltpu.make_async_copy(tokens_ref.at[0, pl.ds(0, rows), pl.ds(0, size)], out_ref, sem)
    copy.start()
    copy.wait()


def live_rows_and_prob_kernel(start, tokens_ref, prob_ref, counts_ref, *refs):
    *outs, prob_copy, counts_copy, sems = refs
    z, y, x, c = coordinates()
    rows = outs[0].shape[0]
    copies = [
        pltpu.make_async_copy(prob_ref, prob_copy, sems.at[len(outs)]),
        pltpu.make_async_copy(counts_ref, counts_copy, sems.at[len(outs) + 1]),
    ]
    for i, out in enumerate(outs):
        size = out.shape[1] - (PROB_COLUMNS if i == len(outs) - 1 else 0)
        source = tokens_ref.at[0, pl.ds(0, rows), pl.ds(start, size)]
        copies.append(pltpu.make_async_copy(source, out.at[:, pl.ds(0, size)], sems.at[i]))
        start += size
    for copy in copies:
        copy.start()
    for copy in copies[:2]:
        copy.wait()
    block = lax.broadcasted_iota(jnp.int32, counts_copy.shape, 0) == x * 2 + c
    expert = lax.broadcasted_iota(jnp.int32, counts_copy.shape, 1) == z * 2 + y
    count = jnp.sum(jnp.where(block & expert, counts_copy[...], 0), axis=1, keepdims=True)
    count = jnp.sum(count, axis=0, keepdims=True)
    slots = prob_copy.shape[1]
    row = lax.broadcasted_iota(jnp.int32, (rows, slots), 0)
    lane = lax.broadcasted_iota(jnp.int32, (rows, slots), 1)
    prob = jnp.sum(jnp.where((row == lane) & (row < count), prob_copy[...], 0.0), axis=1, keepdims=True)
    column = lax.broadcasted_iota(jnp.int32, (rows, PROB_COLUMNS), 1)
    terms = jnp.zeros((rows, PROB_COLUMNS), jnp.float32)
    for i in range(3):
        term = prob.astype(jnp.bfloat16).astype(jnp.float32)
        prob = prob - term
        terms = jnp.where(column == i, term, terms)
    outs[-1][:, size:] = terms.astype(outs[-1].dtype)
    for copy in copies[2:]:
        copy.wait()


def resident_kernel(*refs):
    count = len(refs) // 2
    sems = refs[-1]
    copies = [pltpu.make_async_copy(refs[i], refs[count + i], sems.at[i]) for i in range(count)]
    for copy in copies:
        copy.start()
    for copy in copies:
        copy.wait()


def resident(*arrays):
    return call(
        resident_kernel,
        [pltpu.VMEM(a.shape, a.dtype) for a in arrays],
        [pltpu.with_memory_space_constraint(a, pltpu.HBM) for a in arrays],
        [HBM] * len(arrays),
        [pltpu.SemaphoreType.DMA((len(arrays),))],
        name="resident",
    )


def after(value, *others):
    return lax.optimization_barrier((value, *others))[0]


def coordinates():
    e = lax.axis_index("expert")
    b = lax.axis_index("batch")
    return e // 2, e % 2, b // 2, b % 2


def swap(flag, first, second):
    return jnp.where(flag, second, first), jnp.where(flag, first, second)


def add_product(start, size, tokens, gate_ref, up_ref, gate_acc, up_acc, fresh):
    step = size // 256 * 128
    for i in range(2):
        span = pl.ds(i * step, size - step if i else step)
        source = pl.ds(start + i * step, span.size)
        chunk = jnp.concatenate([ref[:, span] for ref in tokens], axis=0)
        for weight, acc in ((gate_ref, gate_acc), (up_ref, up_acc)):
            product = jnp.dot(chunk, weight[source, :], preferred_element_type=jnp.float32)
            if fresh and i == 0:
                acc[...] = product
            else:
                acc[...] += product


def first_product_kernel(size, *refs):
    *tokens, gate_ref, up_ref, gate_acc, up_acc = refs
    add_product(0, size, tokens, gate_ref, up_ref, gate_acc, up_acc, True)


def expert_kernel(start, size, *refs):
    tokens, (gate_ref, up_ref, gate_in, up_in, down_ref, *outs, gate_acc, up_acc) = refs[:4], refs[4:]
    z, y, x, c = coordinates()
    live = tokens[0].shape[0]
    gate_acc[...] = gate_in[...]
    up_acc[...] = up_in[...]
    add_product(start, size, tokens, gate_ref, up_ref, gate_acc, up_acc, False)
    kept, sent = [], []
    for i, ref in enumerate(tokens):
        span = pl.ds(i * live, live)
        gate = gate_acc[span, :]
        hidden = gate / (1.0 + jnp.exp(-gate)) * up_acc[span, :]
        prob = jnp.sum(ref[:, size : size + 128].astype(jnp.float32), axis=1, keepdims=True)
        hidden = hidden * prob
        slots = hidden.reshape(2, 2, live // 4, -1)
        same, other = swap(y == 1, slots[:, 0], slots[:, 1])
        block = jnp.concatenate([same, other]).reshape(live, -1)
        (sent if i % 2 else kept).append(block)
    ordered_down(jnp.concatenate(kept + sent, axis=0).astype(jnp.bfloat16), down_ref, *outs)


def ordered_down(hidden, down_ref, *outs):
    keep_first, send_first, keep_rest, send_rest = outs
    width = down_ref.shape[1]
    rows = keep_first.shape[0]
    half = hidden.shape[0] // 2
    steps = 4
    for i in range(steps):
        span = pl.ds(i * (width // steps), width // steps)
        terms = jnp.dot(hidden, down_ref[:, span], preferred_element_type=jnp.float32).astype(
            keep_first.dtype
        )
        for base, first, rest in ((0, keep_first, keep_rest), (half, send_first, send_rest)):
            first[:, span] = terms[base + 2 * rows : base + 3 * rows]
            rest[: 2 * rows, span] = terms[base : base + 2 * rows]
            rest[2 * rows :, span] = terms[base + 3 * rows : base + 4 * rows]


def put(out, rows):
    width = min(rows.shape[1], out.shape[1])
    out[:, :width] = rows[:, :width]
    if out.shape[1] > width:
        out[:, width:] = jnp.zeros((rows.shape[0], out.shape[1] - width), out.dtype)


def core_sum(keep_ref, received_ref, start, rows):
    span = pl.ds(start, rows)
    return keep_ref[span, :].astype(jnp.float32) + received_ref[span, :].astype(jnp.float32)


def by_z(rows):
    z, y, x, c = coordinates()
    slot = rows.shape[0] // 2
    return swap((z == 0) | (z == 3), rows[:slot], rows[slot:])


def first_sums_kernel(keep_ref, received_ref, near_ref, far_ref):
    near, far = by_z(core_sum(keep_ref, received_ref, 0, keep_ref.shape[0]))
    put(near_ref, near.astype(near_ref.dtype))
    put(far_ref, far.astype(far_ref.dtype))


def other_sums_kernel(keep_ref, received_ref, near_ref, far_ref, along_ref, diagonal_ref):
    rows = along_ref.shape[0]
    near, far = by_z(core_sum(keep_ref, received_ref, 0, rows))
    near_ref[...] = near.astype(near_ref.dtype)
    far_ref[...] = far.astype(far_ref.dtype)
    put(along_ref, core_sum(keep_ref, received_ref, rows, rows).astype(along_ref.dtype))
    put(diagonal_ref, core_sum(keep_ref, received_ref, 2 * rows, rows).astype(diagonal_ref.dtype))


def add_kernel(first, second, *outs):
    width = first.shape[1]
    total = first[...].astype(jnp.float32) + second[:, :width].astype(jnp.float32)
    for out in outs:
        put(out, total.astype(out.dtype))


def add_by_z_kernel(first, second, *outs):
    width = first.shape[1]
    halves = by_z(first[...].astype(jnp.float32) + second[:, :width].astype(jnp.float32))
    for i, out in enumerate(outs):
        put(out, halves[min(i // 2, 1)].astype(out.dtype))


def run_copies(pairs, sems):
    copies = [pltpu.make_async_copy(source, target, sems.at[i]) for i, (source, target) in enumerate(pairs)]
    for copy in copies:
        copy.start()
    for copy in copies:
        copy.wait()


def place_kernel(layout, zeros, pieces, out_ref, sems):
    z, y, x, c = coordinates()
    width = out_ref.shape[2]
    for mine in range(2):

        @pl.when(z == mine)
        def _():
            pairs = []
            for (index, other, *only), piece in zip(layout, pieces):
                if mine not in (only or (0, 1)):
                    continue
                source = (mine, 1 - mine, 2 + mine, 3 - mine)[index]
                pairs.append((piece.at[:, pl.ds(0, width)], out_ref.at[source * 2 + (y ^ other)]))
            run_copies(pairs, sems)

    if zeros is not None:

        @pl.when(z >= 2)
        def _():
            zeros[...] = jnp.zeros_like(zeros)
            run_copies([(zeros, out_ref.at[i]) for i in range(out_ref.shape[0])], sems)


def place_first_kernel(layout, *refs):
    *pieces, out_ref, zeros, sems = refs
    place_kernel(layout, zeros, pieces, out_ref, sems)


def place_rest_kernel(layout, *refs):
    out_ref, sems = refs[-2:]
    place_kernel(layout, None, refs[: len(layout)], out_ref, sems)


def ports_body(tokens, route_prob, counts, w_gate, w_up, w_down):
    cap, width = tokens.shape[1:]
    units = w_gate.shape[2]
    rows = LIVE // 2
    both_axes = ("expert", "batch")

    def device(z, y, x, c):
        return (z * 2 + y) * 4 + x * 2 + c

    places = [(z, y, x, c) for z in range(4) for y in range(2) for x in range(2) for c in range(2)]

    def other_core(value):
        return lax.ppermute(value, "batch", xor_pairs(4, 1))

    def across_plane(value, dx, dy):
        return lax.ppermute(value, both_axes, [(device(*p), device(p[0], p[1] ^ dy, p[2] ^ dx, p[3])) for p in places])

    def along_z(value, *moves):
        pairs = [(device(s, *p[1:]), device(t, *p[1:])) for s, t in moves for p in places if p[0] == 0]
        return lax.ppermute(value, both_axes, pairs)

    def array(rows, columns, dtype=jnp.bfloat16):
        return jax.ShapeDtypeStruct((rows, columns), dtype)

    depth = (width + PROB_COLUMNS) // 2
    rest = width - depth
    in_hbm = [pltpu.with_memory_space_constraint(a, pltpu.HBM) for a in (tokens, route_prob, counts.T)]
    piece = pltpu.VMEM((LIVE, depth), tokens.dtype)
    own = [
        call(live_rows_kernel, piece, in_hbm[:1], [HBM], [pltpu.SemaphoreType.DMA], name="live_rows"),
        call(
            lambda *refs: live_rows_and_prob_kernel(depth, *refs),
            [piece],
            in_hbm,
            [HBM, HBM, HBM],
            [
                pltpu.VMEM(route_prob.shape, route_prob.dtype),
                pltpu.VMEM(counts.T.shape, counts.dtype),
                pltpu.SemaphoreType.DMA((3,)),
            ],
            name="live_rows_and_prob",
        )[0],
    ]
    across = [lax.ppermute(piece, "batch", xor_pairs(4, 2)) for piece in own]
    near = [other_core(piece) for piece in own]
    gate_w, up_w, down_w = resident(after(w_gate[0], *own), w_up[0], w_down[0])
    across = [after(piece, down_w) for piece in across]
    pieces = [[own[0], near[0], across[0], other_core(across[0])], None]
    gate, upper = call(
        lambda *refs: first_product_kernel(depth, *refs),
        [array(4 * LIVE, units, jnp.float32)] * 2,
        [*pieces[0], gate_w, up_w],
        name="first_product",
    )
    pieces[1] = [own[1], near[1], across[1], other_core(across[1])]
    slot = rows // 2
    keep_first, send_first, keep_rest, send_rest = call(
        lambda *refs: expert_kernel(depth, rest, *refs),
        [array(rows, width), array(rows, width), array(3 * rows, width), array(3 * rows, width)],
        [*pieces[1], gate_w, up_w, gate, upper, down_w],
        scratch=[pltpu.VMEM((4 * LIVE, units), jnp.float32)] * 2,
        name="expert",
    )
    lead_x, rest_x = call(
        first_sums_kernel,
        [array(slot, width + n) for n in (96, 192)],
        [keep_first, other_core(send_first)],
        name="first_sums",
    )
    own_lead, own_rest, own_other, across_other = call(
        other_sums_kernel,
        [array(slot, width), array(slot, width), array(rows, width + 32), array(rows, width + 0)],
        [keep_rest, other_core(after(send_rest, lead_x))],
        name="other_sums",
    )
    lead_1, next_1 = call(
        add_kernel,
        [array(slot, width + n) for n in (128, 0)],
        [own_lead, across_plane(lead_x, 1, 0)],
        name="lead_rows",
    )
    rest_1, = call(add_kernel, [array(slot, width + 0)], [own_rest, across_plane(rest_x, 1, 0)], name="rest_rows")
    from_2 = [along_z(lead_1, (2, 0), (3, 1))]
    from_3 = [along_z(rest_1, (2, 1), (3, 0))]
    next_z = [along_z(next_1, (0, 1), (1, 0))]
    from_y = across_plane(own_other, 0, 1)
    diagonal = across_plane(across_other, 1, 1)
    lead_2, next_2, rest_2, rest_2_to_0, mark = call(
        add_by_z_kernel,
        [array(slot, width + n) for n in (64, 32, 0, 48, -32)],
        [diagonal, from_y],
        name="other_rows",
    )
    from_2.append(along_z(lead_2, (2, 0), (3, 1)))
    to_0, to_1 = along_z(rest_2_to_0, (3, 0)), along_z(rest_2, (2, 1))
    next_z.append(along_z(after(next_2, next_z[0]), (0, 1), (1, 0)))
    mark = other_core(after(mark, from_2[0], from_3[0]))
    out = jax.ShapeDtypeStruct((cap // slot, slot, width), jnp.bfloat16)
    pieces = [rest_1, rest_2, from_2[0], from_3[0], next_z[0]]
    out = call(
        lambda *refs: place_first_kernel([(0, 0), (0, 1), (2, 0), (3, 0), (1, 0)], *refs),
        out,
        pieces,
        [ANY] * len(pieces),
        [pltpu.VMEM((slot, width), jnp.bfloat16), pltpu.SemaphoreType.DMA((cap // slot,))],
        out_specs=HBM,
        name="place_first",
    )
    pieces = [from_2[1], to_0, to_1, next_z[1], mark]
    out = call(
        lambda *refs: place_rest_kernel([(2, 1), (3, 1, 0), (3, 1, 1), (1, 1)], *refs),
        jax.ShapeDtypeStruct(out.shape, out.dtype),
        [*pieces, out],
        [ANY] * len(pieces) + [HBM],
        [pltpu.SemaphoreType.DMA((len(pieces),))],
        out_specs=HBM,
        aliases={len(pieces): 0},
        name="place_rest",
    )
    return out.reshape(1, cap, width)


def solution(mesh):
    in_specs = (
        P("expert", "batch", None),
        P("expert", "batch"),
        P(),
        P("expert", None, "batch"),
        P("expert", None, "batch"),
        P("expert", "batch", None),
    )
    out_specs = P("expert", "batch", None)
    fits = dict(mesh.shape) == {"expert": 8, "batch": 4}
    body = ports_body if fits else general_body
    return jax.shard_map(body, mesh=mesh, in_specs=in_specs, out_specs=out_specs, check_vma=False)
```
